512 devices in a mesh: gx: 16 (over z_lo, core), gy: 4 (over y), gz: 8 (over z_hi, x).
Axes of the slice: x: 4, y: 4, z: 16 (z_hi: 2, z_lo: 8; z = z_hi * 8 + z_lo), core: 2. Of those that a mesh axis runs over, the one named last changes fastest.
Arguments:
- positions: float32 [3, 16, 4, 8, 512], P(None, 'gx', 'gy', 'gz'), may hold values from 0 to 6
- species: int32 [16, 4, 8, 512], P('gx', 'gy', 'gz'), may hold values from 0 to 5
- send_lists: int32 [32, 8, 16, 8], P('gx', 'gy', 'gz'), may hold values from 0 to 511
- pair_center: int32 [16, 4, 8, 8, 128], P('gx', 'gy', 'gz'), may hold values from 0 to 511
- pair_partner: int32 [16, 4, 8, 8, 128], P('gx', 'gy', 'gz'), may hold values from 0 to 959, as said below
- pair_slot_live: int32 [16, 4, 8, 8, 128], P('gx', 'gy', 'gz'), may hold values from 0 to 1, as said below
- w_basis: float32 [8, 128], replicated, may hold values from -2 to 2
- emb_center: float32 [6, 128], replicated, may hold values from -6 to 6
- emb_partner: float32 [6, 128], replicated, may hold values from -6 to 6
- w_env: float32 [128, 64], replicated, may hold values from -0.5 to 0.5
- w_value: float32 [128, 64], replicated, may hold values from -0.5 to 0.5
- w_mix: float32 [192, 128], replicated, may hold values from -0.4375 to 0.4375
- w_out: float32 [128], replicated, may hold values from -0.5 to 0.5
Outputs:
- forces: float32 [3, 16, 4, 8, 512], P(None, 'gx', 'gy', 'gz')
- atom_energy: float32 [16, 4, 8, 512], P('gx', 'gy', 'gz')
The draws below stay inside these ranges and needn't reach their ends.
Inputs may be any that keep to these rules, and one draw needn't show every extreme that they name: `pair_partner`: never the pair's centre. `pair_slot_live`: in every domain the first 8, 4, 2 or 1 blocks hold pairs and the later blocks none; a block that holds pairs has them in its first 64 to 128 slots. Some domain has all 8 blocks holding pairs, one of them full.
All inputs are finite; a program needn't handle non-finite values.
Results may differ from the reference program's by a relative error of at most 0.0003.
Values sent between devices are 32-bit elements; how exact they have to be, the bound alone decides.
No kernel may reach another device: no remote copies, remote signals or barrier semaphores. Data moves between devices by JAX's collectives and lax.ppermute only.
A program may use at most 64 MiB of HBM per device.

```python
import math
import jax
import jax.numpy as jnp
import numpy as np
from jax import lax

A_DEV = 512
M = 8
NB = 8
PAIR_BLOCK_SIZE = 128
LAT = 128
CHAN = 64
NBASIS = 8
NSPEC = 6
TABLE_ROWS = 960
N_GX = 16
N_GY = 4
N_GZ = 8


def pair_draw(key):
    complete_shape = (N_GX, N_GY, N_GZ, NB, PAIR_BLOCK_SIZE)
    domain_list = N_GX * N_GY * N_GZ
    subkeys = jax.random.split(key, 5)
    center_atoms = jax.random.randint(subkeys[0], complete_shape, 0, A_DEV, dtype=jnp.int32)
    partner_atoms = (center_atoms + 1 + jax.random.randint(subkeys[1], complete_shape, 0, TABLE_ROWS - 1, dtype=jnp.int32)) % TABLE_ROWS
    levels = jax.random.randint(subkeys[2], (domain_list,), 0, 4, dtype=jnp.int32)
    busiest = jax.random.randint(subkeys[3], (), 0, domain_list, dtype=jnp.int32)
    domain_ids = jnp.arange(domain_list, dtype=jnp.int32)
    levels = jnp.where(domain_ids == busiest, 0, levels)
    live_blocks = jnp.right_shift(jnp.full((domain_list,), NB, jnp.int32), levels)
    filled_slots = jax.random.randint(subkeys[4], (domain_list, NB), PAIR_BLOCK_SIZE // 2, PAIR_BLOCK_SIZE + 1, dtype=jnp.int32)
    block_ids = jnp.arange(NB, dtype=jnp.int32)[None, :]
    filled_slots = jnp.where((domain_ids[:, None] == busiest) & (block_ids == 0), PAIR_BLOCK_SIZE, filled_slots)
    filled_slots = jnp.where(block_ids < live_blocks[:, None], filled_slots, 0)
    live_flags = (jnp.arange(PAIR_BLOCK_SIZE, dtype=jnp.int32)[None, None, :] < filled_slots[:, :, None]).astype(jnp.int32)
    return (center_atoms, partner_atoms, live_flags.reshape(complete_shape))


def draw_pair_center(key, part):
    return pair_draw(key)[0]


def draw_pair_partner(key, part):
    return pair_draw(key)[1]


def draw_pair_slot_live(key, part):
    return pair_draw(key)[2]


def place_ends(entries, own_key, smallest, high):
    index_at = [jax.random.randint(jax.random.fold_in(own_key, axis), (), 0, length) for axis, length in enumerate(entries.shape)]
    main_axis = entries.shape.index(max(entries.shape))
    neighbour = index_at[:main_axis] + [(index_at[main_axis] + 1) % entries.shape[main_axis]] + index_at[main_axis + 1:]
    return entries.at[tuple(index_at)].set(smallest).at[tuple(neighbour)].set(high)


def steps_of(key, shape, cuts, smallest, largest):
    def one(position, shards_of):
        draws = jax.random.uniform(jax.random.fold_in(jax.random.fold_in(key, 6), position), (shards_of,), jnp.float32, smallest / len(cuts), largest / len(cuts))
        return jnp.repeat(jnp.exp(draws), shape[position] // shards_of).reshape((-1,) + (1,) * (len(shape) - position - 1))

    gain = one(*cuts[0])
    for cut in cuts[1:]:
        gain = gain * one(*cut)
    return gain


def scatter_about(own_key, shape, width, most, kind=jnp.bfloat16):
    values = jax.random.normal(own_key, shape, jnp.float32) * width
    return jnp.minimum(jnp.maximum(values, -most), most).astype(kind)


def setup_inputs(seed: int = 0) -> dict:
    key_list = jax.random.split(jax.random.key(seed), 14)
    positions = jnp.clip(6.0 * jax.random.uniform(key_list[0], (3, N_GX, N_GY, N_GZ, A_DEV), jnp.float32) ** steps_of(key_list[0], (3, N_GX, N_GY, N_GZ, A_DEV), ((1, 16), (2, 4), (3, 8)), -0.2, 0.2), 0.0, 6.0)
    species = place_ends(jax.random.randint(key_list[1], (N_GX, N_GY, N_GZ, A_DEV), 0, NSPEC), jax.random.fold_in(key_list[1], 1), 0, NSPEC - 1).astype(jnp.int32)
    send_lists = place_ends(jax.random.randint(key_list[2], (2 * N_GX, 2 * N_GY, 2 * N_GZ, M), 0, A_DEV), jax.random.fold_in(key_list[2], 1), 0, A_DEV - 1).astype(jnp.int32)
    pair_center = draw_pair_center(jax.random.fold_in(key_list[13], 71), 0)
    pair_partner = draw_pair_partner(jax.random.fold_in(key_list[13], 71), 0)
    pair_slot_live = draw_pair_slot_live(jax.random.fold_in(key_list[13], 71), 0)
    w_basis = scatter_about(key_list[6], (NBASIS, LAT), NBASIS ** -0.5, 2.0, jnp.float32)
    emb_center = scatter_about(key_list[7], (NSPEC, LAT), 1.0, 6.0, jnp.float32)
    emb_partner = scatter_about(key_list[8], (NSPEC, LAT), 1.0, 6.0, jnp.float32)
    w_env = scatter_about(key_list[9], (LAT, CHAN), LAT ** -0.5, 0.5, jnp.float32)
    w_value = scatter_about(key_list[10], (LAT, CHAN), LAT ** -0.5, 0.5, jnp.float32)
    w_mix = scatter_about(key_list[11], (LAT + CHAN, LAT), (LAT + CHAN) ** -0.5, 0.4375, jnp.float32)
    w_out = scatter_about(key_list[12], (LAT,), LAT ** -0.5, 0.5, jnp.float32)
    return dict(positions=positions, species=species, send_lists=send_lists, pair_center=pair_center, pair_partner=pair_partner, pair_slot_live=pair_slot_live, w_basis=w_basis, emb_center=emb_center, emb_partner=emb_partner, w_env=w_env, w_value=w_value, w_mix=w_mix, w_out=w_out)


shell_cells = np.array([(p, q, r) for p in range(4) for q in range(4) for r in range(4) if not (0 < p < 3 and 0 < q < 3 and (0 < r < 3))], dtype=np.int32)
shell_shift = np.where(shell_cells == 0, -1.0, np.where(shell_cells == 3, 1.0, 0.0)).astype(np.float32)
domain_width = 6.0
cutoff = 5.0
basis_range = 12.0
soften = 0.25

def matmul_hi(left, right):
    return jnp.dot(left, right, precision=lax.Precision.HIGHEST, preferred_element_type=jnp.float32)

def features_per_pair(table_position, species_onehot, center_atoms, partner_atoms, live_flags, model_parameters):
    w_basis, emb_center, emb_partner = (model_parameters[0], model_parameters[1], model_parameters[2])
    displacement = table_position[partner_atoms] - table_position[center_atoms]
    radius = jnp.sqrt(lax.optimization_barrier(jnp.sum(displacement * displacement, axis=1)) + soften)
    unit_vector = displacement / radius[:, None]
    orders = jnp.arange(1, w_basis.shape[0] + 1).astype(jnp.float32)
    radial_basis = jnp.sin(radius[:, None] * orders[None, :] * (math.pi / basis_range)) / radius[:, None]
    scaled_values = radius / cutoff
    cutoff_envelope = live_flags.astype(jnp.float32) / ((1.0 + scaled_values * scaled_values) * (1.0 + scaled_values * scaled_values))
    pre_act = matmul_hi(radial_basis, w_basis) + matmul_hi(species_onehot[center_atoms], emb_center) + matmul_hi(species_onehot[partner_atoms], emb_partner)
    latent_features = cutoff_envelope[:, None] * jax.nn.silu(pre_act)
    return (latent_features, unit_vector, cutoff_envelope)

def environment_sum(table_position, species_onehot, center_atoms, partner_atoms, live_flags, model_parameters, atom_total_count):
    latent_features, unit_vector, cutoff_envelope = features_per_pair(table_position, species_onehot, center_atoms, partner_atoms, live_flags, model_parameters)
    weights = matmul_hi(latent_features, model_parameters[3])
    env_terms = (unit_vector[:, :, None] * weights[:, None, :]).reshape(latent_features.shape[0], -1)
    return jax.ops.segment_sum(env_terms, center_atoms, num_segments=atom_total_count)

def energy_per_pair(table_position, environment_table, species_onehot, center_atoms, partner_atoms, live_flags, model_parameters, atom_total_count):
    latent_features, unit_vector, cutoff_envelope = features_per_pair(table_position, species_onehot, center_atoms, partner_atoms, live_flags, model_parameters)
    w_value, w_mix, w_out = (model_parameters[4], model_parameters[5], model_parameters[6])
    values = matmul_hi(latent_features, w_value)
    channels = values.shape[1]
    env_center = environment_table[center_atoms].reshape(-1, 3, channels)
    env_partner = environment_table[partner_atoms].reshape(-1, 3, channels)
    coupling = lax.optimization_barrier(jnp.sum(env_center * unit_vector[:, :, None], axis=1)) + lax.optimization_barrier(jnp.sum(env_center * env_partner, axis=1))
    tensor = values * coupling
    lat_width = latent_features.shape[1]
    hidden = matmul_hi(latent_features, w_mix[:lat_width]) + matmul_hi(tensor, w_mix[lat_width:])
    updated = latent_features + jax.nn.silu(hidden)
    energy_values = cutoff_envelope * matmul_hi(updated, w_out)
    return jax.ops.segment_sum(energy_values, center_atoms, num_segments=atom_total_count)

def reference(positions, species, send_lists, pair_center, pair_partner, pair_slot_live, w_basis, emb_center, emb_partner, w_env, w_value, w_mix, w_out):
    model_parameters = (w_basis, emb_center, emb_partner, w_env, w_value, w_mix, w_out)
    domain_list = N_GX * N_GY * N_GZ
    cell_table = jnp.asarray(shell_cells)
    index_x = jnp.arange(N_GX, dtype=jnp.int32)[:, None, None, None]
    index_y = jnp.arange(N_GY, dtype=jnp.int32)[None, :, None, None]
    index_z = jnp.arange(N_GZ, dtype=jnp.int32)[None, None, :, None]
    complete_shape = (N_GX, N_GY, N_GZ, cell_table.shape[0])
    lattice_x = jnp.broadcast_to((2 * index_x - 1 + cell_table[:, 0]) % (2 * N_GX), complete_shape)
    lattice_y = jnp.broadcast_to((2 * index_y - 1 + cell_table[:, 1]) % (2 * N_GY), complete_shape)
    lattice_z = jnp.broadcast_to((2 * index_z - 1 + cell_table[:, 2]) % (2 * N_GZ), complete_shape)
    ghost_atoms = send_lists[lattice_x, lattice_y, lattice_z]
    owner_x = jnp.broadcast_to((lattice_x // 2)[..., None], ghost_atoms.shape)
    owner_y = jnp.broadcast_to((lattice_y // 2)[..., None], ghost_atoms.shape)
    owner_z = jnp.broadcast_to((lattice_z // 2)[..., None], ghost_atoms.shape)
    cell_shift = jnp.asarray(shell_shift) * domain_width
    ghost_species = species[owner_x, owner_y, owner_z, ghost_atoms]
    table_species = jnp.concatenate([species.reshape(domain_list, -1), ghost_species.reshape(domain_list, -1)], axis=1)
    species_codes = jnp.arange(emb_center.shape[0], dtype=jnp.int32)
    species_onehot = (table_species[..., None] == species_codes).astype(jnp.float32)
    center_atoms = pair_center.reshape(domain_list, -1)
    partner_atoms = pair_partner.reshape(domain_list, -1)
    live_flags = pair_slot_live.reshape(domain_list, -1)

    def tables(coords):
        own_rows = jnp.moveaxis(coords, 0, -1)
        ghost_rows = own_rows[owner_x, owner_y, owner_z, ghost_atoms] + cell_shift[:, None, :]
        return jnp.concatenate([own_rows.reshape(domain_list, -1, 3), ghost_rows.reshape(domain_list, -1, 3)], axis=1)

    def domain_environment(inputs):
        return environment_sum(inputs[0], inputs[1], inputs[2], inputs[3], inputs[4], model_parameters, A_DEV)

    def domain_energy(inputs):
        return energy_per_pair(inputs[0], inputs[1], inputs[2], inputs[3], inputs[4], inputs[5], model_parameters, A_DEV)

    def total(coords):
        table_position = tables(coords)
        owned_environment = lax.map(jax.checkpoint(domain_environment), (table_position, species_onehot, center_atoms, partner_atoms, live_flags))
        grid_env = owned_environment.reshape(N_GX, N_GY, N_GZ, A_DEV, -1)
        ghost_env = grid_env[owner_x, owner_y, owner_z, ghost_atoms].reshape(domain_list, -1, owned_environment.shape[-1])
        environment_table = jnp.concatenate([owned_environment, ghost_env], axis=1)
        energy_values = lax.map(jax.checkpoint(domain_energy), (table_position, environment_table, species_onehot, center_atoms, partner_atoms, live_flags))
        return (jnp.sum(energy_values), energy_values)
    summed, pullback, energy_values = jax.vjp(total, positions, has_aux=True)
    gradient = pullback(jnp.ones_like(summed))[0]
    return (-gradient, energy_values.reshape(N_GX, N_GY, N_GZ, A_DEV))
```

```python
import math

import jax
import jax.numpy as jnp
import numpy as np
from jax import lax
from jax.experimental import pallas as pl
from jax.experimental.pallas import tpu as pltpu
from jax.sharding import PartitionSpec as P

AXES = ("gx", "gy", "gz")
SHAPE = (16, 4, 8)
ATOMS = 512
PAIRS = 1024
LIST = 64
CHAN = 64
STEP = math.pi / 12.0
F32 = jnp.float32
BF16 = jnp.bfloat16


def flat(x, y, z):
    return (x * SHAPE[1] + y) * SHAPE[2] + z


def home(x, y, z):
    x, y, z = x % SHAPE[0], y % SHAPE[1], z % SHAPE[2]
    chip_z, chip_x, core = x, z // 2, z % 2
    return flat((chip_z % 8) * 2 + core, y, (chip_z // 8) * 4 + chip_x)


CELLS = [(x, y, z) for x in range(SHAPE[0]) for y in range(SHAPE[1]) for z in range(SHAPE[2])]
MOVE_IN = [(flat(*c), home(*c)) for c in CELLS]
MOVE_OUT = [(b, a) for a, b in MOVE_IN]


def shifted(axis, by):
    step = [0, 0, 0]
    step[axis] = by
    return [(home(x, y, z), home(x + step[0], y + step[1], z + step[2])) for x, y, z in CELLS]


def spread(cells):
    for axis in (2, 1, 0):
        last = lax.slice_in_dim(cells, 1, 2, axis=axis)
        first = lax.slice_in_dim(cells, 0, 1, axis=axis)
        before = lax.ppermute(last, AXES, shifted(axis, 1))
        after = lax.ppermute(first, AXES, shifted(axis, -1))
        cells = jnp.concatenate([before, cells, after], axis=axis)
    return cells


def collect(cells):
    for axis in (0, 1, 2):
        to_down = lax.slice_in_dim(cells, 0, 1, axis=axis)
        to_up = lax.slice_in_dim(cells, 3, 4, axis=axis)
        from_down = lax.ppermute(to_up, AXES, shifted(axis, 1))
        from_up = lax.ppermute(to_down, AXES, shifted(axis, -1))
        cells = lax.slice_in_dim(cells, 1, 3, axis=axis) + jnp.concatenate([from_down, from_up], axis=axis)
    return cells


def split2(x):
    high = x.astype(BF16)
    low = (x - high.astype(F32)).astype(BF16)
    return high, low


def split3(x):
    high = x.astype(BF16)
    rest = x - high.astype(F32)
    mid = rest.astype(BF16)
    return high, mid, (rest - mid.astype(F32)).astype(BF16)


def dot(a, b, ca, cb):
    return lax.dot_general(a, b, (((ca,), (cb,)), ((), ())), preferred_element_type=F32)


def weighted(w, x):
    wh, wl = split2(w)
    xh, xl = split2(x)
    return dot(wh, xh, 0, 0) + (dot(wl, xh, 0, 0) + dot(wh, xl, 0, 0))


def weighted_t(w, x):
    wh, wl = split2(w)
    xh, xl = split2(x)
    return dot(wh, xh, 1, 0) + (dot(wl, xh, 1, 0) + dot(wh, xl, 1, 0))


def pick(table, onehot, parts=2):
    rows = table.shape[0]
    pieces = split3(table) if parts == 3 else split2(table)
    full = dot(jnp.concatenate(pieces, axis=0), onehot, 1, 0)
    out = full[:rows]
    for i in range(1, parts):
        out = out + full[rows * i : rows * (i + 1)]
    return out


def put(values, onehot, parts=2):
    rows = values.shape[0]
    pieces = split3(values) if parts == 3 else split2(values)
    full = dot(jnp.concatenate(pieces, axis=0), onehot, 1, 1)
    out = full[:rows]
    for i in range(1, parts):
        out = out + full[rows * i : rows * (i + 1)]
    return out


def put_rows(values, onehot):
    high, low = split2(values)
    return dot(onehot, high, 1, 1) + dot(onehot, low, 1, 1)


def lanes(block):
    return jnp.concatenate([block[i : i + 1] for i in range(block.shape[0])], axis=1)


def match(index, count):
    ids = lax.broadcasted_iota(jnp.int32, (count, index.shape[1]), 0)
    return jnp.where(ids == index, 1.0, 0.0).astype(BF16)


def centers_of(packed):
    return lanes(packed[16:24]).astype(jnp.int32)


def partners_of(packed):
    return lanes(packed[24:32]).astype(jnp.int32)


def live_of(packed):
    return lanes(packed[32:40])


def own_table(packed):
    return jnp.concatenate([lanes(packed[4 * k : 4 * k + 4]) for k in range(4)], axis=0)


def ghost_slot(partners):
    rows = partners - ATOMS
    cell = rows >> 3
    skip = jnp.zeros_like(cell)
    for start in (21, 23, 33, 35):
        skip = skip + jnp.where(cell >= start, 16, 0)
    return rows + skip


def k_lists(packed_ref, out_ref, column_ref):
    packed = packed_ref[...]
    names = packed[40:41].astype(jnp.int32)
    found = pick(own_table(packed), match(names, ATOMS), 3)
    wide = jnp.concatenate([found, jnp.zeros((4, 128), F32)], axis=0)
    out_ref[...] = wide.T[:LIST, :4]
    column_ref[...] = jnp.broadcast_to(packed[40:41], (8, 128)).T[:LIST]


def k_own_pairs(packed_ref, out_ref):
    packed = packed_ref[...]
    table = own_table(packed)
    at_center = pick(table, match(centers_of(packed), ATOMS), 3)
    at_partner = pick(table, match(partners_of(packed), ATOMS), 3)
    out_ref[0:3] = at_partner[0:3] - at_center[0:3]
    out_ref[3:4] = at_partner[3:4]
    out_ref[4:5] = at_center[3:4]
    out_ref[5:8] = jnp.zeros((3, PAIRS), F32)


def k_features(packed_ref, part_ref, ghost_ref, shift_ref, column_ref, wb_ref, wav_ref, msg_ref, scal_ref, pre_ref, av_ref):
    packed = packed_ref[...]
    part = part_ref[...]
    ghost = ghost_ref[...] + shift_ref[...]
    slots = match(ghost_slot(partners_of(packed)), 512)
    pieces = split3(ghost)
    far = dot(pieces[0], slots, 0, 0) + (dot(pieces[1], slots, 0, 0) + dot(pieces[2], slots, 0, 0))
    disp = part[0:3] + far[0:3]
    partner_kind = part[3:4] + far[3:4]
    center_kind = part[4:5]
    radius = jnp.sqrt(jnp.sum(disp * disp, axis=0, keepdims=True) + 0.25)
    inv = 1.0 / radius
    unit = disp * inv
    scaled = radius * 0.2
    base = 1.0 + scaled * scaled
    live = live_of(packed)
    cut = live / (base * base)
    orders = lax.broadcasted_iota(jnp.int32, (8, 1), 0).astype(F32) + 1.0
    angle = radius * orders * STEP
    basis = jnp.sin(angle) * inv
    kinds = lax.broadcasted_iota(jnp.int32, (8, 1), 0).astype(F32)
    first = jnp.where(center_kind == kinds, 1.0, 0.0)
    second = jnp.where(partner_kind == kinds, 1.0, 0.0)
    pre = weighted(wb_ref[...], jnp.concatenate([basis, first, second], axis=0))
    latent = cut * (pre * jax.nn.sigmoid(pre))
    av = weighted(wav_ref[...], latent)
    a = av[:CHAN]
    terms = jnp.concatenate([unit[k : k + 1] * a for k in range(3)], axis=0)
    named = jnp.where(column_ref[:, 0:1].astype(jnp.int32) == centers_of(packed), 1.0, 0.0).astype(BF16)
    msg_ref[...] = put_rows(terms, named)
    scal_ref[0:3] = unit
    scal_ref[3:4] = radius
    scal_ref[4:5] = inv
    scal_ref[5:6] = cut
    scal_ref[6:7] = live * (-0.8) * scaled / (base * base * base)
    scal_ref[7:8] = live
    pre_ref[...] = pre
    av_ref[...] = av


def k_own_env(packed_ref, scal_ref, pre_ref, av_ref, wb_ref, wav_ref, wm_ref, ei_ref, ej_ref, lat_ref, hid_ref, tan_ref, nav_ref):
    packed = packed_ref[...]
    scal = scal_ref[...]
    unit, radius, inv, cut, slope = scal[0:3], scal[3:4], scal[4:5], scal[5:6], scal[6:7]
    av = av_ref[...]
    a = av[:CHAN]
    terms = jnp.concatenate([unit[k : k + 1] * a for k in range(3)], axis=0)
    at_center = match(centers_of(packed), ATOMS)
    env = put(terms, at_center)
    ei_ref[...] = pick(env, at_center)
    ej_ref[...] = pick(env, match(partners_of(packed), ATOMS))
    pre = pre_ref[...]
    gate = jax.nn.sigmoid(pre)
    act = pre * gate
    latent = cut * act
    lat_ref[...] = latent
    hid_ref[...] = weighted(wm_ref[0:128], latent)
    orders = lax.broadcasted_iota(jnp.int32, (8, 1), 0).astype(F32) + 1.0
    angle = radius * orders * STEP
    change = (jnp.cos(angle) * (orders * STEP) - jnp.sin(angle) * inv) * inv
    tangent = slope * act + cut * (gate * (1.0 + pre * (1.0 - gate))) * weighted(wb_ref[0:8], change)
    tan_ref[...] = tangent
    nav_ref[...] = weighted(wav_ref[...], tangent)


def k_energy(packed_ref, scal_ref, av_ref, ghost_ref, ei_ref, ejown_ref, hid_ref, wm_ref, wo_ref, msg_ref, ej_ref, h_ref, tb_ref):
    packed = packed_ref[...]
    scal = scal_ref[...]
    unit, cut = scal[0:3], scal[5:6]
    slots = match(ghost_slot(partners_of(packed)), 512)
    high, low = split2(ghost_ref[...])
    ej = ejown_ref[...] + (dot(high, slots, 0, 0) + dot(low, slots, 0, 0))
    ei = ei_ref[...]
    coupling = 0.0
    for k in range(3):
        rows = slice(k * CHAN, (k + 1) * CHAN)
        coupling = coupling + ei[rows] * (unit[k : k + 1] + ej[rows])
    v = av_ref[CHAN:]
    mix = wm_ref[128:]
    h = hid_ref[...] + weighted(mix, v * coupling)
    gate = jax.nn.sigmoid(h)
    out = wo_ref[...]
    hbar = (cut * out) * (gate * (1.0 + h * (1.0 - gate)))
    tbar = weighted_t(mix, hbar)
    cbar = tbar * v
    back = jnp.concatenate([cbar * ei[k * CHAN : (k + 1) * CHAN] for k in range(3)], axis=0)
    msg_ref[...] = put_rows(back, slots)
    ej_ref[...] = ej
    h_ref[...] = h
    tb_ref[...] = tbar


def k_direct(
    packed_ref, scal_ref, av_ref, nav_ref, ei_ref, ej_ref, lat_ref, tan_ref, h_ref, tb_ref, wm_ref, wo_ref, part_ref, energy_ref
):
    packed = packed_ref[...]
    scal = scal_ref[...]
    unit, cut, slope = scal[0:3], scal[5:6], scal[6:7]
    at_center = match(centers_of(packed), ATOMS)
    at_partner = match(partners_of(packed), ATOMS)
    ei, ej = ei_ref[...], ej_ref[...]
    a, v = av_ref[:CHAN], av_ref[CHAN:]
    na, nv = nav_ref[:CHAN], nav_ref[CHAN:]
    tbar = tb_ref[...]
    cbar = tbar * v
    h = h_ref[...]
    gate = jax.nn.sigmoid(h)
    out = wo_ref[...]
    score = jnp.sum(out * (lat_ref[...] + h * gate), axis=0, keepdims=True)
    energy_ref[...] = put(jnp.concatenate([cut * score, jnp.zeros((7, PAIRS), F32)], axis=0), at_center)[0:4]
    ubar = cut * out
    hbar = ubar * (gate * (1.0 + h * (1.0 - gate)))
    lbar = ubar + weighted_t(wm_ref[0:128], hbar)
    coupling = 0.0
    to_center, to_partner, along = [], [], []
    for k in range(3):
        rows = slice(k * CHAN, (k + 1) * CHAN)
        mixed = unit[k : k + 1] + ej[rows]
        coupling = coupling + ei[rows] * mixed
        to_center.append(cbar * mixed)
        to_partner.append(cbar * ei[rows])
        along.append(jnp.sum(to_partner[k], axis=0, keepdims=True))
    vbar = tbar * coupling
    rbar = slope * score + jnp.sum(lbar * tan_ref[...], axis=0, keepdims=True) + jnp.sum(vbar * nv, axis=0, keepdims=True)
    grad = put(jnp.concatenate(to_center, axis=0), at_center) + put(jnp.concatenate(to_partner, axis=0), at_partner)
    gi = pick(grad, at_center)
    for k in range(3):
        rows = slice(k * CHAN, (k + 1) * CHAN)
        along[k] = along[k] + jnp.sum(a * gi[rows], axis=0, keepdims=True)
        rbar = rbar + unit[k : k + 1] * jnp.sum(na * gi[rows], axis=0, keepdims=True)
    part_ref[...] = jnp.concatenate(along + [rbar, jnp.zeros((4, PAIRS), F32)], axis=0)


def k_env_back(packed_ref, scal_ref, av_ref, nav_ref, part_ref, back_ref, column_ref, msg_ref, dbar_ref):
    packed = packed_ref[...]
    scal = scal_ref[...]
    unit, inv = scal[0:3], scal[4:5]
    part = part_ref[...]
    named = jnp.where(column_ref[:, 0:1].astype(jnp.int32) == centers_of(packed), 1.0, 0.0).astype(BF16)
    high, low = split2(back_ref[...])
    gi = dot(high, named, 0, 0) + dot(low, named, 0, 0)
    a, na = av_ref[:CHAN], nav_ref[:CHAN]
    along = []
    rbar = part[3:4]
    for k in range(3):
        rows = slice(k * CHAN, (k + 1) * CHAN)
        along.append(part[k : k + 1] + jnp.sum(a * gi[rows], axis=0, keepdims=True))
        rbar = rbar + unit[k : k + 1] * jnp.sum(na * gi[rows], axis=0, keepdims=True)
    for k in range(3):
        rbar = rbar - inv * along[k] * unit[k : k + 1]
    dbar = jnp.concatenate([along[k] * inv + rbar * unit[k : k + 1] for k in range(3)] + [jnp.zeros((5, PAIRS), F32)], axis=0)
    slots = match(ghost_slot(partners_of(packed)), 512)
    msg_ref[...] = put_rows(dbar, slots)[:, :4]
    dbar_ref[...] = dbar


def k_own_force(packed_ref, dbar_ref, out_ref):
    packed = packed_ref[...]
    dbar = dbar_ref[...]
    out_ref[...] = put(dbar, match(partners_of(packed), ATOMS)) - put(dbar, match(centers_of(packed), ATOMS))


def k_force(own_ref, back_ref, column_ref, energy_ref, out_ref):
    named = jnp.where(
        column_ref[:, 0:1].astype(jnp.int32) == lax.broadcasted_iota(jnp.int32, (LIST, ATOMS), 1), 1.0, 0.0
    ).astype(BF16)
    high, mid, low = split3(back_ref[...])
    returned = dot(high, named, 0, 0) + (dot(mid, named, 0, 0) + dot(low, named, 0, 0))
    total = -(own_ref[0:3] + returned[0:3])
    energy = energy_ref[...]
    for k in range(3):
        for i in range(4):
            out_ref[4 * k + i : 4 * k + i + 1] = total[k : k + 1, 128 * i : 128 * i + 128]
    for i in range(4):
        out_ref[12 + i : 13 + i] = energy[0:1, 128 * i : 128 * i + 128]


def call(kernel, outs, *args):
    shapes = [jax.ShapeDtypeStruct(s, F32) for s in outs]
    spec = pl.BlockSpec(memory_space=pltpu.VMEM)
    return pl.pallas_call(
        kernel,
        out_shape=shapes,
        in_specs=[spec] * len(args),
        out_specs=[spec] * len(outs),
        compiler_params=pltpu.CompilerParams(vmem_limit_bytes=48 * 1024 * 1024),
        name=kernel.__name__,
    )(*args)


GRID_SHIFT = np.zeros((4, 4, 4, 8, 4), np.float32)
for _axis in range(3):
    _at = [slice(None)] * 3
    _at[_axis] = 0
    GRID_SHIFT[tuple(_at) + (slice(None), _axis)] = -6.0
    _at[_axis] = 3
    GRID_SHIFT[tuple(_at) + (slice(None), _axis)] = 6.0
GRID_SHIFT = GRID_SHIFT.reshape(512, 4)


def shards(
    positions,
    species,
    send_lists,
    pair_center,
    pair_partner,
    pair_slot_live,
    w_basis,
    emb_center,
    emb_partner,
    w_env,
    w_value,
    w_mix,
    w_out,
):
    packed = jnp.concatenate(
        [
            positions.reshape(12, 128),
            species.reshape(4, 128).astype(F32),
            pair_center.reshape(8, 128).astype(F32),
            pair_partner.reshape(8, 128).astype(F32),
            pair_slot_live.reshape(8, 128).astype(F32),
            jnp.pad(send_lists.reshape(1, LIST).astype(F32), ((0, 7), (0, 64)), constant_values=-1.0),
        ],
        axis=0,
    )
    zeros = jnp.zeros((2, 128), F32)
    wb = jnp.concatenate([w_basis, emb_center, zeros, emb_partner, zeros], axis=0)
    wav = jnp.concatenate([w_env, w_value], axis=1)
    wo = w_out.reshape(128, 1)

    packed = lax.ppermute(packed, AXES, MOVE_IN)
    msg, column = call(k_lists, [(LIST, 4), (LIST, 8)], packed)
    (part,) = call(k_own_pairs, [(8, PAIRS)], packed)
    ghost = spread(msg.reshape(2, 2, 2, 8, 4)).reshape(512, 4)
    msg, scal, pre, av = call(
        k_features,
        [(LIST, 192), (8, PAIRS), (128, PAIRS), (128, PAIRS)],
        packed,
        part,
        ghost,
        jnp.asarray(GRID_SHIFT),
        column,
        wb,
        wav,
    )
    ei, ej, latent, hid, tangent, nav = call(
        k_own_env,
        [(192, PAIRS), (192, PAIRS)] + [(128, PAIRS)] * 4,
        packed,
        scal,
        pre,
        av,
        wb,
        wav,
        w_mix,
    )
    ghost = spread(msg.reshape(2, 2, 2, 8, 192)).reshape(512, 192)
    msg, ej, h, tbar = call(
        k_energy,
        [(512, 192), (192, PAIRS), (128, PAIRS), (CHAN, PAIRS)],
        packed,
        scal,
        av,
        ghost,
        ei,
        ej,
        hid,
        w_mix,
        wo,
    )
    part, energy = call(
        k_direct,
        [(8, PAIRS), (4, ATOMS)],
        packed,
        scal,
        av,
        nav,
        ei,
        ej,
        latent,
        tangent,
        h,
        tbar,
        w_mix,
        wo,
    )
    back = collect(msg.reshape(4, 4, 4, 8, 192)).reshape(LIST, 192)
    msg, dbar = call(k_env_back, [(512, 4), (8, PAIRS)], packed, scal, av, nav, part, back, column)
    (own,) = call(k_own_force, [(8, ATOMS)], packed, dbar)
    back = collect(msg.reshape(4, 4, 4, 8, 4)).reshape(LIST, 4)
    (out,) = call(k_force, [(16, 128)], own, back, column, energy)
    out = lax.ppermute(out, AXES, MOVE_OUT)
    return out[:12].reshape(3, 1, 1, 1, ATOMS), out[12:].reshape(1, 1, 1, ATOMS)


def solution(mesh):
    in_specs = (
        P(None, "gx", "gy", "gz", None),
        P("gx", "gy", "gz", None),
        P("gx", "gy", "gz", None),
        P("gx", "gy", "gz", None, None),
        P("gx", "gy", "gz", None, None),
        P("gx", "gy", "gz", None, None),
        P(),
        P(),
        P(),
        P(),
        P(),
        P(),
        P(),
    )
    out_specs = (P(None, "gx", "gy", "gz", None), P("gx", "gy", "gz", None))
    return jax.shard_map(shards, mesh=mesh, in_specs=in_specs, out_specs=out_specs, check_vma=False)
```

```python
import math

import jax
import jax.numpy as jnp

from jax import lax
from jax.experimental import pallas as pl
from jax.experimental.pallas import tpu as pltpu
from jax.sharding import PartitionSpec as P

AXES = ("gx", "gy", "gz")
SHAPE = (16, 4, 8)
ATOMS = 512
PAIRS = 1024
LIST = 64
CHAN = 64
STEP = math.pi / 12.0
F32 = jnp.float32
BF16 = jnp.bfloat16


def flat(x, y, z):
    return (x * SHAPE[1] + y) * SHAPE[2] + z


def device(chip_x, chip_y, chip_z, core):
    return flat((chip_z % 8) * 2 + core, chip_y, (chip_z // 8) * 4 + chip_x)


def home(x, y, z):
    x, y, z = x % SHAPE[0], y % SHAPE[1], z % SHAPE[2]
    return device(*PLACE(x, y, z))


def PLACE(x, y, z):
    return z // 2, y, x, z % 2


CELLS = [(x, y, z) for x in range(SHAPE[0]) for y in range(SHAPE[1]) for z in range(SHAPE[2])]
CHIPS = [(x, y, z, c) for x in range(4) for y in range(4) for z in range(16) for c in range(2)]
MOVE_IN = [(flat(*c), home(*c)) for c in CELLS]
MOVE_OUT = [(b, a) for a, b in MOVE_IN]
UP = [(home(x, y, z), home(x, y, z + 1)) for x, y, z in CELLS]
DOWN = [(b, a) for a, b in UP]


def along(spot, axis, position, core):
    spot = list(spot)
    spot[axis], spot[3] = position, core
    return device(*spot)


def snake(axis, count):
    pairs = []
    for spot in CHIPS:
        at, core = spot[axis], spot[3]
        then = at + 1 - 2 * core
        goal = along(spot, axis, then, core) if 0 <= then < count else along(spot, axis, at, 1 - core)
        pairs.append((device(*spot), goal))
    return pairs


def ends(axis, count):
    return [(device(*s), along(s, axis, count - 1 - s[axis], s[3])) for s in CHIPS if s[axis] in (0, count - 1)]


RINGS = {0: (2, 16), 1: (1, 4)}
FORTH = {a: snake(*r) for a, r in RINGS.items()}
BACK = {a: [(j, i) for i, j in p] for a, p in FORTH.items()}
ENDS = {a: ends(*r) for a, r in RINGS.items()}


def send(x, pairs):
    return lax.ppermute(x, AXES, pairs)


def spots():
    gx, gy, gz = (lax.axis_index(a) for a in AXES)
    return {0: (gz // 4) * 8 + gx // 2, 1: gy, 2: gx % 2}


def swap(axis, first, last, here):
    at, upward, count = here[axis], here[2] == 0, RINGS[axis][1]
    forth = send(jnp.where(upward, last, first), FORTH[axis])
    ring = send(jnp.where(at == 0, first, last), ENDS[axis])
    back = send(jnp.where(upward, first, last), BACK[axis])
    before = jnp.where(at != 0, jnp.where(upward, forth, back), ring)
    after = jnp.where(at != count - 1, jnp.where(upward, back, forth), ring)
    return before, after


def spread(low, high, here):
    before, after = swap(0, low, high, here)
    cells = jnp.concatenate([before, low, high, after], axis=0)
    before, after = swap(1, cells[:, 0:1], cells[:, 1:2], here)
    cells = jnp.concatenate([before, cells, after], axis=1)
    before = send(cells[:, :, 1], UP)
    after = send(cells[:, :, 0], DOWN)
    return before, after, cells


def collect(before, after, cells, here):
    first = send(after, UP)
    last = send(before, DOWN)
    cells = cells + jnp.stack([first, last], axis=2)
    for axis in (1, 0):
        first = lax.slice_in_dim(cells, 0, 1, axis=axis)
        last = lax.slice_in_dim(cells, 3, 4, axis=axis)
        from_before, from_after = swap(axis, first, last, here)
        cells = lax.slice_in_dim(cells, 1, 3, axis=axis) + jnp.concatenate([from_before, from_after], axis=axis)
    return cells


def split2(x):
    high = x.astype(BF16)
    low = (x - high.astype(F32)).astype(BF16)
    return high, low


def split3(x):
    high = x.astype(BF16)
    rest = x - high.astype(F32)
    mid = rest.astype(BF16)
    return high, mid, (rest - mid.astype(F32)).astype(BF16)


def dot(a, b, ca, cb):
    return lax.dot_general(a, b, (((ca,), (cb,)), ((), ())), preferred_element_type=F32)


def weighted(w, x):
    wh, wl = split2(w)
    xh, xl = split2(x)
    return dot(wh, xh, 0, 0) + (dot(wl, xh, 0, 0) + dot(wh, xl, 0, 0))


def weighted_t(w, x):
    wh, wl = split2(w)
    xh, xl = split2(x)
    return dot(wh, xh, 1, 0) + (dot(wl, xh, 1, 0) + dot(wh, xl, 1, 0))


def pick(table, onehot, parts=2):
    rows = table.shape[0]
    pieces = split3(table) if parts == 3 else split2(table)
    full = dot(jnp.concatenate(pieces, axis=0), onehot, 1, 0)
    out = full[:rows]
    for i in range(1, parts):
        out = out + full[rows * i : rows * (i + 1)]
    return out


def put(values, onehot, parts=2):
    rows = values.shape[0]
    pieces = split3(values) if parts == 3 else split2(values)
    full = dot(jnp.concatenate(pieces, axis=0), onehot, 1, 1)
    out = full[:rows]
    for i in range(1, parts):
        out = out + full[rows * i : rows * (i + 1)]
    return out


def put_rows(values, onehot):
    high, low = split2(values)
    return dot(onehot, high, 1, 1) + dot(onehot, low, 1, 1)


def lanes(block):
    return jnp.concatenate([block[i : i + 1] for i in range(block.shape[0])], axis=1)


def match(index, count):
    ids = lax.broadcasted_iota(jnp.int32, (count, index.shape[1]), 0)
    return jnp.where(ids == index, 1.0, 0.0).astype(BF16)


def centers_of(packed):
    return lanes(packed[16:24]).astype(jnp.int32)


def partners_of(packed):
    return lanes(packed[24:32]).astype(jnp.int32)


def live_of(packed):
    return lanes(packed[32:40])


def own_table(packed):
    return jnp.concatenate([lanes(packed[4 * k : 4 * k + 4]) for k in range(4)], axis=0)


def ghost_cell(partners):
    rows = partners - ATOMS
    cell = rows >> 3
    skip = jnp.zeros_like(cell)
    for start in (21, 23, 33, 35):
        skip = skip + jnp.where(cell >= start, 2, 0)
    full = cell + skip
    return full >> 4, (full >> 2) & 3, full & 3, rows & 7


def ghost_slot(partners):
    p, q, r, atom = ghost_cell(partners)
    column = p * 4 + q
    slot = jnp.where(r == 0, column * 8, jnp.where(r == 3, column * 8 + 128, 256 + (column * 2 + r - 1) * 8)) + atom
    return jnp.where(partners >= ATOMS, slot, -1)


def k_pack(pos_in, kind_in, names_in, center_in, partner_in, live_in, out_ref, pos_ref, kind_ref, names_ref, center_ref, partner_ref, live_ref, sems):
    moves = [
        pltpu.make_async_copy(source, target, sems.at[i])
        for i, (source, target) in enumerate(
            [
                (pos_in, pos_ref),
                (kind_in, kind_ref),
                (names_in, names_ref),
                (center_in, center_ref),
                (partner_in, partner_ref),
                (live_in, live_ref),
            ]
        )
    ]
    for move in moves:
        move.start()
    out_ref[40:48] = jnp.zeros((8, 128), F32)
    for move in moves:
        move.wait()
    for k in range(3):
        for i in range(4):
            out_ref[4 * k + i : 4 * k + i + 1] = pos_ref[k, 0, 0, 0:1, 128 * i : 128 * i + 128]
    for i in range(4):
        out_ref[12 + i : 13 + i] = kind_ref[0, 0, 0:1, 128 * i : 128 * i + 128].astype(F32)
    out_ref[16:24] = center_ref[0, 0, 0].astype(F32)
    out_ref[24:32] = partner_ref[0, 0, 0].astype(F32)
    out_ref[32:40] = live_ref[0, 0, 0].astype(F32)
    names = [names_ref[i, j, k : k + 1] for i in range(2) for j in range(2) for k in range(2)]
    names.append(jnp.full((1, 64), -1, jnp.int32))
    out_ref[40:41] = jnp.concatenate(names, axis=1).astype(F32)


def pack(*args):
    return pl.pallas_call(
        k_pack,
        out_shape=jax.ShapeDtypeStruct((48, 128), F32),
        in_specs=[pl.BlockSpec(memory_space=pltpu.MemorySpace.HBM)] * len(args),
        out_specs=pl.BlockSpec(memory_space=pltpu.VMEM),
        scratch_shapes=[pltpu.VMEM(a.shape, a.dtype) for a in args] + [pltpu.SemaphoreType.DMA((len(args),))],
        compiler_params=pltpu.CompilerParams(vmem_limit_bytes=48 * 1024 * 1024),
        name="k_pack",
    )(*args)


def k_lists(packed_ref, low_ref, high_ref, column_ref):
    packed = packed_ref[...]
    names = packed[40:41].astype(jnp.int32)
    found = pick(own_table(packed), match(names, ATOMS), 3)
    wide = jnp.concatenate([found, jnp.zeros((124, 128), F32)], axis=0).T
    low_ref[...] = wide[:32]
    high_ref[...] = wide[32:64]
    column_ref[...] = jnp.broadcast_to(packed[40:41], (8, 128)).T[:LIST]


def k_own_pairs(packed_ref, out_ref):
    packed = packed_ref[...]
    table = own_table(packed)
    at_center = pick(table, match(centers_of(packed), ATOMS), 3)
    at_partner = pick(table, match(partners_of(packed), ATOMS), 3)
    out_ref[0:3] = at_partner[0:3] - at_center[0:3]
    out_ref[3:4] = at_partner[3:4]
    out_ref[4:5] = at_center[3:4]
    out_ref[5:8] = jnp.zeros((3, PAIRS), F32)


def k_features(
    packed_ref, part_ref, before_ref, after_ref, cells_ref, column_ref, wb_ref, wav_ref, low_ref, high_ref, scal_ref, pre_ref, av_ref
):
    packed = packed_ref[...]
    part = part_ref[...]
    ghost = jnp.concatenate([before_ref[...], after_ref[...], cells_ref[...]], axis=0).T[0:8]
    partners = partners_of(packed)
    slots = match(ghost_slot(partners), 512)
    pieces = split3(ghost)
    far = dot(jnp.concatenate(pieces, axis=0), slots, 1, 0)
    far = far[0:8] + (far[8:16] + far[16:24])
    moved = [jnp.where(c == 0, -6.0, jnp.where(c == 3, 6.0, 0.0)) for c in ghost_cell(partners)[:3]]
    moved = jnp.where(partners >= ATOMS, jnp.concatenate(moved, axis=0), 0.0)
    disp = part[0:3] + (far[0:3] + moved)
    partner_kind = part[3:4] + far[3:4]
    center_kind = part[4:5]
    radius = jnp.sqrt(jnp.sum(disp * disp, axis=0, keepdims=True) + 0.25)
    inv = 1.0 / radius
    unit = disp * inv
    scaled = radius * 0.2
    base = 1.0 + scaled * scaled
    live = live_of(packed)
    cut = live / (base * base)
    orders = lax.broadcasted_iota(jnp.int32, (8, 1), 0).astype(F32) + 1.0
    angle = radius * orders * STEP
    basis = jnp.sin(angle) * inv
    kinds = lax.broadcasted_iota(jnp.int32, (8, 1), 0).astype(F32)
    first = jnp.where(center_kind == kinds, 1.0, 0.0)
    second = jnp.where(partner_kind == kinds, 1.0, 0.0)
    pre = weighted(wb_ref[...], jnp.concatenate([basis, first, second], axis=0))
    latent = cut * (pre * jax.nn.sigmoid(pre))
    av = weighted(wav_ref[...], latent)
    a = av[:CHAN]
    terms = jnp.concatenate([unit[k : k + 1] * a for k in range(3)], axis=0)
    named = jnp.where(column_ref[:, 0:1].astype(jnp.int32) == centers_of(packed), 1.0, 0.0).astype(BF16)
    msg = put_rows(terms, named)
    low_ref[...] = msg[:32]
    high_ref[...] = msg[32:]
    scal_ref[0:3] = unit
    scal_ref[3:4] = radius
    scal_ref[4:5] = inv
    scal_ref[5:6] = cut
    scal_ref[6:7] = live * (-0.8) * scaled / (base * base * base)
    scal_ref[7:8] = live
    pre_ref[...] = pre
    av_ref[...] = av


def k_own_env(packed_ref, scal_ref, pre_ref, av_ref, wb_ref, wav_ref, wm_ref, ei_ref, ej_ref, lat_ref, hid_ref, tan_ref, nav_ref):
    packed = packed_ref[...]
    scal = scal_ref[...]
    unit, radius, inv, cut, slope = scal[0:3], scal[3:4], scal[4:5], scal[5:6], scal[6:7]
    av = av_ref[...]
    a = av[:CHAN]
    terms = jnp.concatenate([unit[k : k + 1] * a for k in range(3)], axis=0)
    at_center = match(centers_of(packed), ATOMS)
    env = put(terms, at_center)
    ei_ref[...] = pick(env, at_center)
    ej_ref[...] = pick(env, match(partners_of(packed), ATOMS))
    pre = pre_ref[...]
    gate = jax.nn.sigmoid(pre)
    act = pre * gate
    latent = cut * act
    lat_ref[...] = latent
    hid_ref[...] = weighted(wm_ref[0:128], latent)
    orders = lax.broadcasted_iota(jnp.int32, (8, 1), 0).astype(F32) + 1.0
    angle = radius * orders * STEP
    change = (jnp.cos(angle) * (orders * STEP) - jnp.sin(angle) * inv) * inv
    tangent = slope * act + cut * (gate * (1.0 + pre * (1.0 - gate))) * weighted(wb_ref[0:8], change)
    tan_ref[...] = tangent
    nav_ref[...] = weighted(wav_ref[...], tangent)


def k_energy(
    packed_ref,
    scal_ref,
    av_ref,
    before_ref,
    after_ref,
    cells_ref,
    ei_ref,
    ejown_ref,
    hid_ref,
    wm_ref,
    wo_ref,
    to_before_ref,
    to_after_ref,
    to_cells_ref,
    ej_ref,
    h_ref,
    tb_ref,
):
    packed = packed_ref[...]
    scal = scal_ref[...]
    unit, cut = scal[0:3], scal[5:6]
    slots = match(ghost_slot(partners_of(packed)), 512)
    high, low = split2(jnp.concatenate([before_ref[...], after_ref[...], cells_ref[...]], axis=0))
    ej = ejown_ref[...] + (dot(high, slots, 0, 0) + dot(low, slots, 0, 0))
    ei = ei_ref[...]
    coupling = 0.0
    for k in range(3):
        rows = slice(k * CHAN, (k + 1) * CHAN)
        coupling = coupling + ei[rows] * (unit[k : k + 1] + ej[rows])
    v = av_ref[CHAN:]
    mix = wm_ref[128:]
    h = hid_ref[...] + weighted(mix, v * coupling)
    gate = jax.nn.sigmoid(h)
    out = wo_ref[...]
    hbar = (cut * out) * (gate * (1.0 + h * (1.0 - gate)))
    tbar = weighted_t(mix, hbar)
    cbar = tbar * v
    back = jnp.concatenate([cbar * ei[k * CHAN : (k + 1) * CHAN] for k in range(3)], axis=0)
    msg = put_rows(back, slots)
    to_before_ref[...] = msg[:128]
    to_after_ref[...] = msg[128:256]
    to_cells_ref[...] = msg[256:]
    ej_ref[...] = ej
    h_ref[...] = h
    tb_ref[...] = tbar


def k_direct(
    packed_ref, scal_ref, av_ref, nav_ref, ei_ref, ej_ref, lat_ref, tan_ref, h_ref, tb_ref, wm_ref, wo_ref, part_ref, energy_ref
):
    packed = packed_ref[...]
    scal = scal_ref[...]
    unit, cut, slope = scal[0:3], scal[5:6], scal[6:7]
    at_center = match(centers_of(packed), ATOMS)
    at_partner = match(partners_of(packed), ATOMS)
    ei, ej = ei_ref[...], ej_ref[...]
    a, v = av_ref[:CHAN], av_ref[CHAN:]
    na, nv = nav_ref[:CHAN], nav_ref[CHAN:]
    tbar = tb_ref[...]
    cbar = tbar * v
    h = h_ref[...]
    gate = jax.nn.sigmoid(h)
    out = wo_ref[...]
    score = jnp.sum(out * (lat_ref[...] + h * gate), axis=0, keepdims=True)
    energy_ref[...] = put(jnp.concatenate([cut * score, jnp.zeros((7, PAIRS), F32)], axis=0), at_center)[0:4]
    ubar = cut * out
    hbar = ubar * (gate * (1.0 + h * (1.0 - gate)))
    lbar = ubar + weighted_t(wm_ref[0:128], hbar)
    coupling = 0.0
    to_center, to_partner, along = [], [], []
    for k in range(3):
        rows = slice(k * CHAN, (k + 1) * CHAN)
        mixed = unit[k : k + 1] + ej[rows]
        coupling = coupling + ei[rows] * mixed
        to_center.append(cbar * mixed)
        to_partner.append(cbar * ei[rows])
        along.append(jnp.sum(to_partner[k], axis=0, keepdims=True))
    vbar = tbar * coupling
    rbar = slope * score + jnp.sum(lbar * tan_ref[...], axis=0, keepdims=True) + jnp.sum(vbar * nv, axis=0, keepdims=True)
    grad = put(jnp.concatenate(to_center, axis=0), at_center) + put(jnp.concatenate(to_partner, axis=0), at_partner)
    gi = pick(grad, at_center)
    for k in range(3):
        rows = slice(k * CHAN, (k + 1) * CHAN)
        along[k] = along[k] + jnp.sum(a * gi[rows], axis=0, keepdims=True)
        rbar = rbar + unit[k : k + 1] * jnp.sum(na * gi[rows], axis=0, keepdims=True)
    part_ref[...] = jnp.concatenate(along + [rbar, jnp.zeros((4, PAIRS), F32)], axis=0)


def k_env_back(
    packed_ref,
    scal_ref,
    av_ref,
    nav_ref,
    part_ref,
    back_ref,
    column_ref,
    to_before_ref,
    to_after_ref,
    to_cells_ref,
    dbar_ref,
):
    packed = packed_ref[...]
    scal = scal_ref[...]
    unit, inv = scal[0:3], scal[4:5]
    part = part_ref[...]
    named = jnp.where(column_ref[:, 0:1].astype(jnp.int32) == centers_of(packed), 1.0, 0.0).astype(BF16)
    high, low = split2(back_ref[...])
    gi = dot(high, named, 0, 0) + dot(low, named, 0, 0)
    a, na = av_ref[:CHAN], nav_ref[:CHAN]
    along = []
    rbar = part[3:4]
    for k in range(3):
        rows = slice(k * CHAN, (k + 1) * CHAN)
        along.append(part[k : k + 1] + jnp.sum(a * gi[rows], axis=0, keepdims=True))
        rbar = rbar + unit[k : k + 1] * jnp.sum(na * gi[rows], axis=0, keepdims=True)
    for k in range(3):
        rbar = rbar - inv * along[k] * unit[k : k + 1]
    dbar = jnp.concatenate([along[k] * inv + rbar * unit[k : k + 1] for k in range(3)] + [jnp.zeros((5, PAIRS), F32)], axis=0)
    slots = match(ghost_slot(partners_of(packed)), 512)
    msg = jnp.concatenate([put_rows(dbar, slots), jnp.zeros((512, 120), F32)], axis=1)
    to_before_ref[...] = msg[:128]
    to_after_ref[...] = msg[128:256]
    to_cells_ref[...] = msg[256:]
    dbar_ref[...] = dbar


def k_own_force(packed_ref, dbar_ref, out_ref):
    packed = packed_ref[...]
    dbar = dbar_ref[...]
    out_ref[...] = put(dbar, match(partners_of(packed), ATOMS)) - put(dbar, match(centers_of(packed), ATOMS))


def k_force(own_ref, back_ref, column_ref, energy_ref, out_ref):
    named = jnp.where(
        column_ref[:, 0:1].astype(jnp.int32) == lax.broadcasted_iota(jnp.int32, (LIST, ATOMS), 1), 1.0, 0.0
    ).astype(BF16)
    returned = pick(back_ref[...].T[0:8], named, 3)
    total = -(own_ref[0:3] + returned[0:3])
    energy = energy_ref[...]
    for k in range(3):
        for i in range(4):
            out_ref[4 * k + i : 4 * k + i + 1] = total[k : k + 1, 128 * i : 128 * i + 128]
    for i in range(4):
        out_ref[12 + i : 13 + i] = energy[0:1, 128 * i : 128 * i + 128]


def k_unpack(in_ref, force_ref, energy_ref):
    for k in range(3):
        for i in range(4):
            force_ref[k, 0, 0, 0:1, 128 * i : 128 * i + 128] = in_ref[4 * k + i : 4 * k + i + 1]
    for i in range(4):
        energy_ref[0, 0, 0:1, 128 * i : 128 * i + 128] = in_ref[12 + i : 13 + i]


def call(kernel, outs, *args):
    shapes = [jax.ShapeDtypeStruct(s, F32) for s in outs]
    spec = pl.BlockSpec(memory_space=pltpu.VMEM)
    return pl.pallas_call(
        kernel,
        out_shape=shapes,
        in_specs=[spec] * len(args),
        out_specs=[spec] * len(outs),
        compiler_params=pltpu.CompilerParams(vmem_limit_bytes=48 * 1024 * 1024),
        name=kernel.__name__,
    )(*args)


def shards(
    positions,
    species,
    send_lists,
    pair_center,
    pair_partner,
    pair_slot_live,
    w_basis,
    emb_center,
    emb_partner,
    w_env,
    w_value,
    w_mix,
    w_out,
):
    packed = pack(positions, species, send_lists, pair_center, pair_partner, pair_slot_live)
    here = spots()
    zeros = jnp.zeros((2, 128), F32)
    wb = jnp.concatenate([w_basis, emb_center, zeros, emb_partner, zeros], axis=0)
    wav = jnp.concatenate([w_env, w_value], axis=1)
    wo = w_out.reshape(128, 1)

    packed = send(packed, MOVE_IN)
    low, high, column = call(k_lists, [(32, 128), (32, 128), (LIST, 8)], packed)
    (part,) = call(k_own_pairs, [(8, PAIRS)], packed)
    low, high = low.reshape(1, 2, 2, 8, 128), high.reshape(1, 2, 2, 8, 128)
    ghosts = [g.reshape(-1, 128) for g in spread(low, high, here)]
    low, high, scal, pre, av = call(
        k_features,
        [(32, 192), (32, 192), (8, PAIRS), (128, PAIRS), (128, PAIRS)],
        packed,
        part,
        *ghosts,
        column,
        wb,
        wav,
    )
    ei, ej, latent, hid, tangent, nav = call(
        k_own_env,
        [(192, PAIRS), (192, PAIRS)] + [(128, PAIRS)] * 4,
        packed,
        scal,
        pre,
        av,
        wb,
        wav,
        w_mix,
    )
    low, high = low.reshape(1, 2, 2, 8, 192), high.reshape(1, 2, 2, 8, 192)
    ghosts = [g.reshape(-1, 192) for g in spread(low, high, here)]
    before, after, cells, ej, h, tbar = call(
        k_energy,
        [(128, 192), (128, 192), (256, 192), (192, PAIRS), (128, PAIRS), (CHAN, PAIRS)],
        packed,
        scal,
        av,
        *ghosts,
        ei,
        ej,
        hid,
        w_mix,
        wo,
    )
    part, energy = call(
        k_direct,
        [(8, PAIRS), (4, ATOMS)],
        packed,
        scal,
        av,
        nav,
        ei,
        ej,
        latent,
        tangent,
        h,
        tbar,
        w_mix,
        wo,
    )
    before, after = before.reshape(4, 4, 8, 192), after.reshape(4, 4, 8, 192)
    back = collect(before, after, cells.reshape(4, 4, 2, 8, 192), here).reshape(LIST, 192)
    before, after, cells, dbar = call(
        k_env_back, [(128, 128), (128, 128), (256, 128), (8, PAIRS)], packed, scal, av, nav, part, back, column
    )
    (own,) = call(k_own_force, [(8, ATOMS)], packed, dbar)
    before, after = before.reshape(4, 4, 8, 128), after.reshape(4, 4, 8, 128)
    back = collect(before, after, cells.reshape(4, 4, 2, 8, 128), here).reshape(LIST, 128)
    (out,) = call(k_force, [(16, 128)], own, back, column, energy)
    out = send(out, MOVE_OUT)
    return call(k_unpack, [(3, 1, 1, 1, ATOMS), (1, 1, 1, ATOMS)], out)


def solution(mesh):
    in_specs = (
        P(None, "gx", "gy", "gz", None),
        P("gx", "gy", "gz", None),
        P("gx", "gy", "gz", None),
        P("gx", "gy", "gz", None, None),
        P("gx", "gy", "gz", None, None),
        P("gx", "gy", "gz", None, None),
        P(),
        P(),
        P(),
        P(),
        P(),
        P(),
        P(),
    )
    out_specs = (P(None, "gx", "gy", "gz", None), P("gx", "gy", "gz", None))
    return jax.shard_map(shards, mesh=mesh, in_specs=in_specs, out_specs=out_specs, check_vma=False)
```

```python
import math

import jax
import jax.numpy as jnp

from jax import lax
from jax.experimental import pallas as pl
from jax.experimental.pallas import tpu as pltpu
from jax.sharding import PartitionSpec as P

AXES = ("gx", "gy", "gz")
SHAPE = (16, 4, 8)
ATOMS = 512
PAIRS = 1024
LIST = 64
CHAN = 64
STEP = math.pi / 12.0
F32 = jnp.float32
BF16 = jnp.bfloat16


def flat(x, y, z):
    return (x * SHAPE[1] + y) * SHAPE[2] + z


def device(chip_x, chip_y, chip_z, core):
    return flat((chip_z % 8) * 2 + core, chip_y, (chip_z // 8) * 4 + chip_x)


def home(x, y, z):
    x, y, z = x % SHAPE[0], y % SHAPE[1], z % SHAPE[2]
    return device((z // 2 + 3) % 4, y, (x - 4) % 16, z % 2)


CELLS = [(x, y, z) for x in range(SHAPE[0]) for y in range(SHAPE[1]) for z in range(SHAPE[2])]
CHIPS = [(x, y, z, c) for x in range(4) for y in range(4) for z in range(16) for c in range(2)]
MOVE_IN = [(flat(*c), home(*c)) for c in CELLS]
MOVE_OUT = [(b, a) for a, b in MOVE_IN]
UP = [(home(x, y, z), home(x, y, z + 1)) for x, y, z in CELLS]
DOWN = [(b, a) for a, b in UP]


def along(spot, axis, position, core):
    spot = list(spot)
    spot[axis], spot[3] = position, core
    return device(*spot)


def snake(axis, count):
    pairs = []
    for spot in CHIPS:
        at, core = spot[axis], spot[3]
        then = at + 1 - 2 * core
        goal = along(spot, axis, then, core) if 0 <= then < count else along(spot, axis, at, 1 - core)
        pairs.append((device(*spot), goal))
    return pairs


def ends(axis, count):
    return [(device(*s), along(s, axis, count - 1 - s[axis], s[3])) for s in CHIPS if s[axis] in (0, count - 1)]


RINGS = {0: (2, 16), 1: (1, 4)}
FORTH = {a: snake(*r) for a, r in RINGS.items()}
BACK = {a: [(j, i) for i, j in p] for a, p in FORTH.items()}
ENDS = {a: ends(*r) for a, r in RINGS.items()}


def send(x, pairs):
    return lax.ppermute(x, AXES, pairs)


def spots():
    gx, gy, gz = (lax.axis_index(a) for a in AXES)
    return {0: (gz // 4) * 8 + gx // 2, 1: gy, 2: gx % 2}


def swap(axis, first, last, here):
    at, upward, count = here[axis], here[2] == 0, RINGS[axis][1]
    forth = send(jnp.where(upward, last, first), FORTH[axis])
    ring = send(jnp.where(at == 0, first, last), ENDS[axis])
    back = send(jnp.where(upward, first, last), BACK[axis])
    start, end = at == 0, at == count - 1
    before = jnp.where(~start, jnp.where(upward, forth, back), jnp.where(start, ring, back))
    after = jnp.where(end, jnp.where(end, ring, back), jnp.where(~upward, forth, back))
    return before, after


def spread(low, high, here):
    before, after = swap(0, low, high, here)
    cells = jnp.concatenate([before, low, high, after], axis=0)
    before, after = swap(1, cells[:, 0:1], cells[:, 1:2], here)
    cells = jnp.concatenate([before, cells, after], axis=1)
    before = send(cells[:, :, 1], UP)
    after = send(cells[:, :, 0], DOWN)
    return before, after, cells


def collect(before, after, cells, here):
    first = send(after, UP)
    last = send(before, DOWN)
    cells = cells + jnp.stack([first, last], axis=2)
    for axis in (1, 0):
        first = lax.slice_in_dim(cells, 0, 1, axis=axis)
        last = lax.slice_in_dim(cells, 3, 4, axis=axis)
        from_before, from_after = swap(axis, first, last, here)
        cells = lax.slice_in_dim(cells, 1, 3, axis=axis) + jnp.concatenate([from_before, from_after], axis=axis)
    return cells


def split2(x):
    high = x.astype(BF16)
    low = (x - high.astype(F32)).astype(BF16)
    return high, low


def split3(x):
    high = x.astype(BF16)
    rest = x - high.astype(F32)
    mid = rest.astype(BF16)
    return high, mid, (rest - mid.astype(F32)).astype(BF16)


def dot(a, b, ca, cb):
    return lax.dot_general(a, b, (((ca,), (cb,)), ((), ())), preferred_element_type=F32)


def weighted(w, x):
    wh, wl = split2(w)
    xh, xl = split2(x)
    return dot(wh, xh, 0, 0) + (dot(wl, xh, 0, 0) + dot(wh, xl, 0, 0))


def weighted_t(w, x):
    wh, wl = split2(w)
    xh, xl = split2(x)
    return dot(wh, xh, 1, 0) + (dot(wl, xh, 1, 0) + dot(wh, xl, 1, 0))


def pick(table, onehot, parts=2):
    rows = table.shape[0]
    pieces = split3(table) if parts == 3 else split2(table)
    full = dot(jnp.concatenate(pieces, axis=0), onehot, 1, 0)
    out = full[:rows]
    for i in range(1, parts):
        out = out + full[rows * i : rows * (i + 1)]
    return out


def put(values, onehot, parts=2):
    rows = values.shape[0]
    pieces = split3(values) if parts == 3 else split2(values)
    full = dot(jnp.concatenate(pieces, axis=0), onehot, 1, 1)
    out = full[:rows]
    for i in range(1, parts):
        out = out + full[rows * i : rows * (i + 1)]
    return out


def put_rows(values, onehot):
    high, low = split2(values)
    return dot(onehot, high, 1, 1) + dot(onehot, low, 1, 1)


def lanes(block):
    return jnp.concatenate([block[i : i + 1] for i in range(block.shape[0])], axis=1)


def match(index, count):
    ids = lax.broadcasted_iota(jnp.int32, (count, index.shape[1]), 0)
    return jnp.where(ids == index, 1.0, 0.0).astype(BF16)


def centers_of(packed):
    return lanes(packed[16:24]).astype(jnp.int32)


def partners_of(packed):
    return lanes(packed[24:32]).astype(jnp.int32)


def live_of(packed):
    return lanes(packed[32:40])


def own_table(packed):
    return jnp.concatenate([lanes(packed[4 * k : 4 * k + 4]) for k in range(4)], axis=0)


def ghost_cell(partners):
    rows = partners - ATOMS
    cell = rows >> 3
    skip = jnp.zeros_like(cell)
    for start in (21, 23, 33, 35):
        skip = skip + jnp.where(cell >= start, 2, 0)
    full = cell + skip
    return full >> 4, (full >> 2) & 3, full & 3, rows & 7


def ghost_slot(partners):
    p, q, r, atom = ghost_cell(partners)
    column = p * 4 + q
    slot = jnp.where(r == 0, column * 8, jnp.where(r == 3, column * 8 + 128, 256 + (column * 2 + r - 1) * 8)) + atom
    return jnp.where(partners >= ATOMS, slot, -1)


def k_pack(pos_in, kind_in, names_in, center_in, partner_in, live_in, out_ref, pos_ref, kind_ref, names_ref, center_ref, partner_ref, live_ref, sems):
    moves = [
        pltpu.make_async_copy(source, target, sems.at[i])
        for i, (source, target) in enumerate(
            [
                (pos_in, pos_ref),
                (kind_in, kind_ref),
                (names_in, names_ref),
                (center_in, center_ref),
                (partner_in, partner_ref),
                (live_in, live_ref),
            ]
        )
    ]
    for move in moves:
        move.start()
    out_ref[40:48] = jnp.zeros((8, 128), F32)
    for move in moves:
        move.wait()
    for k in range(3):
        for i in range(4):
            out_ref[4 * k + i : 4 * k + i + 1] = pos_ref[k, 0, 0, 0:1, 128 * i : 128 * i + 128]
    for i in range(4):
        out_ref[12 + i : 13 + i] = kind_ref[0, 0, 0:1, 128 * i : 128 * i + 128].astype(F32)
    out_ref[16:24] = center_ref[0, 0, 0].astype(F32)
    out_ref[24:32] = partner_ref[0, 0, 0].astype(F32)
    out_ref[32:40] = live_ref[0, 0, 0].astype(F32)
    names = [names_ref[i, j, k : k + 1] for i in range(2) for j in range(2) for k in range(2)]
    names.append(jnp.full((1, 64), -1, jnp.int32))
    out_ref[40:41] = jnp.concatenate(names, axis=1).astype(F32)


def pack(*args):
    return pl.pallas_call(
        k_pack,
        out_shape=jax.ShapeDtypeStruct((48, 128), F32),
        in_specs=[pl.BlockSpec(memory_space=pltpu.MemorySpace.HBM)] * len(args),
        out_specs=pl.BlockSpec(memory_space=pltpu.VMEM),
        scratch_shapes=[pltpu.VMEM(a.shape, a.dtype) for a in args] + [pltpu.SemaphoreType.DMA((len(args),))],
        compiler_params=pltpu.CompilerParams(vmem_limit_bytes=60 * 1024 * 1024),
        name="k_pack",
    )(*args)


def k_lists(packed_ref, low_ref, high_ref, column_ref):
    packed = packed_ref[...]
    names = packed[40:41].astype(jnp.int32)
    found = pick(own_table(packed), match(names, ATOMS), 3)
    wide = jnp.concatenate([found, jnp.zeros((124, 128), F32)], axis=0).T
    low_ref[...] = wide[:32]
    high_ref[...] = wide[32:64]
    column_ref[...] = jnp.broadcast_to(packed[40:41], (8, 128)).T[:LIST]


def k_own_pairs(packed_ref, column_ref, out_ref, center_ref, partner_ref, slots_ref, named_ref):
    packed = packed_ref[...]
    table = own_table(packed)
    centers, partners = centers_of(packed), partners_of(packed)
    center_hot, partner_hot = match(centers, ATOMS), match(partners, ATOMS)
    center_ref[...] = center_hot
    partner_ref[...] = partner_hot
    slots_ref[...] = match(ghost_slot(partners), 512)
    named_ref[...] = jnp.where(column_ref[:, 0:1].astype(jnp.int32) == centers, 1.0, 0.0).astype(BF16)
    at_center = pick(table, center_hot, 3)
    at_partner = pick(table, partner_hot, 3)
    out_ref[0:3] = at_partner[0:3] - at_center[0:3]
    out_ref[3:4] = at_partner[3:4]
    out_ref[4:5] = at_center[3:4]
    out_ref[5:8] = jnp.zeros((3, PAIRS), F32)


def k_features(
    packed_ref, part_ref, slots_ref, named_ref, before_ref, after_ref, cells_ref, wb_ref, wav_ref, low_ref, high_ref, scal_ref, pre_ref, av_ref
):
    packed = packed_ref[...]
    part = part_ref[...]
    ghost = jnp.concatenate([before_ref[...], after_ref[...], cells_ref[...]], axis=0).T[0:8]
    partners = partners_of(packed)
    slots = slots_ref[...]
    pieces = split3(ghost)
    far = dot(jnp.concatenate(pieces, axis=0), slots, 1, 0)
    far = far[0:8] + (far[8:16] + far[16:24])
    moved = [jnp.where(c == 0, -6.0, jnp.where(c == 3, 6.0, 0.0)) for c in ghost_cell(partners)[:3]]
    moved = jnp.where(partners >= ATOMS, jnp.concatenate(moved, axis=0), 0.0)
    disp = part[0:3] + (far[0:3] + moved)
    partner_kind = part[3:4] + far[3:4]
    center_kind = part[4:5]
    radius = jnp.sqrt(jnp.sum(disp * disp, axis=0, keepdims=True) + 0.25)
    inv = 1.0 / radius
    unit = disp * inv
    scaled = radius * 0.2
    base = 1.0 + scaled * scaled
    live = live_of(packed)
    cut = live / (base * base)
    orders = lax.broadcasted_iota(jnp.int32, (8, 1), 0).astype(F32) + 1.0
    angle = radius * orders * STEP
    basis = jnp.sin(angle) * inv
    kinds = lax.broadcasted_iota(jnp.int32, (8, 1), 0).astype(F32)
    first = jnp.where(center_kind == kinds, 1.0, 0.0)
    second = jnp.where(partner_kind == kinds, 1.0, 0.0)
    pre = weighted(wb_ref[...], jnp.concatenate([basis, first, second], axis=0))
    latent = cut * (pre * jax.nn.sigmoid(pre))
    av = weighted(wav_ref[...], latent)
    a = av[:CHAN]
    terms = jnp.concatenate([unit[k : k + 1] * a for k in range(3)], axis=0)
    msg = put_rows(terms, named_ref[...])
    low_ref[...] = msg[:32]
    high_ref[...] = msg[32:]
    scal_ref[0:3] = unit
    scal_ref[3:4] = radius
    scal_ref[4:5] = inv
    scal_ref[5:6] = cut
    scal_ref[6:7] = live * (-0.8) * scaled / (base * base * base)
    scal_ref[7:8] = live
    pre_ref[...] = pre
    av_ref[...] = av


def k_own_env(center_ref, partner_ref, scal_ref, pre_ref, av_ref, wb_ref, wav_ref, wm_ref, ei_ref, ej_ref, lat_ref, hid_ref, tan_ref, nav_ref):
    scal = scal_ref[...]
    unit, radius, inv, cut, slope = scal[0:3], scal[3:4], scal[4:5], scal[5:6], scal[6:7]
    av = av_ref[...]
    a = av[:CHAN]
    terms = jnp.concatenate([unit[k : k + 1] * a for k in range(3)], axis=0)
    at_center = center_ref[...]
    env = put(terms, at_center)
    ei_ref[...] = pick(env, at_center)
    ej_ref[...] = pick(env, partner_ref[...])
    pre = pre_ref[...]
    gate = jax.nn.sigmoid(pre)
    act = pre * gate
    latent = cut * act
    lat_ref[...] = latent
    hid_ref[...] = weighted(wm_ref[0:128], latent)
    orders = lax.broadcasted_iota(jnp.int32, (8, 1), 0).astype(F32) + 1.0
    angle = radius * orders * STEP
    change = (jnp.cos(angle) * (orders * STEP) - jnp.sin(angle) * inv) * inv
    tangent = slope * act + cut * (gate * (1.0 + pre * (1.0 - gate))) * weighted(wb_ref[0:8], change)
    tan_ref[...] = tangent
    nav_ref[...] = weighted(wav_ref[...], tangent)


def k_energy(
    slots_ref,
    scal_ref,
    av_ref,
    before_ref,
    after_ref,
    cells_ref,
    ei_ref,
    ejown_ref,
    hid_ref,
    wm_ref,
    wo_ref,
    to_before_ref,
    to_after_ref,
    to_cells_ref,
    ej_ref,
    h_ref,
    tb_ref,
):
    scal = scal_ref[...]
    unit, cut = scal[0:3], scal[5:6]
    slots = slots_ref[...]
    high, low = split2(jnp.concatenate([before_ref[...], after_ref[...], cells_ref[...]], axis=0))
    ej = ejown_ref[...] + (dot(high, slots, 0, 0) + dot(low, slots, 0, 0))
    ei = ei_ref[...]
    coupling = 0.0
    for k in range(3):
        rows = slice(k * CHAN, (k + 1) * CHAN)
        coupling = coupling + ei[rows] * (unit[k : k + 1] + ej[rows])
    v = av_ref[CHAN:]
    mix = wm_ref[128:]
    h = hid_ref[...] + weighted(mix, v * coupling)
    gate = jax.nn.sigmoid(h)
    out = wo_ref[...]
    hbar = (cut * out) * (gate * (1.0 + h * (1.0 - gate)))
    tbar = weighted_t(mix, hbar)
    cbar = tbar * v
    back = jnp.concatenate([cbar * ei[k * CHAN : (k + 1) * CHAN] for k in range(3)], axis=0)
    msg = put_rows(back, slots)
    to_before_ref[...] = msg[:128]
    to_after_ref[...] = msg[128:256]
    to_cells_ref[...] = msg[256:]
    ej_ref[...] = ej
    h_ref[...] = h
    tb_ref[...] = tbar


def k_direct(
    center_ref, partner_ref, scal_ref, av_ref, nav_ref, ei_ref, ej_ref, lat_ref, tan_ref, h_ref, tb_ref, wm_ref, wo_ref, part_ref, energy_ref
):
    scal = scal_ref[...]
    unit, cut, slope = scal[0:3], scal[5:6], scal[6:7]
    at_center = center_ref[...]
    at_partner = partner_ref[...]
    ei, ej = ei_ref[...], ej_ref[...]
    a, v = av_ref[:CHAN], av_ref[CHAN:]
    na, nv = nav_ref[:CHAN], nav_ref[CHAN:]
    tbar = tb_ref[...]
    cbar = tbar * v
    h = h_ref[...]
    gate = jax.nn.sigmoid(h)
    out = wo_ref[...]
    score = jnp.sum(out * (lat_ref[...] + h * gate), axis=0, keepdims=True)
    energy_ref[...] = put(jnp.concatenate([cut * score, jnp.zeros((7, PAIRS), F32)], axis=0), at_center)[0:4]
    ubar = cut * out
    hbar = ubar * (gate * (1.0 + h * (1.0 - gate)))
    lbar = ubar + weighted_t(wm_ref[0:128], hbar)
    coupling = 0.0
    to_center, to_partner, along = [], [], []
    for k in range(3):
        rows = slice(k * CHAN, (k + 1) * CHAN)
        mixed = unit[k : k + 1] + ej[rows]
        coupling = coupling + ei[rows] * mixed
        to_center.append(cbar * mixed)
        to_partner.append(cbar * ei[rows])
        along.append(jnp.sum(to_partner[k], axis=0, keepdims=True))
    vbar = tbar * coupling
    rbar = slope * score + jnp.sum(lbar * tan_ref[...], axis=0, keepdims=True) + jnp.sum(vbar * nv, axis=0, keepdims=True)
    grad = put(jnp.concatenate(to_center, axis=0), at_center) + put(jnp.concatenate(to_partner, axis=0), at_partner)
    gi = pick(grad, at_center)
    for k in range(3):
        rows = slice(k * CHAN, (k + 1) * CHAN)
        along[k] = along[k] + jnp.sum(a * gi[rows], axis=0, keepdims=True)
        rbar = rbar + unit[k : k + 1] * jnp.sum(na * gi[rows], axis=0, keepdims=True)
    part_ref[...] = jnp.concatenate(along + [rbar, jnp.zeros((4, PAIRS), F32)], axis=0)


def k_env_back(
    slots_ref,
    named_ref,
    scal_ref,
    av_ref,
    nav_ref,
    part_ref,
    back_ref,
    to_before_ref,
    to_after_ref,
    to_cells_ref,
    dbar_ref,
):
    scal = scal_ref[...]
    unit, inv = scal[0:3], scal[4:5]
    part = part_ref[...]
    named = named_ref[...]
    high, low = split2(back_ref[...])
    gi = dot(high, named, 0, 0) + dot(low, named, 0, 0)
    a, na = av_ref[:CHAN], nav_ref[:CHAN]
    along = []
    rbar = part[3:4]
    for k in range(3):
        rows = slice(k * CHAN, (k + 1) * CHAN)
        along.append(part[k : k + 1] + jnp.sum(a * gi[rows], axis=0, keepdims=True))
        rbar = rbar + unit[k : k + 1] * jnp.sum(na * gi[rows], axis=0, keepdims=True)
    for k in range(3):
        rbar = rbar - inv * along[k] * unit[k : k + 1]
    dbar = jnp.concatenate([along[k] * inv + rbar * unit[k : k + 1] for k in range(3)] + [jnp.zeros((5, PAIRS), F32)], axis=0)
    slots = slots_ref[...]
    msg = jnp.concatenate([put_rows(dbar, slots), jnp.zeros((512, 120), F32)], axis=1)
    to_before_ref[...] = msg[:128]
    to_after_ref[...] = msg[128:256]
    to_cells_ref[...] = msg[256:]
    dbar_ref[...] = dbar


def k_own_force(center_ref, partner_ref, dbar_ref, out_ref):
    dbar = dbar_ref[...]
    out_ref[...] = put(dbar, partner_ref[...]) - put(dbar, center_ref[...])


def k_force(own_ref, back_ref, column_ref, energy_ref, out_ref):
    named = jnp.where(
        column_ref[:, 0:1].astype(jnp.int32) == lax.broadcasted_iota(jnp.int32, (LIST, ATOMS), 1), 1.0, 0.0
    ).astype(BF16)
    returned = pick(back_ref[...].T[0:8], named, 3)
    total = -(own_ref[0:3] + returned[0:3])
    energy = energy_ref[...]
    for k in range(3):
        for i in range(4):
            out_ref[4 * k + i : 4 * k + i + 1] = total[k : k + 1, 128 * i : 128 * i + 128]
    for i in range(4):
        out_ref[12 + i : 13 + i] = energy[0:1, 128 * i : 128 * i + 128]


def k_unpack(in_ref, force_ref, energy_ref):
    for k in range(3):
        for i in range(4):
            force_ref[k, 0, 0, 0:1, 128 * i : 128 * i + 128] = in_ref[4 * k + i : 4 * k + i + 1]
    for i in range(4):
        energy_ref[0, 0, 0:1, 128 * i : 128 * i + 128] = in_ref[12 + i : 13 + i]


def call(kernel, outs, *args):
    shapes = [jax.ShapeDtypeStruct(s[:2], BF16) if s[2:] == (BF16,) else jax.ShapeDtypeStruct(s, F32) for s in outs]
    spec = pl.BlockSpec(memory_space=pltpu.VMEM)
    return pl.pallas_call(
        kernel,
        out_shape=shapes,
        in_specs=[spec] * len(args),
        out_specs=[spec] * len(outs),
        compiler_params=pltpu.CompilerParams(vmem_limit_bytes=24 * 1024 * 1024),
        name=kernel.__name__,
    )(*args)


def shards(
    positions,
    species,
    send_lists,
    pair_center,
    pair_partner,
    pair_slot_live,
    w_basis,
    emb_center,
    emb_partner,
    w_env,
    w_value,
    w_mix,
    w_out,
):
    packed = pack(positions, species, send_lists, pair_center, pair_partner, pair_slot_live)
    here = spots()
    zeros = jnp.zeros((2, 128), F32)
    wb = jnp.concatenate([w_basis, emb_center, zeros, emb_partner, zeros], axis=0)
    wav = jnp.concatenate([w_env, w_value], axis=1)
    wo = w_out.reshape(128, 1)

    packed = send(packed, MOVE_IN)
    low, high, column = call(k_lists, [(32, 128), (32, 128), (LIST, 8)], packed)
    hot = (ATOMS, PAIRS, BF16)
    part, center, partner, slots, named = call(
        k_own_pairs, [(8, PAIRS), hot, hot, hot, (LIST, PAIRS, BF16)], packed, column
    )
    low, high = low.reshape(1, 2, 2, 8, 128), high.reshape(1, 2, 2, 8, 128)
    ghosts = [g.reshape(-1, 128) for g in spread(low, high, here)]
    low, high, scal, pre, av = call(
        k_features,
        [(32, 192), (32, 192), (8, PAIRS), (128, PAIRS), (128, PAIRS)],
        packed,
        part,
        slots,
        named,
        *ghosts,
        wb,
        wav,
    )
    ei, ej, latent, hid, tangent, nav = call(
        k_own_env,
        [(192, PAIRS), (192, PAIRS)] + [(128, PAIRS)] * 4,
        center,
        partner,
        scal,
        pre,
        av,
        wb,
        wav,
        w_mix,
    )
    low, high = low.reshape(1, 2, 2, 8, 192), high.reshape(1, 2, 2, 8, 192)
    ghosts = [g.reshape(-1, 192) for g in spread(low, high, here)]
    before, after, cells, ej, h, tbar = call(
        k_energy,
        [(128, 192), (128, 192), (256, 192), (192, PAIRS), (128, PAIRS), (CHAN, PAIRS)],
        slots,
        scal,
        av,
        *ghosts,
        ei,
        ej,
        hid,
        w_mix,
        wo,
    )
    part, energy = call(
        k_direct,
        [(8, PAIRS), (4, ATOMS)],
        center,
        partner,
        scal,
        av,
        nav,
        ei,
        ej,
        latent,
        tangent,
        h,
        tbar,
        w_mix,
        wo,
    )
    before, after = before.reshape(4, 4, 8, 192), after.reshape(4, 4, 8, 192)
    back = collect(before, after, cells.reshape(4, 4, 2, 8, 192), here).reshape(LIST, 192)
    before, after, cells, dbar = call(
        k_env_back, [(128, 128), (128, 128), (256, 128), (8, PAIRS)], slots, named, scal, av, nav, part, back
    )
    (own,) = call(k_own_force, [(8, ATOMS)], center, partner, dbar)
    before, after = before.reshape(4, 4, 8, 128), after.reshape(4, 4, 8, 128)
    back = collect(before, after, cells.reshape(4, 4, 2, 8, 128), here).reshape(LIST, 128)
    (out,) = call(k_force, [(16, 128)], own, back, column, energy)
    out = send(out, MOVE_OUT)
    return call(k_unpack, [(3, 1, 1, 1, ATOMS), (1, 1, 1, ATOMS)], out)


def solution(mesh):
    in_specs = (
        P(None, "gx", "gy", "gz", None),
        P("gx", "gy", "gz", None),
        P("gx", "gy", "gz", None),
        P("gx", "gy", "gz", None, None),
        P("gx", "gy", "gz", None, None),
        P("gx", "gy", "gz", None, None),
        P(),
        P(),
        P(),
        P(),
        P(),
        P(),
        P(),
    )
    out_specs = (P(None, "gx", "gy", "gz", None), P("gx", "gy", "gz", None))
    return jax.shard_map(shards, mesh=mesh, in_specs=in_specs, out_specs=out_specs, check_vma=False)
```

```python
import math

import jax
import jax.numpy as jnp

from jax import lax
from jax.experimental import pallas as pl
from jax.experimental.pallas import tpu as pltpu
from jax.sharding import PartitionSpec as P

AXES = ("gx", "gy", "gz")
SHAPE = (16, 4, 8)
ATOMS = 512
PAIRS = 1024
LIST = 64
CHAN = 64
STEP = math.pi / 12.0
F32 = jnp.float32
BF16 = jnp.bfloat16


def flat(x, y, z):
    return (x * SHAPE[1] + y) * SHAPE[2] + z


def device(chip_x, chip_y, chip_z, core):
    return flat((chip_z % 8) * 2 + core, chip_y, (chip_z // 8) * 4 + chip_x)


def home(x, y, z):
    x, y, z = x % SHAPE[0], y % SHAPE[1], z % SHAPE[2]
    return device(z // 2, y, x, z % 2)


CELLS = [(x, y, z) for x in range(SHAPE[0]) for y in range(SHAPE[1]) for z in range(SHAPE[2])]
CHIPS = [(x, y, z, c) for x in range(4) for y in range(4) for z in range(16) for c in range(2)]
MOVE_IN = [(flat(*c), home(*c)) for c in CELLS]
MOVE_OUT = [(b, a) for a, b in MOVE_IN]
UP = [(home(x, y, z), home(x, y, z + 1)) for x, y, z in CELLS]
DOWN = [(b, a) for a, b in UP]


def along(spot, axis, position, core):
    spot = list(spot)
    spot[axis], spot[3] = position, core
    return device(*spot)


def snake(axis, count):
    pairs = []
    for spot in CHIPS:
        at, core = spot[axis], spot[3]
        then = at + 1 - 2 * core
        goal = along(spot, axis, then, core) if 0 <= then < count else along(spot, axis, at, 1 - core)
        pairs.append((device(*spot), goal))
    return pairs


def ends(axis, count):
    return [(device(*s), along(s, axis, count - 1 - s[axis], s[3])) for s in CHIPS if s[axis] in (0, count - 1)]


RINGS = {0: (2, 16), 1: (1, 4)}
FORTH = {a: snake(*r) for a, r in RINGS.items()}
BACK = {a: [(j, i) for i, j in p] for a, p in FORTH.items()}
ENDS = {a: ends(*r) for a, r in RINGS.items()}


def send(x, pairs):
    return lax.ppermute(x, AXES, pairs)


def spots():
    gx, gy, gz = (lax.axis_index(a) for a in AXES)
    return {0: (gz // 4) * 8 + gx // 2, 1: gy, 2: gx % 2}


def swap(axis, first, last, here):
    at, upward, count = here[axis], here[2] == 0, RINGS[axis][1]
    forth = send(jnp.where(upward, last, first), FORTH[axis])
    ring = send(jnp.where(at == 0, first, last), ENDS[axis])
    back = send(jnp.where(upward, first, last), BACK[axis])
    start, end = at == 0, at == count - 1
    before = jnp.where(~start, jnp.where(upward, forth, back), jnp.where(start, ring, back))
    after = jnp.where(end, jnp.where(end, ring, back), jnp.where(~upward, forth, back))
    return before, after


def spread(low, high, here):
    before, after = swap(0, low, high, here)
    cells = jnp.concatenate([before, low, high, after], axis=0)
    before, after = swap(1, cells[:, 0:1], cells[:, 1:2], here)
    cells = jnp.concatenate([before, cells, after], axis=1)
    before = send(cells[:, :, 1], UP)
    after = send(cells[:, :, 0], DOWN)
    return before, after, cells


def collect(before, after, cells, here):
    first = send(after, UP)
    last = send(before, DOWN)
    cells = cells + jnp.stack([first, last], axis=2)
    for axis in (1, 0):
        first = lax.slice_in_dim(cells, 0, 1, axis=axis)
        last = lax.slice_in_dim(cells, 3, 4, axis=axis)
        from_before, from_after = swap(axis, first, last, here)
        cells = lax.slice_in_dim(cells, 1, 3, axis=axis) + jnp.concatenate([from_before, from_after], axis=axis)
    return cells


def split2(x):
    high = x.astype(BF16)
    low = (x - high.astype(F32)).astype(BF16)
    return high, low


def split3(x):
    high = x.astype(BF16)
    rest = x - high.astype(F32)
    mid = rest.astype(BF16)
    return high, mid, (rest - mid.astype(F32)).astype(BF16)


def dot(a, b, ca, cb):
    return lax.dot_general(a, b, (((ca,), (cb,)), ((), ())), preferred_element_type=F32)


def weighted(w, x):
    wh, wl = split2(w)
    xh, xl = split2(x)
    return dot(wh, xh, 0, 0) + (dot(wl, xh, 0, 0) + dot(wh, xl, 0, 0))


def weighted_t(w, x):
    wh, wl = split2(w)
    xh, xl = split2(x)
    return dot(wh, xh, 1, 0) + (dot(wl, xh, 1, 0) + dot(wh, xl, 1, 0))


def pick(table, onehot, parts=2):
    rows = table.shape[0]
    pieces = split3(table) if parts == 3 else split2(table)
    full = dot(jnp.concatenate(pieces, axis=0), onehot, 1, 0)
    out = full[:rows]
    for i in range(1, parts):
        out = out + full[rows * i : rows * (i + 1)]
    return out


def put(values, onehot, parts=2):
    rows = values.shape[0]
    pieces = split3(values) if parts == 3 else split2(values)
    full = dot(jnp.concatenate(pieces, axis=0), onehot, 1, 1)
    out = full[:rows]
    for i in range(1, parts):
        out = out + full[rows * i : rows * (i + 1)]
    return out


def put_rows(values, onehot):
    high, low = split2(values)
    return dot(onehot, high, 1, 1) + dot(onehot, low, 1, 1)


def lanes(block):
    return jnp.concatenate([block[i : i + 1] for i in range(block.shape[0])], axis=1)


def match(index, count):
    ids = lax.broadcasted_iota(jnp.int32, (count, index.shape[1]), 0)
    return jnp.where(ids == index, 1.0, 0.0).astype(BF16)


def centers_of(packed):
    return lanes(packed[16:24]).astype(jnp.int32)


def partners_of(packed):
    return lanes(packed[24:32]).astype(jnp.int32)


def live_of(packed):
    return lanes(packed[32:40])


def own_table(packed):
    return jnp.concatenate([lanes(packed[4 * k : 4 * k + 4]) for k in range(4)], axis=0)


def ghost_cell(partners):
    rows = partners - ATOMS
    cell = rows >> 3
    skip = jnp.zeros_like(cell)
    for start in (21, 23, 33, 35):
        skip = skip + jnp.where(cell >= start, 2, 0)
    full = cell + skip
    return full >> 4, (full >> 2) & 3, full & 3, rows & 7


def ghost_slot(partners):
    p, q, r, atom = ghost_cell(partners)
    column = p * 4 + q
    slot = jnp.where(r == 0, column * 8, jnp.where(r == 3, column * 8 + 128, 256 + (column * 2 + r - 1) * 8)) + atom
    return jnp.where(partners >= ATOMS, slot, -1)


def k_pack(pos_in, kind_in, names_in, center_in, partner_in, live_in, out_ref, pos_ref, kind_ref, names_ref, center_ref, partner_ref, live_ref, sems):
    moves = [
        pltpu.make_async_copy(source, target, sems.at[i])
        for i, (source, target) in enumerate(
            [
                (pos_in, pos_ref),
                (kind_in, kind_ref),
                (names_in, names_ref),
                (center_in, center_ref),
                (partner_in, partner_ref),
                (live_in, live_ref),
            ]
        )
    ]
    for move in moves:
        move.start()
    out_ref[40:48] = jnp.zeros((8, 128), F32)
    for move in moves:
        move.wait()
    for k in range(3):
        for i in range(4):
            out_ref[4 * k + i : 4 * k + i + 1] = pos_ref[k, 0, 0, 0:1, 128 * i : 128 * i + 128]
    for i in range(4):
        out_ref[12 + i : 13 + i] = kind_ref[0, 0, 0:1, 128 * i : 128 * i + 128].astype(F32)
    out_ref[16:24] = center_ref[0, 0, 0].astype(F32)
    out_ref[24:32] = partner_ref[0, 0, 0].astype(F32)
    out_ref[32:40] = live_ref[0, 0, 0].astype(F32)
    names = [names_ref[i, j, k : k + 1] for i in range(2) for j in range(2) for k in range(2)]
    names.append(jnp.full((1, 64), -1, jnp.int32))
    out_ref[40:41] = jnp.concatenate(names, axis=1).astype(F32)


def pack(*args):
    return pl.pallas_call(
        k_pack,
        out_shape=jax.ShapeDtypeStruct((48, 128), F32),
        in_specs=[pl.BlockSpec(memory_space=pltpu.MemorySpace.HBM)] * len(args),
        out_specs=pl.BlockSpec(memory_space=pltpu.VMEM),
        scratch_shapes=[pltpu.VMEM(a.shape, a.dtype) for a in args] + [pltpu.SemaphoreType.DMA((len(args),))],
        compiler_params=pltpu.CompilerParams(vmem_limit_bytes=60 * 1024 * 1024),
        name="k_pack",
    )(*args)


def k_lists(packed_ref, low_ref, high_ref, column_ref):
    packed = packed_ref[...]
    names = packed[40:41].astype(jnp.int32)
    found = pick(own_table(packed), match(names, ATOMS), 3)
    wide = jnp.concatenate([found, jnp.zeros((124, 128), F32)], axis=0).T
    low_ref[...] = wide[:32]
    high_ref[...] = wide[32:64]
    column_ref[...] = jnp.broadcast_to(packed[40:41], (8, 128)).T[:LIST]


def k_own_pairs(packed_ref, out_ref):
    packed = packed_ref[...]
    table = own_table(packed)
    at_center = pick(table, match(centers_of(packed), ATOMS), 3)
    at_partner = pick(table, match(partners_of(packed), ATOMS), 3)
    out_ref[0:3] = at_partner[0:3] - at_center[0:3]
    out_ref[3:4] = at_partner[3:4]
    out_ref[4:5] = at_center[3:4]
    out_ref[5:8] = jnp.zeros((3, PAIRS), F32)


def k_features(
    packed_ref, part_ref, before_ref, after_ref, cells_ref, column_ref, wb_ref, wav_ref, low_ref, high_ref, scal_ref, pre_ref, av_ref
):
    packed = packed_ref[...]
    part = part_ref[...]
    ghost = jnp.concatenate([before_ref[...], after_ref[...], cells_ref[...]], axis=0).T[0:8]
    partners = partners_of(packed)
    slots = match(ghost_slot(partners), 512)
    pieces = split3(ghost)
    far = dot(jnp.concatenate(pieces, axis=0), slots, 1, 0)
    far = far[0:8] + (far[8:16] + far[16:24])
    moved = [jnp.where(c == 0, -6.0, jnp.where(c == 3, 6.0, 0.0)) for c in ghost_cell(partners)[:3]]
    moved = jnp.where(partners >= ATOMS, jnp.concatenate(moved, axis=0), 0.0)
    disp = part[0:3] + (far[0:3] + moved)
    partner_kind = part[3:4] + far[3:4]
    center_kind = part[4:5]
    radius = jnp.sqrt(jnp.sum(disp * disp, axis=0, keepdims=True) + 0.25)
    inv = 1.0 / radius
    unit = disp * inv
    scaled = radius * 0.2
    base = 1.0 + scaled * scaled
    live = live_of(packed)
    cut = live / (base * base)
    orders = lax.broadcasted_iota(jnp.int32, (8, 1), 0).astype(F32) + 1.0
    angle = radius * orders * STEP
    basis = jnp.sin(angle) * inv
    kinds = lax.broadcasted_iota(jnp.int32, (8, 1), 0).astype(F32)
    first = jnp.where(center_kind == kinds, 1.0, 0.0)
    second = jnp.where(partner_kind == kinds, 1.0, 0.0)
    pre = weighted(wb_ref[...], jnp.concatenate([basis, first, second], axis=0))
    latent = cut * (pre * jax.nn.sigmoid(pre))
    av = weighted(wav_ref[...], latent)
    a = av[:CHAN]
    terms = jnp.concatenate([unit[k : k + 1] * a for k in range(3)], axis=0)
    named = jnp.where(column_ref[:, 0:1].astype(jnp.int32) == centers_of(packed), 1.0, 0.0).astype(BF16)
    msg = put_rows(terms, named)
    low_ref[...] = msg[:32]
    high_ref[...] = msg[32:]
    scal_ref[0:3] = unit
    scal_ref[3:4] = radius
    scal_ref[4:5] = inv
    scal_ref[5:6] = cut
    scal_ref[6:7] = live * (-0.8) * scaled / (base * base * base)
    scal_ref[7:8] = live
    pre_ref[...] = pre
    av_ref[...] = av


def k_own_env(packed_ref, scal_ref, pre_ref, av_ref, wb_ref, wav_ref, wm_ref, ei_ref, ej_ref, lat_ref, hid_ref, tan_ref, nav_ref):
    packed = packed_ref[...]
    scal = scal_ref[...]
    unit, radius, inv, cut, slope = scal[0:3], scal[3:4], scal[4:5], scal[5:6], scal[6:7]
    av = av_ref[...]
    a = av[:CHAN]
    terms = jnp.concatenate([unit[k : k + 1] * a for k in range(3)], axis=0)
    at_center = match(centers_of(packed), ATOMS)
    env = put(terms, at_center)
    ei_ref[...] = pick(env, at_center)
    ej_ref[...] = pick(env, match(partners_of(packed), ATOMS))
    pre = pre_ref[...]
    gate = jax.nn.sigmoid(pre)
    act = pre * gate
    latent = cut * act
    lat_ref[...] = latent
    hid_ref[...] = weighted(wm_ref[0:128], latent)
    orders = lax.broadcasted_iota(jnp.int32, (8, 1), 0).astype(F32) + 1.0
    angle = radius * orders * STEP
    change = (jnp.cos(angle) * (orders * STEP) - jnp.sin(angle) * inv) * inv
    tangent = slope * act + cut * (gate * (1.0 + pre * (1.0 - gate))) * weighted(wb_ref[0:8], change)
    tan_ref[...] = tangent
    nav_ref[...] = weighted(wav_ref[...], tangent)


def k_energy(
    packed_ref,
    scal_ref,
    av_ref,
    before_ref,
    after_ref,
    cells_ref,
    ei_ref,
    ejown_ref,
    hid_ref,
    wm_ref,
    wo_ref,
    to_before_ref,
    to_after_ref,
    to_cells_ref,
    ej_ref,
    h_ref,
    tb_ref,
):
    packed = packed_ref[...]
    scal = scal_ref[...]
    unit, cut = scal[0:3], scal[5:6]
    slots = match(ghost_slot(partners_of(packed)), 512)
    high, low = split2(jnp.concatenate([before_ref[...], after_ref[...], cells_ref[...]], axis=0))
    ej = ejown_ref[...] + (dot(high, slots, 0, 0) + dot(low, slots, 0, 0))
    ei = ei_ref[...]
    coupling = 0.0
    for k in range(3):
        rows = slice(k * CHAN, (k + 1) * CHAN)
        coupling = coupling + ei[rows] * (unit[k : k + 1] + ej[rows])
    v = av_ref[CHAN:]
    mix = wm_ref[128:]
    h = hid_ref[...] + weighted(mix, v * coupling)
    gate = jax.nn.sigmoid(h)
    out = wo_ref[...]
    hbar = (cut * out) * (gate * (1.0 + h * (1.0 - gate)))
    tbar = weighted_t(mix, hbar)
    cbar = tbar * v
    back = jnp.concatenate([cbar * ei[k * CHAN : (k + 1) * CHAN] for k in range(3)], axis=0)
    msg = put_rows(back, slots)
    to_before_ref[...] = msg[:128]
    to_after_ref[...] = msg[128:256]
    to_cells_ref[...] = msg[256:]
    ej_ref[...] = ej
    h_ref[...] = h
    tb_ref[...] = tbar


def k_direct(
    packed_ref, scal_ref, av_ref, nav_ref, ei_ref, ej_ref, lat_ref, tan_ref, h_ref, tb_ref, wm_ref, wo_ref, part_ref, energy_ref
):
    packed = packed_ref[...]
    scal = scal_ref[...]
    unit, cut, slope = scal[0:3], scal[5:6], scal[6:7]
    at_center = match(centers_of(packed), ATOMS)
    at_partner = match(partners_of(packed), ATOMS)
    ei, ej = ei_ref[...], ej_ref[...]
    a, v = av_ref[:CHAN], av_ref[CHAN:]
    na, nv = nav_ref[:CHAN], nav_ref[CHAN:]
    tbar = tb_ref[...]
    cbar = tbar * v
    h = h_ref[...]
    gate = jax.nn.sigmoid(h)
    out = wo_ref[...]
    score = jnp.sum(out * (lat_ref[...] + h * gate), axis=0, keepdims=True)
    energy_ref[...] = put(jnp.concatenate([cut * score, jnp.zeros((7, PAIRS), F32)], axis=0), at_center)[0:4]
    ubar = cut * out
    hbar = ubar * (gate * (1.0 + h * (1.0 - gate)))
    lbar = ubar + weighted_t(wm_ref[0:128], hbar)
    coupling = 0.0
    to_center, to_partner, along = [], [], []
    for k in range(3):
        rows = slice(k * CHAN, (k + 1) * CHAN)
        mixed = unit[k : k + 1] + ej[rows]
        coupling = coupling + ei[rows] * mixed
        to_center.append(cbar * mixed)
        to_partner.append(cbar * ei[rows])
        along.append(jnp.sum(to_partner[k], axis=0, keepdims=True))
    vbar = tbar * coupling
    rbar = slope * score + jnp.sum(lbar * tan_ref[...], axis=0, keepdims=True) + jnp.sum(vbar * nv, axis=0, keepdims=True)
    grad = put(jnp.concatenate(to_center, axis=0), at_center) + put(jnp.concatenate(to_partner, axis=0), at_partner)
    gi = pick(grad, at_center)
    for k in range(3):
        rows = slice(k * CHAN, (k + 1) * CHAN)
        along[k] = along[k] + jnp.sum(a * gi[rows], axis=0, keepdims=True)
        rbar = rbar + unit[k : k + 1] * jnp.sum(na * gi[rows], axis=0, keepdims=True)
    part_ref[...] = jnp.concatenate(along + [rbar, jnp.zeros((4, PAIRS), F32)], axis=0)


def k_env_back(
    packed_ref,
    scal_ref,
    av_ref,
    nav_ref,
    part_ref,
    back_ref,
    column_ref,
    to_before_ref,
    to_after_ref,
    to_cells_ref,
    dbar_ref,
):
    packed = packed_ref[...]
    scal = scal_ref[...]
    unit, inv = scal[0:3], scal[4:5]
    part = part_ref[...]
    named = jnp.where(column_ref[:, 0:1].astype(jnp.int32) == centers_of(packed), 1.0, 0.0).astype(BF16)
    high, low = split2(back_ref[...])
    gi = dot(high, named, 0, 0) + dot(low, named, 0, 0)
    a, na = av_ref[:CHAN], nav_ref[:CHAN]
    along = []
    rbar = part[3:4]
    for k in range(3):
        rows = slice(k * CHAN, (k + 1) * CHAN)
        along.append(part[k : k + 1] + jnp.sum(a * gi[rows], axis=0, keepdims=True))
        rbar = rbar + unit[k : k + 1] * jnp.sum(na * gi[rows], axis=0, keepdims=True)
    for k in range(3):
        rbar = rbar - inv * along[k] * unit[k : k + 1]
    dbar = jnp.concatenate([along[k] * inv + rbar * unit[k : k + 1] for k in range(3)] + [jnp.zeros((5, PAIRS), F32)], axis=0)
    slots = match(ghost_slot(partners_of(packed)), 512)
    msg = jnp.concatenate([put_rows(dbar, slots), jnp.zeros((512, 120), F32)], axis=1)
    to_before_ref[...] = msg[:128]
    to_after_ref[...] = msg[128:256]
    to_cells_ref[...] = msg[256:]
    dbar_ref[...] = dbar


def k_own_force(packed_ref, dbar_ref, out_ref):
    packed = packed_ref[...]
    dbar = dbar_ref[...]
    out_ref[...] = put(dbar, match(partners_of(packed), ATOMS)) - put(dbar, match(centers_of(packed), ATOMS))


def k_force(own_ref, back_ref, column_ref, energy_ref, out_ref):
    named = jnp.where(
        column_ref[:, 0:1].astype(jnp.int32) == lax.broadcasted_iota(jnp.int32, (LIST, ATOMS), 1), 1.0, 0.0
    ).astype(BF16)
    returned = pick(back_ref[...].T[0:8], named, 3)
    total = -(own_ref[0:3] + returned[0:3])
    energy = energy_ref[...]
    for k in range(3):
        for i in range(4):
            out_ref[4 * k + i : 4 * k + i + 1] = total[k : k + 1, 128 * i : 128 * i + 128]
    for i in range(4):
        out_ref[12 + i : 13 + i] = energy[0:1, 128 * i : 128 * i + 128]


def k_unpack(in_ref, force_ref, energy_ref):
    for k in range(3):
        for i in range(4):
            force_ref[k, 0, 0, 0:1, 128 * i : 128 * i + 128] = in_ref[4 * k + i : 4 * k + i + 1]
    for i in range(4):
        energy_ref[0, 0, 0:1, 128 * i : 128 * i + 128] = in_ref[12 + i : 13 + i]


def call(kernel, outs, *args):
    shapes = [jax.ShapeDtypeStruct(s, F32) for s in outs]
    spec = pl.BlockSpec(memory_space=pltpu.VMEM)
    return pl.pallas_call(
        kernel,
        out_shape=shapes,
        in_specs=[spec] * len(args),
        out_specs=[spec] * len(outs),
        compiler_params=pltpu.CompilerParams(vmem_limit_bytes=48 * 1024 * 1024),
        name=kernel.__name__,
    )(*args)


def shards(
    positions,
    species,
    send_lists,
    pair_center,
    pair_partner,
    pair_slot_live,
    w_basis,
    emb_center,
    emb_partner,
    w_env,
    w_value,
    w_mix,
    w_out,
):
    packed = pack(positions, species, send_lists, pair_center, pair_partner, pair_slot_live)
    here = spots()
    zeros = jnp.zeros((2, 128), F32)
    wb = jnp.concatenate([w_basis, emb_center, zeros, emb_partner, zeros], axis=0)
    wav = jnp.concatenate([w_env, w_value], axis=1)
    wo = w_out.reshape(128, 1)

    packed = send(packed, MOVE_IN)
    low, high, column = call(k_lists, [(32, 128), (32, 128), (LIST, 8)], packed)
    (part,) = call(k_own_pairs, [(8, PAIRS)], packed)
    low, high = low.reshape(1, 2, 2, 8, 128), high.reshape(1, 2, 2, 8, 128)
    ghosts = [g.reshape(-1, 128) for g in spread(low, high, here)]
    low, high, scal, pre, av = call(
        k_features,
        [(32, 192), (32, 192), (8, PAIRS), (128, PAIRS), (128, PAIRS)],
        packed,
        part,
        *ghosts,
        column,
        wb,
        wav,
    )
    ei, ej, latent, hid, tangent, nav = call(
        k_own_env,
        [(192, PAIRS), (192, PAIRS)] + [(128, PAIRS)] * 4,
        packed,
        scal,
        pre,
        av,
        wb,
        wav,
        w_mix,
    )
    low, high = low.reshape(1, 2, 2, 8, 192), high.reshape(1, 2, 2, 8, 192)
    ghosts = [g.reshape(-1, 192) for g in spread(low, high, here)]
    before, after, cells, ej, h, tbar = call(
        k_energy,
        [(128, 192), (128, 192), (256, 192), (192, PAIRS), (128, PAIRS), (CHAN, PAIRS)],
        packed,
        scal,
        av,
        *ghosts,
        ei,
        ej,
        hid,
        w_mix,
        wo,
    )
    part, energy = call(
        k_direct,
        [(8, PAIRS), (4, ATOMS)],
        packed,
        scal,
        av,
        nav,
        ei,
        ej,
        latent,
        tangent,
        h,
        tbar,
        w_mix,
        wo,
    )
    before, after = before.reshape(4, 4, 8, 192), after.reshape(4, 4, 8, 192)
    back = collect(before, after, cells.reshape(4, 4, 2, 8, 192), here).reshape(LIST, 192)
    before, after, cells, dbar = call(
        k_env_back, [(128, 128), (128, 128), (256, 128), (8, PAIRS)], packed, scal, av, nav, part, back, column
    )
    (own,) = call(k_own_force, [(8, ATOMS)], packed, dbar)
    before, after = before.reshape(4, 4, 8, 128), after.reshape(4, 4, 8, 128)
    back = collect(before, after, cells.reshape(4, 4, 2, 8, 128), here).reshape(LIST, 128)
    (out,) = call(k_force, [(16, 128)], own, back, column, energy)
    out = send(out, MOVE_OUT)
    return call(k_unpack, [(3, 1, 1, 1, ATOMS), (1, 1, 1, ATOMS)], out)


def solution(mesh):
    in_specs = (
        P(None, "gx", "gy", "gz", None),
        P("gx", "gy", "gz", None),
        P("gx", "gy", "gz", None),
        P("gx", "gy", "gz", None, None),
        P("gx", "gy", "gz", None, None),
        P("gx", "gy", "gz", None, None),
        P(),
        P(),
        P(),
        P(),
        P(),
        P(),
        P(),
    )
    out_specs = (P(None, "gx", "gy", "gz", None), P("gx", "gy", "gz", None))
    return jax.shard_map(shards, mesh=mesh, in_specs=in_specs, out_specs=out_specs, check_vma=False)
```

```python
import math

import jax
import jax.numpy as jnp

from jax import lax
from jax.experimental import pallas as pl
from jax.experimental.pallas import tpu as pltpu
from jax.sharding import PartitionSpec as P

AXES = ("gx", "gy", "gz")
SHAPE = (16, 4, 8)
ATOMS = 512
PAIRS = 1024
LIST = 64
CHAN = 64
STEP = math.pi / 12.0
F32 = jnp.float32
BF16 = jnp.bfloat16


def flat(x, y, z):
    return (x * SHAPE[1] + y) * SHAPE[2] + z


def device(chip_x, chip_y, chip_z, core):
    return flat((chip_z % 8) * 2 + core, chip_y, (chip_z // 8) * 4 + chip_x)


def home(x, y, z):
    x, y, z = x % SHAPE[0], y % SHAPE[1], z % SHAPE[2]
    return device(z // 2, y, x, z % 2)


CELLS = [(x, y, z) for x in range(SHAPE[0]) for y in range(SHAPE[1]) for z in range(SHAPE[2])]
CHIPS = [(x, y, z, c) for x in range(4) for y in range(4) for z in range(16) for c in range(2)]
MOVE_IN = [(flat(*c), home(*c)) for c in CELLS]
MOVE_OUT = [(b, a) for a, b in MOVE_IN]
UP = [(home(x, y, z), home(x, y, z + 1)) for x, y, z in CELLS]
DOWN = [(b, a) for a, b in UP]


def along(spot, axis, position, core):
    spot = list(spot)
    spot[axis], spot[3] = position, core
    return device(*spot)


def snake(axis, count):
    pairs = []
    for spot in CHIPS:
        at, core = spot[axis], spot[3]
        then = at + 1 - 2 * core
        goal = along(spot, axis, then, core) if 0 <= then < count else along(spot, axis, at, 1 - core)
        pairs.append((device(*spot), goal))
    return pairs


def ends(axis, count):
    return [(device(*s), along(s, axis, count - 1 - s[axis], s[3])) for s in CHIPS if s[axis] in (0, count - 1)]


RINGS = {0: (2, 16), 1: (1, 4)}
FORTH = {a: snake(*r) for a, r in RINGS.items()}
BACK = {a: [(j, i) for i, j in p] for a, p in FORTH.items()}
ENDS = {a: ends(*r) for a, r in RINGS.items()}


def send(x, pairs):
    return lax.ppermute(x, AXES, pairs)


def spots():
    gx, gy, gz = (lax.axis_index(a) for a in AXES)
    return {0: (gz // 4) * 8 + gx // 2, 1: gy, 2: gx % 2}


def swap(axis, first, last, here):
    at, upward, count = here[axis], here[2] == 0, RINGS[axis][1]
    forth = send(jnp.where(upward, last, first), FORTH[axis])
    ring = send(jnp.where(at == 0, first, last), ENDS[axis])
    back = send(jnp.where(upward, first, last), BACK[axis])
    start, end = at == 0, at == count - 1
    before = jnp.where(~start, jnp.where(upward, forth, back), jnp.where(start, ring, back))
    after = jnp.where(end, jnp.where(end, ring, back), jnp.where(~upward, forth, back))
    return before, after


def spread(low, high, here):
    before, after = swap(0, low, high, here)
    cells = jnp.concatenate([before, low, high, after], axis=0)
    before, after = swap(1, cells[:, 0:1], cells[:, 1:2], here)
    cells = jnp.concatenate([before, cells, after], axis=1)
    before = send(cells[:, :, 1], UP)
    after = send(cells[:, :, 0], DOWN)
    return before, after, cells


def collect(before, after, cells, here, beside):
    first = send(after, UP)
    last = send(before, DOWN)
    cells = cells + jnp.stack([first, last], axis=2)
    cells, beside = lax.optimization_barrier((cells, beside))
    for axis in (1, 0):
        first = lax.slice_in_dim(cells, 0, 1, axis=axis)
        last = lax.slice_in_dim(cells, 3, 4, axis=axis)
        from_before, from_after = swap(axis, first, last, here)
        cells = lax.slice_in_dim(cells, 1, 3, axis=axis) + jnp.concatenate([from_before, from_after], axis=axis)
    return cells, beside


def split2(x):
    high = x.astype(BF16)
    low = (x - high.astype(F32)).astype(BF16)
    return high, low


def split3(x):
    high = x.astype(BF16)
    rest = x - high.astype(F32)
    mid = rest.astype(BF16)
    return high, mid, (rest - mid.astype(F32)).astype(BF16)


def dot(a, b, ca, cb):
    return lax.dot_general(a, b, (((ca,), (cb,)), ((), ())), preferred_element_type=F32)


def weighted(w, x):
    wh, wl = split2(w)
    xh, xl = split2(x)
    return dot(wh, xh, 0, 0) + (dot(wl, xh, 0, 0) + dot(wh, xl, 0, 0))


def weighted_t(w, x):
    wh, wl = split2(w)
    xh, xl = split2(x)
    return dot(wh, xh, 1, 0) + (dot(wl, xh, 1, 0) + dot(wh, xl, 1, 0))


def pick(table, onehot, parts=2):
    rows = table.shape[0]
    pieces = split3(table) if parts == 3 else split2(table)
    full = dot(jnp.concatenate(pieces, axis=0), onehot, 1, 0)
    out = full[:rows]
    for i in range(1, parts):
        out = out + full[rows * i : rows * (i + 1)]
    return out


def put(values, onehot, parts=2):
    rows = values.shape[0]
    pieces = split3(values) if parts == 3 else split2(values)
    full = dot(jnp.concatenate(pieces, axis=0), onehot, 1, 1)
    out = full[:rows]
    for i in range(1, parts):
        out = out + full[rows * i : rows * (i + 1)]
    return out


def put_rows(values, onehot):
    high, low = split2(values)
    return dot(onehot, high, 1, 1) + dot(onehot, low, 1, 1)


def lanes(block):
    return jnp.concatenate([block[i : i + 1] for i in range(block.shape[0])], axis=1)


def match(index, count):
    ids = lax.broadcasted_iota(jnp.int32, (count, index.shape[1]), 0)
    return jnp.where(ids == index, 1.0, 0.0).astype(BF16)


def centers_of(packed):
    return lanes(packed[16:24]).astype(jnp.int32)


def partners_of(packed):
    return lanes(packed[24:32]).astype(jnp.int32)


def live_of(packed):
    return lanes(packed[32:40])


def own_table(packed):
    return jnp.concatenate([lanes(packed[4 * k : 4 * k + 4]) for k in range(4)], axis=0)


def ghost_cell(partners):
    rows = partners - ATOMS
    cell = rows >> 3
    skip = jnp.zeros_like(cell)
    for start in (21, 23, 33, 35):
        skip = skip + jnp.where(cell >= start, 2, 0)
    full = cell + skip
    return full >> 4, (full >> 2) & 3, full & 3, rows & 7


def ghost_slot(partners):
    p, q, r, atom = ghost_cell(partners)
    column = p * 4 + q
    slot = jnp.where(r == 0, column * 8, jnp.where(r == 3, column * 8 + 128, 256 + (column * 2 + r - 1) * 8)) + atom
    return jnp.where(partners >= ATOMS, slot, -1)


def k_pack(pos_in, kind_in, names_in, center_in, partner_in, live_in, out_ref, pos_ref, kind_ref, names_ref, center_ref, partner_ref, live_ref, sems):
    moves = [
        pltpu.make_async_copy(source, target, sems.at[i])
        for i, (source, target) in enumerate(
            [
                (pos_in, pos_ref),
                (kind_in, kind_ref),
                (names_in, names_ref),
                (center_in, center_ref),
                (partner_in, partner_ref),
                (live_in, live_ref),
            ]
        )
    ]
    for move in moves:
        move.start()
    out_ref[40:48] = jnp.zeros((8, 128), F32)
    for move in moves:
        move.wait()
    for k in range(3):
        for i in range(4):
            out_ref[4 * k + i : 4 * k + i + 1] = pos_ref[k, 0, 0, 0:1, 128 * i : 128 * i + 128]
    for i in range(4):
        out_ref[12 + i : 13 + i] = kind_ref[0, 0, 0:1, 128 * i : 128 * i + 128].astype(F32)
    out_ref[16:24] = center_ref[0, 0, 0].astype(F32)
    out_ref[24:32] = partner_ref[0, 0, 0].astype(F32)
    out_ref[32:40] = live_ref[0, 0, 0].astype(F32)
    names = [names_ref[i, j, k : k + 1] for i in range(2) for j in range(2) for k in range(2)]
    names.append(jnp.full((1, 64), -1, jnp.int32))
    out_ref[40:41] = jnp.concatenate(names, axis=1).astype(F32)


def pack(*args):
    return pl.pallas_call(
        k_pack,
        out_shape=jax.ShapeDtypeStruct((48, 128), F32),
        in_specs=[pl.BlockSpec(memory_space=pltpu.MemorySpace.HBM)] * len(args),
        out_specs=pl.BlockSpec(memory_space=pltpu.VMEM),
        scratch_shapes=[pltpu.VMEM(a.shape, a.dtype) for a in args] + [pltpu.SemaphoreType.DMA((len(args),))],
        compiler_params=pltpu.CompilerParams(vmem_limit_bytes=60 * 1024 * 1024),
        name="k_pack",
    )(*args)


def k_lists(packed_ref, low_ref, high_ref, column_ref):
    packed = packed_ref[...]
    names = packed[40:41].astype(jnp.int32)
    found = pick(own_table(packed), match(names, ATOMS), 3)
    wide = jnp.concatenate([found, jnp.zeros((124, 128), F32)], axis=0).T
    low_ref[...] = wide[:32]
    high_ref[...] = wide[32:64]
    column_ref[...] = jnp.broadcast_to(packed[40:41], (8, 128)).T[:LIST]


def k_own_pairs(packed_ref, out_ref):
    packed = packed_ref[...]
    table = own_table(packed)
    at_center = pick(table, match(centers_of(packed), ATOMS), 3)
    at_partner = pick(table, match(partners_of(packed), ATOMS), 3)
    out_ref[0:3] = at_partner[0:3] - at_center[0:3]
    out_ref[3:4] = at_partner[3:4]
    out_ref[4:5] = at_center[3:4]
    out_ref[5:8] = jnp.zeros((3, PAIRS), F32)


def k_features(
    packed_ref, part_ref, before_ref, after_ref, cells_ref, column_ref, wb_ref, wav_ref, low_ref, high_ref, scal_ref, pre_ref, av_ref
):
    packed = packed_ref[...]
    part = part_ref[...]
    ghost = jnp.concatenate([before_ref[...], after_ref[...], cells_ref[...]], axis=0).T[0:8]
    partners = partners_of(packed)
    slots = match(ghost_slot(partners), 512)
    pieces = split3(ghost)
    far = dot(jnp.concatenate(pieces, axis=0), slots, 1, 0)
    far = far[0:8] + (far[8:16] + far[16:24])
    moved = [jnp.where(c == 0, -6.0, jnp.where(c == 3, 6.0, 0.0)) for c in ghost_cell(partners)[:3]]
    moved = jnp.where(partners >= ATOMS, jnp.concatenate(moved, axis=0), 0.0)
    disp = part[0:3] + (far[0:3] + moved)
    partner_kind = part[3:4] + far[3:4]
    center_kind = part[4:5]
    radius = jnp.sqrt(jnp.sum(disp * disp, axis=0, keepdims=True) + 0.25)
    inv = 1.0 / radius
    unit = disp * inv
    scaled = radius * 0.2
    base = 1.0 + scaled * scaled
    live = live_of(packed)
    cut = live / (base * base)
    orders = lax.broadcasted_iota(jnp.int32, (8, 1), 0).astype(F32) + 1.0
    angle = radius * orders * STEP
    basis = jnp.sin(angle) * inv
    kinds = lax.broadcasted_iota(jnp.int32, (8, 1), 0).astype(F32)
    first = jnp.where(center_kind == kinds, 1.0, 0.0)
    second = jnp.where(partner_kind == kinds, 1.0, 0.0)
    pre = weighted(wb_ref[...], jnp.concatenate([basis, first, second], axis=0))
    latent = cut * (pre * jax.nn.sigmoid(pre))
    av = weighted(wav_ref[...], latent)
    a = av[:CHAN]
    terms = jnp.concatenate([unit[k : k + 1] * a for k in range(3)], axis=0)
    named = jnp.where(column_ref[:, 0:1].astype(jnp.int32) == centers_of(packed), 1.0, 0.0).astype(BF16)
    msg = put_rows(terms, named)
    low_ref[...] = msg[:32]
    high_ref[...] = msg[32:]
    scal_ref[0:3] = unit
    scal_ref[3:4] = radius
    scal_ref[4:5] = inv
    scal_ref[5:6] = cut
    scal_ref[6:7] = live * (-0.8) * scaled / (base * base * base)
    scal_ref[7:8] = live
    pre_ref[...] = pre
    av_ref[...] = av


def k_own_env(packed_ref, scal_ref, pre_ref, av_ref, wb_ref, wav_ref, wm_ref, ei_ref, ej_ref, lat_ref, hid_ref, tan_ref, nav_ref):
    packed = packed_ref[...]
    scal = scal_ref[...]
    unit, radius, inv, cut, slope = scal[0:3], scal[3:4], scal[4:5], scal[5:6], scal[6:7]
    av = av_ref[...]
    a = av[:CHAN]
    terms = jnp.concatenate([unit[k : k + 1] * a for k in range(3)], axis=0)
    at_center = match(centers_of(packed), ATOMS)
    env = put(terms, at_center)
    ei_ref[...] = pick(env, at_center)
    ej_ref[...] = pick(env, match(partners_of(packed), ATOMS))
    pre = pre_ref[...]
    gate = jax.nn.sigmoid(pre)
    act = pre * gate
    latent = cut * act
    lat_ref[...] = latent
    hid_ref[...] = weighted(wm_ref[0:128], latent)
    orders = lax.broadcasted_iota(jnp.int32, (8, 1), 0).astype(F32) + 1.0
    angle = radius * orders * STEP
    change = (jnp.cos(angle) * (orders * STEP) - jnp.sin(angle) * inv) * inv
    tangent = slope * act + cut * (gate * (1.0 + pre * (1.0 - gate))) * weighted(wb_ref[0:8], change)
    tan_ref[...] = tangent
    nav_ref[...] = weighted(wav_ref[...], tangent)


def k_energy(
    packed_ref,
    scal_ref,
    av_ref,
    before_ref,
    after_ref,
    cells_ref,
    ei_ref,
    ejown_ref,
    hid_ref,
    wm_ref,
    wo_ref,
    to_before_ref,
    to_after_ref,
    to_cells_ref,
    ej_ref,
    h_ref,
    tb_ref,
):
    packed = packed_ref[...]
    scal = scal_ref[...]
    unit, cut = scal[0:3], scal[5:6]
    slots = match(ghost_slot(partners_of(packed)), 512)
    high, low = split2(jnp.concatenate([before_ref[...], after_ref[...], cells_ref[...]], axis=0))
    ej = ejown_ref[...] + (dot(high, slots, 0, 0) + dot(low, slots, 0, 0))
    ei = ei_ref[...]
    coupling = 0.0
    for k in range(3):
        rows = slice(k * CHAN, (k + 1) * CHAN)
        coupling = coupling + ei[rows] * (unit[k : k + 1] + ej[rows])
    v = av_ref[CHAN:]
    mix = wm_ref[128:]
    h = hid_ref[...] + weighted(mix, v * coupling)
    gate = jax.nn.sigmoid(h)
    out = wo_ref[...]
    hbar = (cut * out) * (gate * (1.0 + h * (1.0 - gate)))
    tbar = weighted_t(mix, hbar)
    cbar = tbar * v
    back = jnp.concatenate([cbar * ei[k * CHAN : (k + 1) * CHAN] for k in range(3)], axis=0)
    msg = put_rows(back, slots)
    to_before_ref[...] = msg[:128]
    to_after_ref[...] = msg[128:256]
    to_cells_ref[...] = msg[256:]
    ej_ref[...] = ej
    h_ref[...] = h
    tb_ref[...] = tbar


def k_direct(
    packed_ref, scal_ref, av_ref, nav_ref, ei_ref, ej_ref, lat_ref, tan_ref, h_ref, tb_ref, wm_ref, wo_ref, part_ref, energy_ref
):
    packed = packed_ref[...]
    scal = scal_ref[...]
    unit, cut, slope = scal[0:3], scal[5:6], scal[6:7]
    at_center = match(centers_of(packed), ATOMS)
    at_partner = match(partners_of(packed), ATOMS)
    ei, ej = ei_ref[...], ej_ref[...]
    a, v = av_ref[:CHAN], av_ref[CHAN:]
    na, nv = nav_ref[:CHAN], nav_ref[CHAN:]
    tbar = tb_ref[...]
    cbar = tbar * v
    h = h_ref[...]
    gate = jax.nn.sigmoid(h)
    out = wo_ref[...]
    score = jnp.sum(out * (lat_ref[...] + h * gate), axis=0, keepdims=True)
    energy_ref[...] = put(jnp.concatenate([cut * score, jnp.zeros((7, PAIRS), F32)], axis=0), at_center)[0:4]
    ubar = cut * out
    hbar = ubar * (gate * (1.0 + h * (1.0 - gate)))
    lbar = ubar + weighted_t(wm_ref[0:128], hbar)
    coupling = 0.0
    to_center, to_partner, along = [], [], []
    for k in range(3):
        rows = slice(k * CHAN, (k + 1) * CHAN)
        mixed = unit[k : k + 1] + ej[rows]
        coupling = coupling + ei[rows] * mixed
        to_center.append(cbar * mixed)
        to_partner.append(cbar * ei[rows])
        along.append(jnp.sum(to_partner[k], axis=0, keepdims=True))
    vbar = tbar * coupling
    rbar = slope * score + jnp.sum(lbar * tan_ref[...], axis=0, keepdims=True) + jnp.sum(vbar * nv, axis=0, keepdims=True)
    grad = put(jnp.concatenate(to_center, axis=0), at_center) + put(jnp.concatenate(to_partner, axis=0), at_partner)
    gi = pick(grad, at_center)
    for k in range(3):
        rows = slice(k * CHAN, (k + 1) * CHAN)
        along[k] = along[k] + jnp.sum(a * gi[rows], axis=0, keepdims=True)
        rbar = rbar + unit[k : k + 1] * jnp.sum(na * gi[rows], axis=0, keepdims=True)
    part_ref[...] = jnp.concatenate(along + [rbar, jnp.zeros((4, PAIRS), F32)], axis=0)


def k_env_back(
    packed_ref,
    scal_ref,
    av_ref,
    nav_ref,
    part_ref,
    back_ref,
    column_ref,
    to_before_ref,
    to_after_ref,
    to_cells_ref,
    dbar_ref,
):
    packed = packed_ref[...]
    scal = scal_ref[...]
    unit, inv = scal[0:3], scal[4:5]
    part = part_ref[...]
    named = jnp.where(column_ref[:, 0:1].astype(jnp.int32) == centers_of(packed), 1.0, 0.0).astype(BF16)
    high, low = split2(back_ref[...])
    gi = dot(high, named, 0, 0) + dot(low, named, 0, 0)
    a, na = av_ref[:CHAN], nav_ref[:CHAN]
    along = []
    rbar = part[3:4]
    for k in range(3):
        rows = slice(k * CHAN, (k + 1) * CHAN)
        along.append(part[k : k + 1] + jnp.sum(a * gi[rows], axis=0, keepdims=True))
        rbar = rbar + unit[k : k + 1] * jnp.sum(na * gi[rows], axis=0, keepdims=True)
    for k in range(3):
        rbar = rbar - inv * along[k] * unit[k : k + 1]
    dbar = jnp.concatenate([along[k] * inv + rbar * unit[k : k + 1] for k in range(3)] + [jnp.zeros((5, PAIRS), F32)], axis=0)
    slots = match(ghost_slot(partners_of(packed)), 512)
    msg = jnp.concatenate([put_rows(dbar, slots), jnp.zeros((512, 120), F32)], axis=1)
    to_before_ref[...] = msg[:128]
    to_after_ref[...] = msg[128:256]
    to_cells_ref[...] = msg[256:]
    dbar_ref[...] = dbar


def k_own_force(packed_ref, dbar_ref, out_ref):
    packed = packed_ref[...]
    dbar = dbar_ref[...]
    out_ref[...] = put(dbar, match(partners_of(packed), ATOMS)) - put(dbar, match(centers_of(packed), ATOMS))


def k_force(own_ref, back_ref, column_ref, energy_ref, out_ref):
    named = jnp.where(
        column_ref[:, 0:1].astype(jnp.int32) == lax.broadcasted_iota(jnp.int32, (LIST, ATOMS), 1), 1.0, 0.0
    ).astype(BF16)
    returned = pick(back_ref[...].T[0:8], named, 3)
    total = -(own_ref[0:3] + returned[0:3])
    energy = energy_ref[...]
    for k in range(3):
        for i in range(4):
            out_ref[4 * k + i : 4 * k + i + 1] = total[k : k + 1, 128 * i : 128 * i + 128]
    for i in range(4):
        out_ref[12 + i : 13 + i] = energy[0:1, 128 * i : 128 * i + 128]


def k_unpack(in_ref, force_ref, energy_ref):
    for k in range(3):
        for i in range(4):
            force_ref[k, 0, 0, 0:1, 128 * i : 128 * i + 128] = in_ref[4 * k + i : 4 * k + i + 1]
    for i in range(4):
        energy_ref[0, 0, 0:1, 128 * i : 128 * i + 128] = in_ref[12 + i : 13 + i]


def call(kernel, outs, *args):
    shapes = [jax.ShapeDtypeStruct(s, F32) for s in outs]
    spec = pl.BlockSpec(memory_space=pltpu.VMEM)
    return pl.pallas_call(
        kernel,
        out_shape=shapes,
        in_specs=[spec] * len(args),
        out_specs=[spec] * len(outs),
        compiler_params=pltpu.CompilerParams(vmem_limit_bytes=48 * 1024 * 1024),
        name=kernel.__name__,
    )(*args)


def shards(
    positions,
    species,
    send_lists,
    pair_center,
    pair_partner,
    pair_slot_live,
    w_basis,
    emb_center,
    emb_partner,
    w_env,
    w_value,
    w_mix,
    w_out,
):
    packed = pack(positions, species, send_lists, pair_center, pair_partner, pair_slot_live)
    here = spots()
    zeros = jnp.zeros((2, 128), F32)
    wb = jnp.concatenate([w_basis, emb_center, zeros, emb_partner, zeros], axis=0)
    wav = jnp.concatenate([w_env, w_value], axis=1)
    wo = w_out.reshape(128, 1)

    packed = send(packed, MOVE_IN)
    low, high, column = call(k_lists, [(32, 128), (32, 128), (LIST, 8)], packed)
    (part,) = call(k_own_pairs, [(8, PAIRS)], packed)
    low, high = low.reshape(1, 2, 2, 8, 128), high.reshape(1, 2, 2, 8, 128)
    ghosts = [g.reshape(-1, 128) for g in spread(low, high, here)]
    low, high, scal, pre, av = call(
        k_features,
        [(32, 192), (32, 192), (8, PAIRS), (128, PAIRS), (128, PAIRS)],
        packed,
        part,
        *ghosts,
        column,
        wb,
        wav,
    )
    ei, ej, latent, hid, tangent, nav = call(
        k_own_env,
        [(192, PAIRS), (192, PAIRS)] + [(128, PAIRS)] * 4,
        packed,
        scal,
        pre,
        av,
        wb,
        wav,
        w_mix,
    )
    low, high = low.reshape(1, 2, 2, 8, 192), high.reshape(1, 2, 2, 8, 192)
    ghosts = [g.reshape(-1, 192) for g in spread(low, high, here)]
    before, after, cells, ej, h, tbar = call(
        k_energy,
        [(128, 192), (128, 192), (256, 192), (192, PAIRS), (128, PAIRS), (CHAN, PAIRS)],
        packed,
        scal,
        av,
        *ghosts,
        ei,
        ej,
        hid,
        w_mix,
        wo,
    )
    part, energy = call(
        k_direct,
        [(8, PAIRS), (4, ATOMS)],
        packed,
        scal,
        av,
        nav,
        ei,
        ej,
        latent,
        tangent,
        h,
        tbar,
        w_mix,
        wo,
    )
    before, after = before.reshape(4, 4, 8, 192), after.reshape(4, 4, 8, 192)
    back, (part, energy) = collect(before, after, cells.reshape(4, 4, 2, 8, 192), here, (part, energy))
    back = back.reshape(LIST, 192)
    before, after, cells, dbar = call(
        k_env_back, [(128, 128), (128, 128), (256, 128), (8, PAIRS)], packed, scal, av, nav, part, back, column
    )
    (own,) = call(k_own_force, [(8, ATOMS)], packed, dbar)
    before, after = before.reshape(4, 4, 8, 128), after.reshape(4, 4, 8, 128)
    back, own = collect(before, after, cells.reshape(4, 4, 2, 8, 128), here, own)
    back = back.reshape(LIST, 128)
    (out,) = call(k_force, [(16, 128)], own, back, column, energy)
    out = send(out, MOVE_OUT)
    return call(k_unpack, [(3, 1, 1, 1, ATOMS), (1, 1, 1, ATOMS)], out)


def solution(mesh):
    in_specs = (
        P(None, "gx", "gy", "gz", None),
        P("gx", "gy", "gz", None),
        P("gx", "gy", "gz", None),
        P("gx", "gy", "gz", None, None),
        P("gx", "gy", "gz", None, None),
        P("gx", "gy", "gz", None, None),
        P(),
        P(),
        P(),
        P(),
        P(),
        P(),
        P(),
    )
    out_specs = (P(None, "gx", "gy", "gz", None), P("gx", "gy", "gz", None))
    return jax.shard_map(shards, mesh=mesh, in_specs=in_specs, out_specs=out_specs, check_vma=False)
```

```python
import math

import jax
import jax.numpy as jnp

from jax import lax
from jax.experimental import pallas as pl
from jax.experimental.pallas import tpu as pltpu
from jax.sharding import PartitionSpec as P

AXES = ("gx", "gy", "gz")
SHAPE = (16, 4, 8)
ATOMS = 512
PAIRS = 1024
LIST = 64
CHAN = 64
STEP = math.pi / 12.0
F32 = jnp.float32
BF16 = jnp.bfloat16


def flat(x, y, z):
    return (x * SHAPE[1] + y) * SHAPE[2] + z


def device(chip_x, chip_y, chip_z, core):
    return flat((chip_z % 8) * 2 + core, chip_y, (chip_z // 8) * 4 + chip_x)


def home(x, y, z):
    x, y, z = x % SHAPE[0], y % SHAPE[1], z % SHAPE[2]
    return device(z // 2, y, (x - 1) % 16, z % 2)


CELLS = [(x, y, z) for x in range(SHAPE[0]) for y in range(SHAPE[1]) for z in range(SHAPE[2])]
CHIPS = [(x, y, z, c) for x in range(4) for y in range(4) for z in range(16) for c in range(2)]
MOVE_IN = [(flat(*c), home(*c)) for c in CELLS]
MOVE_OUT = [(b, a) for a, b in MOVE_IN]
UP = [(home(x, y, z), home(x, y, z + 1)) for x, y, z in CELLS]
DOWN = [(b, a) for a, b in UP]


def along(spot, axis, position, core):
    spot = list(spot)
    spot[axis], spot[3] = position, core
    return device(*spot)


def snake(axis, count):
    pairs = []
    for spot in CHIPS:
        at, core = spot[axis], spot[3]
        then = at + 1 - 2 * core
        goal = along(spot, axis, then, core) if 0 <= then < count else along(spot, axis, at, 1 - core)
        pairs.append((device(*spot), goal))
    return pairs


def ends(axis, count):
    return [(device(*s), along(s, axis, count - 1 - s[axis], s[3])) for s in CHIPS if s[axis] in (0, count - 1)]


RINGS = {0: (2, 16), 1: (1, 4)}
FORTH = {a: snake(*r) for a, r in RINGS.items()}
BACK = {a: [(j, i) for i, j in p] for a, p in FORTH.items()}
ENDS = {a: ends(*r) for a, r in RINGS.items()}


def send(x, pairs):
    return lax.ppermute(x, AXES, pairs)


def spots():
    gx, gy, gz = (lax.axis_index(a) for a in AXES)
    return {0: (gz // 4) * 8 + gx // 2, 1: gy, 2: gx % 2}


def swap(axis, first, last, here):
    at, upward, count = here[axis], here[2] == 0, RINGS[axis][1]
    forth = send(jnp.where(upward, last, first), FORTH[axis])
    ring = send(jnp.where(at == 0, first, last), ENDS[axis])
    back = send(jnp.where(upward, first, last), BACK[axis])
    start, end = at == 0, at == count - 1
    before = jnp.where(~start, jnp.where(upward, forth, back), jnp.where(start, ring, back))
    after = jnp.where(end, jnp.where(end, ring, back), jnp.where(~upward, forth, back))
    return before, after


def spread(low, high, here):
    before, after = swap(0, low, high, here)
    cells = jnp.concatenate([before, low, high, after], axis=0)
    before, after = swap(1, cells[:, 0:1], cells[:, 1:2], here)
    cells = jnp.concatenate([before, cells, after], axis=1)
    before = send(cells[:, :, 1], UP)
    after = send(cells[:, :, 0], DOWN)
    return before, after, cells


def collect(before, after, cells, here, beside):
    first = send(after, UP)
    last = send(before, DOWN)
    cells = cells + jnp.stack([first, last], axis=2)
    cells, beside = lax.optimization_barrier((cells, beside))
    for axis in (1, 0):
        first = lax.slice_in_dim(cells, 0, 1, axis=axis)
        last = lax.slice_in_dim(cells, 3, 4, axis=axis)
        from_before, from_after = swap(axis, first, last, here)
        cells = lax.slice_in_dim(cells, 1, 3, axis=axis) + jnp.concatenate([from_before, from_after], axis=axis)
    return cells, beside


def split2(x):
    high = x.astype(BF16)
    low = (x - high.astype(F32)).astype(BF16)
    return high, low


def split3(x):
    high = x.astype(BF16)
    rest = x - high.astype(F32)
    mid = rest.astype(BF16)
    return high, mid, (rest - mid.astype(F32)).astype(BF16)


def dot(a, b, ca, cb):
    return lax.dot_general(a, b, (((ca,), (cb,)), ((), ())), preferred_element_type=F32)


def weighted(w, x):
    wh, wl = split2(w)
    xh, xl = split2(x)
    return dot(wh, xh, 0, 0) + (dot(wl, xh, 0, 0) + dot(wh, xl, 0, 0))


def weighted_t(w, x):
    wh, wl = split2(w)
    xh, xl = split2(x)
    return dot(wh, xh, 1, 0) + (dot(wl, xh, 1, 0) + dot(wh, xl, 1, 0))


def pick(table, onehot, parts=2):
    rows = table.shape[0]
    pieces = split3(table) if parts == 3 else split2(table)
    full = dot(jnp.concatenate(pieces, axis=0), onehot, 1, 0)
    out = full[:rows]
    for i in range(1, parts):
        out = out + full[rows * i : rows * (i + 1)]
    return out


def put(values, onehot, parts=2):
    rows = values.shape[0]
    pieces = split3(values) if parts == 3 else split2(values)
    full = dot(jnp.concatenate(pieces, axis=0), onehot, 1, 1)
    out = full[:rows]
    for i in range(1, parts):
        out = out + full[rows * i : rows * (i + 1)]
    return out


def put_rows(values, onehot):
    high, low = split2(values)
    return dot(onehot, high, 1, 1) + dot(onehot, low, 1, 1)


def lanes(block):
    return jnp.concatenate([block[i : i + 1] for i in range(block.shape[0])], axis=1)


def match(index, count):
    ids = lax.broadcasted_iota(jnp.int32, (count, index.shape[1]), 0)
    return jnp.where(ids == index, 1.0, 0.0).astype(BF16)


def centers_of(packed):
    return lanes(packed[16:24]).astype(jnp.int32)


def partners_of(packed):
    return lanes(packed[24:32]).astype(jnp.int32)


def live_of(packed):
    return lanes(packed[32:40])


def own_table(packed):
    return jnp.concatenate([lanes(packed[4 * k : 4 * k + 4]) for k in range(4)], axis=0)


def ghost_cell(partners):
    rows = partners - ATOMS
    cell = rows >> 3
    skip = jnp.zeros_like(cell)
    for start in (21, 23, 33, 35):
        skip = skip + jnp.where(cell >= start, 2, 0)
    full = cell + skip
    return full >> 4, (full >> 2) & 3, full & 3, rows & 7


def ghost_slot(partners):
    p, q, r, atom = ghost_cell(partners)
    column = p * 4 + q
    slot = jnp.where(r == 0, column * 8, jnp.where(r == 3, column * 8 + 128, 256 + (column * 2 + r - 1) * 8)) + atom
    return jnp.where(partners >= ATOMS, slot, -1)


def k_pack(pos_in, kind_in, names_in, center_in, partner_in, live_in, out_ref, pos_ref, kind_ref, names_ref, center_ref, partner_ref, live_ref, sems):
    moves = [
        pltpu.make_async_copy(source, target, sems.at[i])
        for i, (source, target) in enumerate(
            [
                (pos_in, pos_ref),
                (kind_in, kind_ref),
                (names_in, names_ref),
                (center_in, center_ref),
                (partner_in, partner_ref),
                (live_in, live_ref),
            ]
        )
    ]
    for move in moves:
        move.start()
    out_ref[40:48] = jnp.zeros((8, 128), F32)
    for move in moves:
        move.wait()
    for k in range(3):
        for i in range(4):
            out_ref[4 * k + i : 4 * k + i + 1] = pos_ref[k, 0, 0, 0:1, 128 * i : 128 * i + 128]
    for i in range(4):
        out_ref[12 + i : 13 + i] = kind_ref[0, 0, 0:1, 128 * i : 128 * i + 128].astype(F32)
    out_ref[16:24] = center_ref[0, 0, 0].astype(F32)
    out_ref[24:32] = partner_ref[0, 0, 0].astype(F32)
    out_ref[32:40] = live_ref[0, 0, 0].astype(F32)
    names = [names_ref[i, j, k : k + 1] for i in range(2) for j in range(2) for k in range(2)]
    names.append(jnp.full((1, 64), -1, jnp.int32))
    out_ref[40:41] = jnp.concatenate(names, axis=1).astype(F32)


def pack(*args):
    return pl.pallas_call(
        k_pack,
        out_shape=jax.ShapeDtypeStruct((48, 128), F32),
        in_specs=[pl.BlockSpec(memory_space=pltpu.MemorySpace.HBM)] * len(args),
        out_specs=pl.BlockSpec(memory_space=pltpu.VMEM),
        scratch_shapes=[pltpu.VMEM(a.shape, a.dtype) for a in args] + [pltpu.SemaphoreType.DMA((len(args),))],
        compiler_params=pltpu.CompilerParams(vmem_limit_bytes=60 * 1024 * 1024),
        name="k_pack",
    )(*args)


def k_lists(packed_ref, low_ref, high_ref, column_ref):
    packed = packed_ref[...]
    names = packed[40:41].astype(jnp.int32)
    found = pick(own_table(packed), match(names, ATOMS), 3)
    wide = jnp.concatenate([found, jnp.zeros((124, 128), F32)], axis=0).T
    low_ref[...] = wide[:32]
    high_ref[...] = wide[32:64]
    column_ref[...] = jnp.broadcast_to(packed[40:41], (8, 128)).T[:LIST]


def k_own_pairs(packed_ref, out_ref):
    packed = packed_ref[...]
    table = own_table(packed)
    at_center = pick(table, match(centers_of(packed), ATOMS), 3)
    at_partner = pick(table, match(partners_of(packed), ATOMS), 3)
    out_ref[0:3] = at_partner[0:3] - at_center[0:3]
    out_ref[3:4] = at_partner[3:4]
    out_ref[4:5] = at_center[3:4]
    out_ref[5:8] = jnp.zeros((3, PAIRS), F32)


def k_features(
    packed_ref, part_ref, before_ref, after_ref, cells_ref, column_ref, wb_ref, wav_ref, low_ref, high_ref, scal_ref, pre_ref, av_ref
):
    packed = packed_ref[...]
    part = part_ref[...]
    ghost = jnp.concatenate([before_ref[...], after_ref[...], cells_ref[...]], axis=0).T[0:8]
    partners = partners_of(packed)
    slots = match(ghost_slot(partners), 512)
    pieces = split3(ghost)
    far = dot(jnp.concatenate(pieces, axis=0), slots, 1, 0)
    far = far[0:8] + (far[8:16] + far[16:24])
    moved = [jnp.where(c == 0, -6.0, jnp.where(c == 3, 6.0, 0.0)) for c in ghost_cell(partners)[:3]]
    moved = jnp.where(partners >= ATOMS, jnp.concatenate(moved, axis=0), 0.0)
    disp = part[0:3] + (far[0:3] + moved)
    partner_kind = part[3:4] + far[3:4]
    center_kind = part[4:5]
    radius = jnp.sqrt(jnp.sum(disp * disp, axis=0, keepdims=True) + 0.25)
    inv = 1.0 / radius
    unit = disp * inv
    scaled = radius * 0.2
    base = 1.0 + scaled * scaled
    live = live_of(packed)
    cut = live / (base * base)
    orders = lax.broadcasted_iota(jnp.int32, (8, 1), 0).astype(F32) + 1.0
    angle = radius * orders * STEP
    basis = jnp.sin(angle) * inv
    kinds = lax.broadcasted_iota(jnp.int32, (8, 1), 0).astype(F32)
    first = jnp.where(center_kind == kinds, 1.0, 0.0)
    second = jnp.where(partner_kind == kinds, 1.0, 0.0)
    pre = weighted(wb_ref[...], jnp.concatenate([basis, first, second], axis=0))
    latent = cut * (pre * jax.nn.sigmoid(pre))
    av = weighted(wav_ref[...], latent)
    a = av[:CHAN]
    terms = jnp.concatenate([unit[k : k + 1] * a for k in range(3)], axis=0)
    named = jnp.where(column_ref[:, 0:1].astype(jnp.int32) == centers_of(packed), 1.0, 0.0).astype(BF16)
    msg = put_rows(terms, named)
    low_ref[...] = msg[:32]
    high_ref[...] = msg[32:]
    scal_ref[0:3] = unit
    scal_ref[3:4] = radius
    scal_ref[4:5] = inv
    scal_ref[5:6] = cut
    scal_ref[6:7] = live * (-0.8) * scaled / (base * base * base)
    scal_ref[7:8] = live
    pre_ref[...] = pre
    av_ref[...] = av


def k_own_env(packed_ref, scal_ref, pre_ref, av_ref, wb_ref, wav_ref, wm_ref, ei_ref, ej_ref, lat_ref, hid_ref, tan_ref, nav_ref):
    packed = packed_ref[...]
    scal = scal_ref[...]
    unit, radius, inv, cut, slope = scal[0:3], scal[3:4], scal[4:5], scal[5:6], scal[6:7]
    av = av_ref[...]
    a = av[:CHAN]
    terms = jnp.concatenate([unit[k : k + 1] * a for k in range(3)], axis=0)
    at_center = match(centers_of(packed), ATOMS)
    env = put(terms, at_center)
    ei_ref[...] = pick(env, at_center)
    ej_ref[...] = pick(env, match(partners_of(packed), ATOMS))
    pre = pre_ref[...]
    gate = jax.nn.sigmoid(pre)
    act = pre * gate
    latent = cut * act
    lat_ref[...] = latent
    hid_ref[...] = weighted(wm_ref[0:128], latent)
    orders = lax.broadcasted_iota(jnp.int32, (8, 1), 0).astype(F32) + 1.0
    angle = radius * orders * STEP
    change = (jnp.cos(angle) * (orders * STEP) - jnp.sin(angle) * inv) * inv
    tangent = slope * act + cut * (gate * (1.0 + pre * (1.0 - gate))) * weighted(wb_ref[0:8], change)
    tan_ref[...] = tangent
    nav_ref[...] = weighted(wav_ref[...], tangent)


def k_energy(
    packed_ref,
    scal_ref,
    av_ref,
    before_ref,
    after_ref,
    cells_ref,
    ei_ref,
    ejown_ref,
    hid_ref,
    wm_ref,
    wo_ref,
    to_before_ref,
    to_after_ref,
    to_cells_ref,
    ej_ref,
    h_ref,
    tb_ref,
):
    packed = packed_ref[...]
    scal = scal_ref[...]
    unit, cut = scal[0:3], scal[5:6]
    slots = match(ghost_slot(partners_of(packed)), 512)
    high, low = split2(jnp.concatenate([before_ref[...], after_ref[...], cells_ref[...]], axis=0))
    ej = ejown_ref[...] + (dot(high, slots, 0, 0) + dot(low, slots, 0, 0))
    ei = ei_ref[...]
    coupling = 0.0
    for k in range(3):
        rows = slice(k * CHAN, (k + 1) * CHAN)
        coupling = coupling + ei[rows] * (unit[k : k + 1] + ej[rows])
    v = av_ref[CHAN:]
    mix = wm_ref[128:]
    h = hid_ref[...] + weighted(mix, v * coupling)
    gate = jax.nn.sigmoid(h)
    out = wo_ref[...]
    hbar = (cut * out) * (gate * (1.0 + h * (1.0 - gate)))
    tbar = weighted_t(mix, hbar)
    cbar = tbar * v
    back = jnp.concatenate([cbar * ei[k * CHAN : (k + 1) * CHAN] for k in range(3)], axis=0)
    msg = put_rows(back, slots)
    to_before_ref[...] = msg[:128]
    to_after_ref[...] = msg[128:256]
    to_cells_ref[...] = msg[256:]
    ej_ref[...] = ej
    h_ref[...] = h
    tb_ref[...] = tbar


def k_direct(
    packed_ref, scal_ref, av_ref, nav_ref, ei_ref, ej_ref, lat_ref, tan_ref, h_ref, tb_ref, wm_ref, wo_ref, part_ref, energy_ref
):
    packed = packed_ref[...]
    scal = scal_ref[...]
    unit, cut, slope = scal[0:3], scal[5:6], scal[6:7]
    at_center = match(centers_of(packed), ATOMS)
    at_partner = match(partners_of(packed), ATOMS)
    ei, ej = ei_ref[...], ej_ref[...]
    a, v = av_ref[:CHAN], av_ref[CHAN:]
    na, nv = nav_ref[:CHAN], nav_ref[CHAN:]
    tbar = tb_ref[...]
    cbar = tbar * v
    h = h_ref[...]
    gate = jax.nn.sigmoid(h)
    out = wo_ref[...]
    score = jnp.sum(out * (lat_ref[...] + h * gate), axis=0, keepdims=True)
    energy_ref[...] = put(jnp.concatenate([cut * score, jnp.zeros((7, PAIRS), F32)], axis=0), at_center)[0:4]
    ubar = cut * out
    hbar = ubar * (gate * (1.0 + h * (1.0 - gate)))
    lbar = ubar + weighted_t(wm_ref[0:128], hbar)
    coupling = 0.0
    to_center, to_partner, along = [], [], []
    for k in range(3):
        rows = slice(k * CHAN, (k + 1) * CHAN)
        mixed = unit[k : k + 1] + ej[rows]
        coupling = coupling + ei[rows] * mixed
        to_center.append(cbar * mixed)
        to_partner.append(cbar * ei[rows])
        along.append(jnp.sum(to_partner[k], axis=0, keepdims=True))
    vbar = tbar * coupling
    rbar = slope * score + jnp.sum(lbar * tan_ref[...], axis=0, keepdims=True) + jnp.sum(vbar * nv, axis=0, keepdims=True)
    grad = put(jnp.concatenate(to_center, axis=0), at_center) + put(jnp.concatenate(to_partner, axis=0), at_partner)
    gi = pick(grad, at_center)
    for k in range(3):
        rows = slice(k * CHAN, (k + 1) * CHAN)
        along[k] = along[k] + jnp.sum(a * gi[rows], axis=0, keepdims=True)
        rbar = rbar + unit[k : k + 1] * jnp.sum(na * gi[rows], axis=0, keepdims=True)
    part_ref[...] = jnp.concatenate(along + [rbar, jnp.zeros((4, PAIRS), F32)], axis=0)


def k_env_back(
    packed_ref,
    scal_ref,
    av_ref,
    nav_ref,
    part_ref,
    back_ref,
    column_ref,
    to_before_ref,
    to_after_ref,
    to_cells_ref,
    dbar_ref,
):
    packed = packed_ref[...]
    scal = scal_ref[...]
    unit, inv = scal[0:3], scal[4:5]
    part = part_ref[...]
    named = jnp.where(column_ref[:, 0:1].astype(jnp.int32) == centers_of(packed), 1.0, 0.0).astype(BF16)
    high, low = split2(back_ref[...])
    gi = dot(high, named, 0, 0) + dot(low, named, 0, 0)
    a, na = av_ref[:CHAN], nav_ref[:CHAN]
    along = []
    rbar = part[3:4]
    for k in range(3):
        rows = slice(k * CHAN, (k + 1) * CHAN)
        along.append(part[k : k + 1] + jnp.sum(a * gi[rows], axis=0, keepdims=True))
        rbar = rbar + unit[k : k + 1] * jnp.sum(na * gi[rows], axis=0, keepdims=True)
    for k in range(3):
        rbar = rbar - inv * along[k] * unit[k : k + 1]
    dbar = jnp.concatenate([along[k] * inv + rbar * unit[k : k + 1] for k in range(3)] + [jnp.zeros((5, PAIRS), F32)], axis=0)
    slots = match(ghost_slot(partners_of(packed)), 512)
    msg = jnp.concatenate([put_rows(dbar, slots), jnp.zeros((512, 120), F32)], axis=1)
    to_before_ref[...] = msg[:128]
    to_after_ref[...] = msg[128:256]
    to_cells_ref[...] = msg[256:]
    dbar_ref[...] = dbar


def k_own_force(packed_ref, dbar_ref, out_ref):
    packed = packed_ref[...]
    dbar = dbar_ref[...]
    out_ref[...] = put(dbar, match(partners_of(packed), ATOMS)) - put(dbar, match(centers_of(packed), ATOMS))


def k_force(own_ref, back_ref, column_ref, energy_ref, out_ref):
    named = jnp.where(
        column_ref[:, 0:1].astype(jnp.int32) == lax.broadcasted_iota(jnp.int32, (LIST, ATOMS), 1), 1.0, 0.0
    ).astype(BF16)
    returned = pick(back_ref[...].T[0:8], named, 3)
    total = -(own_ref[0:3] + returned[0:3])
    energy = energy_ref[...]
    for k in range(3):
        for i in range(4):
            out_ref[4 * k + i : 4 * k + i + 1] = total[k : k + 1, 128 * i : 128 * i + 128]
    for i in range(4):
        out_ref[12 + i : 13 + i] = energy[0:1, 128 * i : 128 * i + 128]


def k_unpack(in_ref, force_ref, energy_ref):
    for k in range(3):
        for i in range(4):
            force_ref[k, 0, 0, 0:1, 128 * i : 128 * i + 128] = in_ref[4 * k + i : 4 * k + i + 1]
    for i in range(4):
        energy_ref[0, 0, 0:1, 128 * i : 128 * i + 128] = in_ref[12 + i : 13 + i]


def call(kernel, outs, *args):
    shapes = [jax.ShapeDtypeStruct(s, F32) for s in outs]
    spec = pl.BlockSpec(memory_space=pltpu.VMEM)
    return pl.pallas_call(
        kernel,
        out_shape=shapes,
        in_specs=[spec] * len(args),
        out_specs=[spec] * len(outs),
        compiler_params=pltpu.CompilerParams(vmem_limit_bytes=48 * 1024 * 1024),
        name=kernel.__name__,
    )(*args)


def shards(
    positions,
    species,
    send_lists,
    pair_center,
    pair_partner,
    pair_slot_live,
    w_basis,
    emb_center,
    emb_partner,
    w_env,
    w_value,
    w_mix,
    w_out,
):
    packed = pack(positions, species, send_lists, pair_center, pair_partner, pair_slot_live)
    here = spots()
    zeros = jnp.zeros((2, 128), F32)
    wb = jnp.concatenate([w_basis, emb_center, zeros, emb_partner, zeros], axis=0)
    wav = jnp.concatenate([w_env, w_value], axis=1)
    wo = w_out.reshape(128, 1)

    packed = send(packed, MOVE_IN)
    low, high, column = call(k_lists, [(32, 128), (32, 128), (LIST, 8)], packed)
    (part,) = call(k_own_pairs, [(8, PAIRS)], packed)
    low, high = low.reshape(1, 2, 2, 8, 128), high.reshape(1, 2, 2, 8, 128)
    ghosts = [g.reshape(-1, 128) for g in spread(low, high, here)]
    low, high, scal, pre, av = call(
        k_features,
        [(32, 192), (32, 192), (8, PAIRS), (128, PAIRS), (128, PAIRS)],
        packed,
        part,
        *ghosts,
        column,
        wb,
        wav,
    )
    ei, ej, latent, hid, tangent, nav = call(
        k_own_env,
        [(192, PAIRS), (192, PAIRS)] + [(128, PAIRS)] * 4,
        packed,
        scal,
        pre,
        av,
        wb,
        wav,
        w_mix,
    )
    low, high = low.reshape(1, 2, 2, 8, 192), high.reshape(1, 2, 2, 8, 192)
    ghosts = [g.reshape(-1, 192) for g in spread(low, high, here)]
    before, after, cells, ej, h, tbar = call(
        k_energy,
        [(128, 192), (128, 192), (256, 192), (192, PAIRS), (128, PAIRS), (CHAN, PAIRS)],
        packed,
        scal,
        av,
        *ghosts,
        ei,
        ej,
        hid,
        w_mix,
        wo,
    )
    part, energy = call(
        k_direct,
        [(8, PAIRS), (4, ATOMS)],
        packed,
        scal,
        av,
        nav,
        ei,
        ej,
        latent,
        tangent,
        h,
        tbar,
        w_mix,
        wo,
    )
    before, after = before.reshape(4, 4, 8, 192), after.reshape(4, 4, 8, 192)
    back, (part, energy) = collect(before, after, cells.reshape(4, 4, 2, 8, 192), here, (part, energy))
    back = back.reshape(LIST, 192)
    before, after, cells, dbar = call(
        k_env_back, [(128, 128), (128, 128), (256, 128), (8, PAIRS)], packed, scal, av, nav, part, back, column
    )
    (own,) = call(k_own_force, [(8, ATOMS)], packed, dbar)
    before, after = before.reshape(4, 4, 8, 128), after.reshape(4, 4, 8, 128)
    back, own = collect(before, after, cells.reshape(4, 4, 2, 8, 128), here, own)
    back = back.reshape(LIST, 128)
    (out,) = call(k_force, [(16, 128)], own, back, column, energy)
    out = send(out, MOVE_OUT)
    return call(k_unpack, [(3, 1, 1, 1, ATOMS), (1, 1, 1, ATOMS)], out)


def solution(mesh):
    in_specs = (
        P(None, "gx", "gy", "gz", None),
        P("gx", "gy", "gz", None),
        P("gx", "gy", "gz", None),
        P("gx", "gy", "gz", None, None),
        P("gx", "gy", "gz", None, None),
        P("gx", "gy", "gz", None, None),
        P(),
        P(),
        P(),
        P(),
        P(),
        P(),
        P(),
    )
    out_specs = (P(None, "gx", "gy", "gz", None), P("gx", "gy", "gz", None))
    return jax.shard_map(shards, mesh=mesh, in_specs=in_specs, out_specs=out_specs, check_vma=False)
```

```python
import math

import jax
import jax.numpy as jnp

from jax import lax
from jax.experimental import pallas as pl
from jax.experimental.pallas import tpu as pltpu
from jax.sharding import PartitionSpec as P

AXES = ("gx", "gy", "gz")
SHAPE = (16, 4, 8)
ATOMS = 512
PAIRS = 1024
LIST = 64
CHAN = 64
STEP = math.pi / 12.0
F32 = jnp.float32
BF16 = jnp.bfloat16


def flat(x, y, z):
    return (x * SHAPE[1] + y) * SHAPE[2] + z


def device(chip_x, chip_y, chip_z, core):
    return flat((chip_z % 8) * 2 + core, chip_y, (chip_z // 8) * 4 + chip_x)


def home(x, y, z):
    x, y, z = x % SHAPE[0], y % SHAPE[1], z % SHAPE[2]
    return device(z // 2, y, x, z % 2)


CELLS = [(x, y, z) for x in range(SHAPE[0]) for y in range(SHAPE[1]) for z in range(SHAPE[2])]
CHIPS = [(x, y, z, c) for x in range(4) for y in range(4) for z in range(16) for c in range(2)]
MOVE_IN = [(flat(*c), home(*c)) for c in CELLS]
MOVE_OUT = [(b, a) for a, b in MOVE_IN]
UP = [(home(x, y, z), home(x, y, z + 1)) for x, y, z in CELLS]
DOWN = [(b, a) for a, b in UP]


def along(spot, axis, position, core):
    spot = list(spot)
    spot[axis], spot[3] = position, core
    return device(*spot)


def snake(axis, count):
    pairs = []
    for spot in CHIPS:
        at, core = spot[axis], spot[3]
        then = at + 1 - 2 * core
        goal = along(spot, axis, then, core) if 0 <= then < count else along(spot, axis, at, 1 - core)
        pairs.append((device(*spot), goal))
    return pairs


def ends(axis, count):
    return [(device(*s), along(s, axis, count - 1 - s[axis], s[3])) for s in CHIPS if s[axis] in (0, count - 1)]


RINGS = {0: (2, 16), 1: (1, 4)}
FORTH = {a: snake(*r) for a, r in RINGS.items()}
BACK = {a: [(j, i) for i, j in p] for a, p in FORTH.items()}
ENDS = {a: ends(*r) for a, r in RINGS.items()}


def send(x, pairs):
    return lax.ppermute(x, AXES, pairs)


def spots():
    gx, gy, gz = (lax.axis_index(a) for a in AXES)
    return {0: (gz // 4) * 8 + gx // 2, 1: gy, 2: gx % 2}


def swap(axis, first, last, here):
    at, upward, count = here[axis], here[2] == 0, RINGS[axis][1]
    forth = send(jnp.where(upward, last, first), FORTH[axis])
    ring = send(jnp.where(at == 0, first, last), ENDS[axis])
    back = send(jnp.where(upward, first, last), BACK[axis])
    start, end = at == 0, at == count - 1
    before = jnp.where(~start, jnp.where(upward, forth, back), jnp.where(start, ring, back))
    after = jnp.where(end, jnp.where(end, ring, back), jnp.where(~upward, forth, back))
    return before, after


def spread(low, high, here):
    before, after = swap(0, low, high, here)
    cells = jnp.concatenate([before, low, high, after], axis=0)
    before, after = swap(1, cells[:, 0:1], cells[:, 1:2], here)
    cells = jnp.concatenate([before, cells, after], axis=1)
    before = send(cells[:, :, 1], UP)
    after = send(cells[:, :, 0], DOWN)
    return before, after, cells


def collect(before, after, cells, here, beside):
    first = send(after, UP)
    last = send(before, DOWN)
    cells = cells + jnp.stack([first, last], axis=2)
    cells, beside = lax.optimization_barrier((cells, beside))
    for axis in (1, 0):
        first = lax.slice_in_dim(cells, 0, 1, axis=axis)
        last = lax.slice_in_dim(cells, 3, 4, axis=axis)
        from_before, from_after = swap(axis, first, last, here)
        cells = lax.slice_in_dim(cells, 1, 3, axis=axis) + jnp.concatenate([from_before, from_after], axis=axis)
    return cells, beside


def split2(x):
    high = x.astype(BF16)
    low = (x - high.astype(F32)).astype(BF16)
    return high, low


def split3(x):
    high = x.astype(BF16)
    rest = x - high.astype(F32)
    mid = rest.astype(BF16)
    return high, mid, (rest - mid.astype(F32)).astype(BF16)


def dot(a, b, ca, cb):
    return lax.dot_general(a, b, (((ca,), (cb,)), ((), ())), preferred_element_type=F32)


def halves(x):
    high = x.astype(BF16).astype(F32)
    return high, x - high


def weighted(w, x):
    wh, wl = halves(w)
    xh, xl = halves(x)
    left = jnp.concatenate([wh, wl, wh], axis=0).astype(BF16)
    return dot(left, jnp.concatenate([xh, xh, xl], axis=0).astype(BF16), 0, 0)


def weighted_t(w, x):
    wh, wl = halves(w)
    xh, xl = halves(x)
    left = jnp.concatenate([wh, wl, wh], axis=1).astype(BF16)
    return dot(left, jnp.concatenate([xh, xh, xl], axis=0).astype(BF16), 1, 0)


def pick(table, onehot, parts=2):
    rows = table.shape[0]
    pieces = split3(table) if parts == 3 else split2(table)
    full = dot(jnp.concatenate(pieces, axis=0), onehot, 1, 0)
    out = full[:rows]
    for i in range(1, parts):
        out = out + full[rows * i : rows * (i + 1)]
    return out


def put(values, onehot, parts=2):
    rows = values.shape[0]
    pieces = split3(values) if parts == 3 else split2(values)
    full = dot(jnp.concatenate(pieces, axis=0), onehot, 1, 1)
    out = full[:rows]
    for i in range(1, parts):
        out = out + full[rows * i : rows * (i + 1)]
    return out


def put_rows(values, onehot):
    high, low = halves(values)
    if values.shape[0] % 128:
        gap = jnp.zeros((-values.shape[0] % 128, values.shape[1]), F32)
        high, low = jnp.concatenate([high, gap], axis=0), jnp.concatenate([low, gap], axis=0)
    rows = high.shape[0]
    full = dot(onehot, jnp.concatenate([high, low], axis=0).astype(BF16), 1, 1)
    return (full[:, :rows] + full[:, rows:])[:, : values.shape[0]]


def lanes(block):
    return jnp.concatenate([block[i : i + 1] for i in range(block.shape[0])], axis=1)


def match(index, count):
    ids = lax.broadcasted_iota(jnp.int32, (count, index.shape[1]), 0)
    return jnp.where(ids == index, 1.0, 0.0).astype(BF16)


def centers_of(packed):
    return lanes(packed[16:24]).astype(jnp.int32)


def partners_of(packed):
    return lanes(packed[24:32]).astype(jnp.int32)


def live_of(packed):
    return lanes(packed[32:40])


def own_table(packed):
    return jnp.concatenate([lanes(packed[4 * k : 4 * k + 4]) for k in range(4)], axis=0)


def ghost_cell(partners):
    rows = partners - ATOMS
    cell = rows >> 3
    skip = jnp.zeros_like(cell)
    for start in (21, 23, 33, 35):
        skip = skip + jnp.where(cell >= start, 2, 0)
    full = cell + skip
    return full >> 4, (full >> 2) & 3, full & 3, rows & 7


def ghost_slot(partners):
    p, q, r, atom = ghost_cell(partners)
    column = p * 4 + q
    slot = jnp.where(r == 0, column * 8, jnp.where(r == 3, column * 8 + 128, 256 + (column * 2 + r - 1) * 8)) + atom
    return jnp.where(partners >= ATOMS, slot, -1)


def k_pack(pos_in, kind_in, names_in, center_in, partner_in, live_in, out_ref, pos_ref, kind_ref, names_ref, center_ref, partner_ref, live_ref, sems):
    moves = [
        pltpu.make_async_copy(source, target, sems.at[i])
        for i, (source, target) in enumerate(
            [
                (pos_in, pos_ref),
                (kind_in, kind_ref),
                (names_in, names_ref),
                (center_in, center_ref),
                (partner_in, partner_ref),
                (live_in, live_ref),
            ]
        )
    ]
    for move in moves:
        move.start()
    out_ref[40:48] = jnp.zeros((8, 128), F32)
    for move in moves:
        move.wait()
    for k in range(3):
        for i in range(4):
            out_ref[4 * k + i : 4 * k + i + 1] = pos_ref[k, 0, 0, 0:1, 128 * i : 128 * i + 128]
    for i in range(4):
        out_ref[12 + i : 13 + i] = kind_ref[0, 0, 0:1, 128 * i : 128 * i + 128].astype(F32)
    out_ref[16:24] = center_ref[0, 0, 0].astype(F32)
    out_ref[24:32] = partner_ref[0, 0, 0].astype(F32)
    out_ref[32:40] = live_ref[0, 0, 0].astype(F32)
    names = [names_ref[i, j, k : k + 1] for i in range(2) for j in range(2) for k in range(2)]
    names.append(jnp.full((1, 64), -1, jnp.int32))
    out_ref[40:41] = jnp.concatenate(names, axis=1).astype(F32)


def pack(*args):
    return pl.pallas_call(
        k_pack,
        out_shape=jax.ShapeDtypeStruct((48, 128), F32),
        in_specs=[pl.BlockSpec(memory_space=pltpu.MemorySpace.HBM)] * len(args),
        out_specs=pl.BlockSpec(memory_space=pltpu.VMEM),
        scratch_shapes=[pltpu.VMEM(a.shape, a.dtype) for a in args] + [pltpu.SemaphoreType.DMA((len(args),))],
        compiler_params=pltpu.CompilerParams(vmem_limit_bytes=60 * 1024 * 1024),
        name="k_pack",
    )(*args)


def k_lists(packed_ref, low_ref, high_ref, column_ref):
    packed = packed_ref[...]
    names = packed[40:41].astype(jnp.int32)
    found = pick(own_table(packed), match(names, ATOMS), 3)
    wide = jnp.concatenate([found, jnp.zeros((124, 128), F32)], axis=0).T
    low_ref[...] = wide[:32]
    high_ref[...] = wide[32:64]
    column_ref[...] = jnp.broadcast_to(packed[40:41], (8, 128)).T[:LIST]


def k_own_pairs(packed_ref, out_ref):
    packed = packed_ref[...]
    table = own_table(packed)
    at_center = pick(table, match(centers_of(packed), ATOMS), 3)
    at_partner = pick(table, match(partners_of(packed), ATOMS), 3)
    out_ref[0:3] = at_partner[0:3] - at_center[0:3]
    out_ref[3:4] = at_partner[3:4]
    out_ref[4:5] = at_center[3:4]
    out_ref[5:8] = jnp.zeros((3, PAIRS), F32)


def k_features(
    packed_ref, part_ref, before_ref, after_ref, cells_ref, column_ref, wb_ref, wav_ref, low_ref, high_ref, scal_ref, pre_ref, av_ref
):
    packed = packed_ref[...]
    part = part_ref[...]
    ghost = jnp.concatenate([before_ref[...], after_ref[...], cells_ref[...]], axis=0).T[0:8]
    partners = partners_of(packed)
    slots = match(ghost_slot(partners), 512)
    pieces = split3(ghost)
    far = dot(jnp.concatenate(pieces, axis=0), slots, 1, 0)
    far = far[0:8] + (far[8:16] + far[16:24])
    moved = [jnp.where(c == 0, -6.0, jnp.where(c == 3, 6.0, 0.0)) for c in ghost_cell(partners)[:3]]
    moved = jnp.where(partners >= ATOMS, jnp.concatenate(moved, axis=0), 0.0)
    disp = part[0:3] + (far[0:3] + moved)
    partner_kind = part[3:4] + far[3:4]
    center_kind = part[4:5]
    radius = jnp.sqrt(jnp.sum(disp * disp, axis=0, keepdims=True) + 0.25)
    inv = 1.0 / radius
    unit = disp * inv
    scaled = radius * 0.2
    base = 1.0 + scaled * scaled
    live = live_of(packed)
    cut = live / (base * base)
    orders = lax.broadcasted_iota(jnp.int32, (8, 1), 0).astype(F32) + 1.0
    angle = radius * orders * STEP
    basis = jnp.sin(angle) * inv
    kinds = lax.broadcasted_iota(jnp.int32, (8, 1), 0).astype(F32)
    first = jnp.where(center_kind == kinds, 1.0, 0.0)
    second = jnp.where(partner_kind == kinds, 1.0, 0.0)
    pre = weighted(wb_ref[...], jnp.concatenate([basis, first, second], axis=0))
    latent = cut * (pre * jax.nn.sigmoid(pre))
    av = weighted(wav_ref[...], latent)
    a = av[:CHAN]
    terms = jnp.concatenate([unit[k : k + 1] * a for k in range(3)], axis=0)
    named = jnp.where(column_ref[:, 0:1].astype(jnp.int32) == centers_of(packed), 1.0, 0.0).astype(BF16)
    msg = put_rows(terms, named)
    low_ref[...] = msg[:32]
    high_ref[...] = msg[32:]
    scal_ref[0:3] = unit
    scal_ref[3:4] = radius
    scal_ref[4:5] = inv
    scal_ref[5:6] = cut
    scal_ref[6:7] = live * (-0.8) * scaled / (base * base * base)
    scal_ref[7:8] = live
    pre_ref[...] = pre
    av_ref[...] = av


def k_own_env(packed_ref, scal_ref, pre_ref, av_ref, wb_ref, wav_ref, wm_ref, ei_ref, ej_ref, lat_ref, hid_ref, tan_ref, nav_ref):
    packed = packed_ref[...]
    scal = scal_ref[...]
    unit, radius, inv, cut, slope = scal[0:3], scal[3:4], scal[4:5], scal[5:6], scal[6:7]
    av = av_ref[...]
    a = av[:CHAN]
    terms = jnp.concatenate([unit[k : k + 1] * a for k in range(3)], axis=0)
    at_center = match(centers_of(packed), ATOMS)
    env = put(terms, at_center)
    ei_ref[...] = pick(env, at_center)
    ej_ref[...] = pick(env, match(partners_of(packed), ATOMS))
    pre = pre_ref[...]
    gate = jax.nn.sigmoid(pre)
    act = pre * gate
    latent = cut * act
    lat_ref[...] = latent
    hid_ref[...] = weighted(wm_ref[0:128], latent)
    orders = lax.broadcasted_iota(jnp.int32, (8, 1), 0).astype(F32) + 1.0
    angle = radius * orders * STEP
    change = (jnp.cos(angle) * (orders * STEP) - jnp.sin(angle) * inv) * inv
    tangent = slope * act + cut * (gate * (1.0 + pre * (1.0 - gate))) * weighted(wb_ref[0:8], change)
    tan_ref[...] = tangent
    nav_ref[...] = weighted(wav_ref[...], tangent)


def k_energy(
    packed_ref,
    scal_ref,
    av_ref,
    before_ref,
    after_ref,
    cells_ref,
    ei_ref,
    ejown_ref,
    hid_ref,
    wm_ref,
    wo_ref,
    to_before_ref,
    to_after_ref,
    to_cells_ref,
    ej_ref,
    h_ref,
    tb_ref,
):
    packed = packed_ref[...]
    scal = scal_ref[...]
    unit, cut = scal[0:3], scal[5:6]
    slots = match(ghost_slot(partners_of(packed)), 512)
    ghost = jnp.concatenate([before_ref[...], after_ref[...], cells_ref[...]], axis=0)
    ghost = jnp.concatenate([ghost, jnp.zeros((512, 64), F32)], axis=1).T[:192]
    ej = ejown_ref[...] + pick(ghost, slots)
    ei = ei_ref[...]
    coupling = 0.0
    for k in range(3):
        rows = slice(k * CHAN, (k + 1) * CHAN)
        coupling = coupling + ei[rows] * (unit[k : k + 1] + ej[rows])
    v = av_ref[CHAN:]
    mix = wm_ref[128:]
    h = hid_ref[...] + weighted(mix, v * coupling)
    gate = jax.nn.sigmoid(h)
    out = wo_ref[...]
    hbar = (cut * out) * (gate * (1.0 + h * (1.0 - gate)))
    tbar = weighted_t(mix, hbar)
    cbar = tbar * v
    back = jnp.concatenate([cbar * ei[k * CHAN : (k + 1) * CHAN] for k in range(3)], axis=0)
    msg = put_rows(back, slots)
    to_before_ref[...] = msg[:128]
    to_after_ref[...] = msg[128:256]
    to_cells_ref[...] = msg[256:]
    ej_ref[...] = ej
    h_ref[...] = h
    tb_ref[...] = tbar


def k_direct(
    packed_ref, scal_ref, av_ref, nav_ref, ei_ref, ej_ref, lat_ref, tan_ref, h_ref, tb_ref, wm_ref, wo_ref, part_ref, energy_ref
):
    packed = packed_ref[...]
    scal = scal_ref[...]
    unit, cut, slope = scal[0:3], scal[5:6], scal[6:7]
    at_center = match(centers_of(packed), ATOMS)
    at_partner = match(partners_of(packed), ATOMS)
    ei, ej = ei_ref[...], ej_ref[...]
    a, v = av_ref[:CHAN], av_ref[CHAN:]
    na, nv = nav_ref[:CHAN], nav_ref[CHAN:]
    tbar = tb_ref[...]
    cbar = tbar * v
    h = h_ref[...]
    gate = jax.nn.sigmoid(h)
    out = wo_ref[...]
    score = jnp.sum(out * (lat_ref[...] + h * gate), axis=0, keepdims=True)
    energy_ref[...] = put(jnp.concatenate([cut * score, jnp.zeros((7, PAIRS), F32)], axis=0), at_center)[0:4]
    ubar = cut * out
    hbar = ubar * (gate * (1.0 + h * (1.0 - gate)))
    lbar = ubar + weighted_t(wm_ref[0:128], hbar)
    coupling = 0.0
    to_center, to_partner, along = [], [], []
    for k in range(3):
        rows = slice(k * CHAN, (k + 1) * CHAN)
        mixed = unit[k : k + 1] + ej[rows]
        coupling = coupling + ei[rows] * mixed
        to_center.append(cbar * mixed)
        to_partner.append(cbar * ei[rows])
        along.append(jnp.sum(to_partner[k], axis=0, keepdims=True))
    vbar = tbar * coupling
    rbar = slope * score + jnp.sum(lbar * tan_ref[...], axis=0, keepdims=True) + jnp.sum(vbar * nv, axis=0, keepdims=True)
    grad = put(jnp.concatenate(to_center, axis=0), at_center) + put(jnp.concatenate(to_partner, axis=0), at_partner)
    gi = pick(grad, at_center)
    for k in range(3):
        rows = slice(k * CHAN, (k + 1) * CHAN)
        along[k] = along[k] + jnp.sum(a * gi[rows], axis=0, keepdims=True)
        rbar = rbar + unit[k : k + 1] * jnp.sum(na * gi[rows], axis=0, keepdims=True)
    part_ref[...] = jnp.concatenate(along + [rbar, jnp.zeros((4, PAIRS), F32)], axis=0)


def k_env_back(
    packed_ref,
    scal_ref,
    av_ref,
    nav_ref,
    part_ref,
    back_ref,
    column_ref,
    to_before_ref,
    to_after_ref,
    to_cells_ref,
    dbar_ref,
):
    packed = packed_ref[...]
    scal = scal_ref[...]
    unit, inv = scal[0:3], scal[4:5]
    part = part_ref[...]
    named = jnp.where(column_ref[:, 0:1].astype(jnp.int32) == centers_of(packed), 1.0, 0.0).astype(BF16)
    high, low = split2(back_ref[...])
    gi = dot(high, named, 0, 0) + dot(low, named, 0, 0)
    a, na = av_ref[:CHAN], nav_ref[:CHAN]
    along = []
    rbar = part[3:4]
    for k in range(3):
        rows = slice(k * CHAN, (k + 1) * CHAN)
        along.append(part[k : k + 1] + jnp.sum(a * gi[rows], axis=0, keepdims=True))
        rbar = rbar + unit[k : k + 1] * jnp.sum(na * gi[rows], axis=0, keepdims=True)
    for k in range(3):
        rbar = rbar - inv * along[k] * unit[k : k + 1]
    dbar = jnp.concatenate([along[k] * inv + rbar * unit[k : k + 1] for k in range(3)] + [jnp.zeros((5, PAIRS), F32)], axis=0)
    slots = match(ghost_slot(partners_of(packed)), 512)
    msg = put_rows(jnp.concatenate([dbar, jnp.zeros((120, PAIRS), F32)], axis=0), slots)
    to_before_ref[...] = msg[:128]
    to_after_ref[...] = msg[128:256]
    to_cells_ref[...] = msg[256:]
    dbar_ref[...] = dbar


def k_own_force(packed_ref, dbar_ref, out_ref):
    packed = packed_ref[...]
    dbar = dbar_ref[...]
    out_ref[...] = put(dbar, match(partners_of(packed), ATOMS)) - put(dbar, match(centers_of(packed), ATOMS))


def k_force(own_ref, back_ref, column_ref, energy_ref, out_ref):
    named = jnp.where(
        column_ref[:, 0:1].astype(jnp.int32) == lax.broadcasted_iota(jnp.int32, (LIST, ATOMS), 1), 1.0, 0.0
    ).astype(BF16)
    returned = pick(back_ref[...].T[0:8], named, 3)
    total = -(own_ref[0:3] + returned[0:3])
    energy = energy_ref[...]
    for k in range(3):
        for i in range(4):
            out_ref[4 * k + i : 4 * k + i + 1] = total[k : k + 1, 128 * i : 128 * i + 128]
    for i in range(4):
        out_ref[12 + i : 13 + i] = energy[0:1, 128 * i : 128 * i + 128]


def k_unpack(in_ref, force_ref, energy_ref):
    for k in range(3):
        for i in range(4):
            force_ref[k, 0, 0, 0:1, 128 * i : 128 * i + 128] = in_ref[4 * k + i : 4 * k + i + 1]
    for i in range(4):
        energy_ref[0, 0, 0:1, 128 * i : 128 * i + 128] = in_ref[12 + i : 13 + i]


def call(kernel, outs, *args):
    shapes = [jax.ShapeDtypeStruct(s, F32) for s in outs]
    spec = pl.BlockSpec(memory_space=pltpu.VMEM)
    return pl.pallas_call(
        kernel,
        out_shape=shapes,
        in_specs=[spec] * len(args),
        out_specs=[spec] * len(outs),
        compiler_params=pltpu.CompilerParams(vmem_limit_bytes=48 * 1024 * 1024),
        name=kernel.__name__,
    )(*args)


def shards(
    positions,
    species,
    send_lists,
    pair_center,
    pair_partner,
    pair_slot_live,
    w_basis,
    emb_center,
    emb_partner,
    w_env,
    w_value,
    w_mix,
    w_out,
):
    packed = pack(positions, species, send_lists, pair_center, pair_partner, pair_slot_live)
    here = spots()
    zeros = jnp.zeros((2, 128), F32)
    wb = jnp.concatenate([w_basis, emb_center, zeros, emb_partner, zeros], axis=0)
    wav = jnp.concatenate([w_env, w_value], axis=1)
    wo = w_out.reshape(128, 1)

    packed = send(packed, MOVE_IN)
    low, high, column = call(k_lists, [(32, 128), (32, 128), (LIST, 8)], packed)
    (part,) = call(k_own_pairs, [(8, PAIRS)], packed)
    low, high = low.reshape(1, 2, 2, 8, 128), high.reshape(1, 2, 2, 8, 128)
    ghosts = [g.reshape(-1, 128) for g in spread(low, high, here)]
    low, high, scal, pre, av = call(
        k_features,
        [(32, 192), (32, 192), (8, PAIRS), (128, PAIRS), (128, PAIRS)],
        packed,
        part,
        *ghosts,
        column,
        wb,
        wav,
    )
    ei, ej, latent, hid, tangent, nav = call(
        k_own_env,
        [(192, PAIRS), (192, PAIRS)] + [(128, PAIRS)] * 4,
        packed,
        scal,
        pre,
        av,
        wb,
        wav,
        w_mix,
    )
    low, high = low.reshape(1, 2, 2, 8, 192), high.reshape(1, 2, 2, 8, 192)
    ghosts = [g.reshape(-1, 192) for g in spread(low, high, here)]
    before, after, cells, ej, h, tbar = call(
        k_energy,
        [(128, 192), (128, 192), (256, 192), (192, PAIRS), (128, PAIRS), (CHAN, PAIRS)],
        packed,
        scal,
        av,
        *ghosts,
        ei,
        ej,
        hid,
        w_mix,
        wo,
    )
    part, energy = call(
        k_direct,
        [(8, PAIRS), (4, ATOMS)],
        packed,
        scal,
        av,
        nav,
        ei,
        ej,
        latent,
        tangent,
        h,
        tbar,
        w_mix,
        wo,
    )
    before, after = before.reshape(4, 4, 8, 192), after.reshape(4, 4, 8, 192)
    back, (part, energy) = collect(before, after, cells.reshape(4, 4, 2, 8, 192), here, (part, energy))
    back = back.reshape(LIST, 192)
    before, after, cells, dbar = call(
        k_env_back, [(128, 128), (128, 128), (256, 128), (8, PAIRS)], packed, scal, av, nav, part, back, column
    )
    (own,) = call(k_own_force, [(8, ATOMS)], packed, dbar)
    before, after = before.reshape(4, 4, 8, 128), after.reshape(4, 4, 8, 128)
    back, own = collect(before, after, cells.reshape(4, 4, 2, 8, 128), here, own)
    back = back.reshape(LIST, 128)
    (out,) = call(k_force, [(16, 128)], own, back, column, energy)
    out = send(out, MOVE_OUT)
    return call(k_unpack, [(3, 1, 1, 1, ATOMS), (1, 1, 1, ATOMS)], out)


def solution(mesh):
    in_specs = (
        P(None, "gx", "gy", "gz", None),
        P("gx", "gy", "gz", None),
        P("gx", "gy", "gz", None),
        P("gx", "gy", "gz", None, None),
        P("gx", "gy", "gz", None, None),
        P("gx", "gy", "gz", None, None),
        P(),
        P(),
        P(),
        P(),
        P(),
        P(),
        P(),
    )
    out_specs = (P(None, "gx", "gy", "gz", None), P("gx", "gy", "gz", None))
    return jax.shard_map(shards, mesh=mesh, in_specs=in_specs, out_specs=out_specs, check_vma=False)
```

```python
import math

import jax
import jax.numpy as jnp

from jax import lax
from jax.experimental import pallas as pl
from jax.experimental.pallas import tpu as pltpu
from jax.sharding import PartitionSpec as P

AXES = ("gx", "gy", "gz")
SHAPE = (16, 4, 8)
ATOMS = 512
PAIRS = 1024
LIST = 64
CHAN = 64
STEP = math.pi / 12.0
F32 = jnp.float32
BF16 = jnp.bfloat16


def flat(x, y, z):
    return (x * SHAPE[1] + y) * SHAPE[2] + z


def device(chip_x, chip_y, chip_z, core):
    return flat((chip_z % 8) * 2 + core, chip_y, (chip_z // 8) * 4 + chip_x)


def home(x, y, z):
    x, y, z = x % SHAPE[0], y % SHAPE[1], z % SHAPE[2]
    return device(z // 2, y, x, z % 2)


CELLS = [(x, y, z) for x in range(SHAPE[0]) for y in range(SHAPE[1]) for z in range(SHAPE[2])]
CHIPS = [(x, y, z, c) for x in range(4) for y in range(4) for z in range(16) for c in range(2)]
MOVE_IN = [(flat(*c), home(*c)) for c in CELLS]
MOVE_OUT = [(b, a) for a, b in MOVE_IN]
UP = [(home(x, y, z), home(x, y, z + 1)) for x, y, z in CELLS]
DOWN = [(b, a) for a, b in UP]


def along(spot, axis, position, core):
    spot = list(spot)
    spot[axis], spot[3] = position, core
    return device(*spot)


def snake(axis, count):
    pairs = []
    for spot in CHIPS:
        at, core = spot[axis], spot[3]
        then = at + 1 - 2 * core
        goal = along(spot, axis, then, core) if 0 <= then < count else along(spot, axis, at, 1 - core)
        pairs.append((device(*spot), goal))
    return pairs


def ends(axis, count):
    return [(device(*s), along(s, axis, count - 1 - s[axis], s[3])) for s in CHIPS if s[axis] in (0, count - 1)]


RINGS = {0: (2, 16), 1: (1, 4)}
FORTH = {a: snake(*r) for a, r in RINGS.items()}
BACK = {a: [(j, i) for i, j in p] for a, p in FORTH.items()}
ENDS = {a: ends(*r) for a, r in RINGS.items()}


def send(x, pairs):
    return lax.ppermute(x, AXES, pairs)


def spots():
    gx, gy, gz = (lax.axis_index(a) for a in AXES)
    return {0: (gz // 4) * 8 + gx // 2, 1: gy, 2: gx % 2}


def swap(axis, first, last, here):
    at, upward, count = here[axis], here[2] == 0, RINGS[axis][1]
    forth = send(jnp.where(upward, last, first), FORTH[axis])
    ring = send(jnp.where(at == 0, first, last), ENDS[axis])
    back = send(jnp.where(upward, first, last), BACK[axis])
    start, end = at == 0, at == count - 1
    before = jnp.where(~start, jnp.where(upward, forth, back), jnp.where(start, ring, back))
    after = jnp.where(end, jnp.where(end, ring, back), jnp.where(~upward, forth, back))
    return before, after


def spread(low, high, here, first, second):
    before, after = swap(0, low, high, here)
    cells = jnp.concatenate([before, low, high, after], axis=0)
    cells, first = lax.optimization_barrier((cells, first))
    before, after = swap(1, cells[:, 0:1], cells[:, 1:2], here)
    cells = jnp.concatenate([before, cells, after], axis=1)
    cells, second = lax.optimization_barrier((cells, second))
    before = send(cells[:, :, 1], UP)
    after = send(cells[:, :, 0], DOWN)
    return (before, after, cells), first, second


def collect(before, after, cells, here, beside):
    first = send(after, UP)
    last = send(before, DOWN)
    cells = cells + jnp.stack([first, last], axis=2)
    cells, beside = lax.optimization_barrier((cells, beside))
    for axis in (1, 0):
        first = lax.slice_in_dim(cells, 0, 1, axis=axis)
        last = lax.slice_in_dim(cells, 3, 4, axis=axis)
        from_before, from_after = swap(axis, first, last, here)
        cells = lax.slice_in_dim(cells, 1, 3, axis=axis) + jnp.concatenate([from_before, from_after], axis=axis)
    return cells, beside


def split2(x):
    high = x.astype(BF16)
    low = (x - high.astype(F32)).astype(BF16)
    return high, low


def split3(x):
    high = x.astype(BF16)
    rest = x - high.astype(F32)
    mid = rest.astype(BF16)
    return high, mid, (rest - mid.astype(F32)).astype(BF16)


def dot(a, b, ca, cb):
    return lax.dot_general(a, b, (((ca,), (cb,)), ((), ())), preferred_element_type=F32)


def halves(x):
    high = x.astype(BF16).astype(F32)
    return high, x - high


def weighted(w, x):
    wh, wl = halves(w)
    xh, xl = halves(x)
    left = jnp.concatenate([wh, wl, wh], axis=0).astype(BF16)
    return dot(left, jnp.concatenate([xh, xh, xl], axis=0).astype(BF16), 0, 0)


def weighted_t(w, x):
    wh, wl = halves(w)
    xh, xl = halves(x)
    left = jnp.concatenate([wh, wl, wh], axis=1).astype(BF16)
    return dot(left, jnp.concatenate([xh, xh, xl], axis=0).astype(BF16), 1, 0)


def pick(table, onehot, parts=2):
    rows = table.shape[0]
    pieces = split3(table) if parts == 3 else split2(table)
    full = dot(jnp.concatenate(pieces, axis=0), onehot, 1, 0)
    out = full[:rows]
    for i in range(1, parts):
        out = out + full[rows * i : rows * (i + 1)]
    return out


def put(values, onehot, parts=2):
    rows = values.shape[0]
    pieces = split3(values) if parts == 3 else split2(values)
    full = dot(jnp.concatenate(pieces, axis=0), onehot, 1, 1)
    out = full[:rows]
    for i in range(1, parts):
        out = out + full[rows * i : rows * (i + 1)]
    return out


def put_rows(values, onehot):
    high, low = halves(values)
    if values.shape[0] % 128:
        gap = jnp.zeros((-values.shape[0] % 128, values.shape[1]), F32)
        high, low = jnp.concatenate([high, gap], axis=0), jnp.concatenate([low, gap], axis=0)
    rows = high.shape[0]
    full = dot(onehot, jnp.concatenate([high, low], axis=0).astype(BF16), 1, 1)
    return (full[:, :rows] + full[:, rows:])[:, : values.shape[0]]


def lanes(block):
    return jnp.concatenate([block[i : i + 1] for i in range(block.shape[0])], axis=1)


def match(index, count):
    ids = lax.broadcasted_iota(jnp.int32, (count, index.shape[1]), 0)
    return jnp.where(ids == index, 1.0, 0.0).astype(BF16)


def centers_of(packed):
    return lanes(packed[16:24]).astype(jnp.int32)


def partners_of(packed):
    return lanes(packed[24:32]).astype(jnp.int32)


def live_of(packed):
    return lanes(packed[32:40])


def own_table(packed):
    return jnp.concatenate([lanes(packed[4 * k : 4 * k + 4]) for k in range(4)], axis=0)


def ghost_cell(partners):
    rows = partners - ATOMS
    cell = rows >> 3
    skip = jnp.zeros_like(cell)
    for start in (21, 23, 33, 35):
        skip = skip + jnp.where(cell >= start, 2, 0)
    full = cell + skip
    return full >> 4, (full >> 2) & 3, full & 3, rows & 7


def ghost_slot(partners):
    p, q, r, atom = ghost_cell(partners)
    column = p * 4 + q
    slot = jnp.where(r == 0, column * 8, jnp.where(r == 3, column * 8 + 128, 256 + (column * 2 + r - 1) * 8)) + atom
    return jnp.where(partners >= ATOMS, slot, -1)


def k_pack(pos_in, kind_in, names_in, center_in, partner_in, live_in, out_ref, pos_ref, kind_ref, names_ref, center_ref, partner_ref, live_ref, sems):
    moves = [
        pltpu.make_async_copy(source, target, sems.at[i])
        for i, (source, target) in enumerate(
            [
                (pos_in, pos_ref),
                (kind_in, kind_ref),
                (names_in, names_ref),
                (center_in, center_ref),
                (partner_in, partner_ref),
                (live_in, live_ref),
            ]
        )
    ]
    for move in moves:
        move.start()
    out_ref[40:48] = jnp.zeros((8, 128), F32)
    for move in moves:
        move.wait()
    for k in range(3):
        for i in range(4):
            out_ref[4 * k + i : 4 * k + i + 1] = pos_ref[k, 0, 0, 0:1, 128 * i : 128 * i + 128]
    for i in range(4):
        out_ref[12 + i : 13 + i] = kind_ref[0, 0, 0:1, 128 * i : 128 * i + 128].astype(F32)
    out_ref[16:24] = center_ref[0, 0, 0].astype(F32)
    out_ref[24:32] = partner_ref[0, 0, 0].astype(F32)
    out_ref[32:40] = live_ref[0, 0, 0].astype(F32)
    names = [names_ref[i, j, k : k + 1] for i in range(2) for j in range(2) for k in range(2)]
    names.append(jnp.full((1, 64), -1, jnp.int32))
    out_ref[40:41] = jnp.concatenate(names, axis=1).astype(F32)


def pack(*args):
    return pl.pallas_call(
        k_pack,
        out_shape=jax.ShapeDtypeStruct((48, 128), F32),
        in_specs=[pl.BlockSpec(memory_space=pltpu.MemorySpace.HBM)] * len(args),
        out_specs=pl.BlockSpec(memory_space=pltpu.VMEM),
        scratch_shapes=[pltpu.VMEM(a.shape, a.dtype) for a in args] + [pltpu.SemaphoreType.DMA((len(args),))],
        compiler_params=pltpu.CompilerParams(vmem_limit_bytes=60 * 1024 * 1024),
        name="k_pack",
    )(*args)


def k_lists(packed_ref, low_ref, high_ref, column_ref):
    packed = packed_ref[...]
    names = packed[40:41].astype(jnp.int32)
    found = pick(own_table(packed), match(names, ATOMS), 3)
    wide = jnp.concatenate([found, jnp.zeros((124, 128), F32)], axis=0).T
    low_ref[...] = wide[:32]
    high_ref[...] = wide[32:64]
    column_ref[...] = jnp.broadcast_to(packed[40:41], (8, 128)).T[:LIST]


def k_own_pairs(packed_ref, out_ref):
    packed = packed_ref[...]
    table = own_table(packed)
    at_center = pick(table, match(centers_of(packed), ATOMS), 3)
    at_partner = pick(table, match(partners_of(packed), ATOMS), 3)
    out_ref[0:3] = at_partner[0:3] - at_center[0:3]
    out_ref[3:4] = at_partner[3:4]
    out_ref[4:5] = at_center[3:4]
    out_ref[5:8] = jnp.zeros((3, PAIRS), F32)


def k_features(
    packed_ref, part_ref, before_ref, after_ref, cells_ref, column_ref, wb_ref, wav_ref, low_ref, high_ref, scal_ref, pre_ref, av_ref
):
    packed = packed_ref[...]
    part = part_ref[...]
    ghost = jnp.concatenate([before_ref[...], after_ref[...], cells_ref[...]], axis=0).T[0:8]
    partners = partners_of(packed)
    slots = match(ghost_slot(partners), 512)
    pieces = split3(ghost)
    far = dot(jnp.concatenate(pieces, axis=0), slots, 1, 0)
    far = far[0:8] + (far[8:16] + far[16:24])
    moved = [jnp.where(c == 0, -6.0, jnp.where(c == 3, 6.0, 0.0)) for c in ghost_cell(partners)[:3]]
    moved = jnp.where(partners >= ATOMS, jnp.concatenate(moved, axis=0), 0.0)
    disp = part[0:3] + (far[0:3] + moved)
    partner_kind = part[3:4] + far[3:4]
    center_kind = part[4:5]
    radius = jnp.sqrt(jnp.sum(disp * disp, axis=0, keepdims=True) + 0.25)
    inv = 1.0 / radius
    unit = disp * inv
    scaled = radius * 0.2
    base = 1.0 + scaled * scaled
    live = live_of(packed)
    cut = live / (base * base)
    orders = lax.broadcasted_iota(jnp.int32, (8, 1), 0).astype(F32) + 1.0
    angle = radius * orders * STEP
    basis = jnp.sin(angle) * inv
    kinds = lax.broadcasted_iota(jnp.int32, (8, 1), 0).astype(F32)
    first = jnp.where(center_kind == kinds, 1.0, 0.0)
    second = jnp.where(partner_kind == kinds, 1.0, 0.0)
    pre = weighted(wb_ref[...], jnp.concatenate([basis, first, second], axis=0))
    latent = cut * (pre * jax.nn.sigmoid(pre))
    av = weighted(wav_ref[...], latent)
    a = av[:CHAN]
    terms = jnp.concatenate([unit[k : k + 1] * a for k in range(3)], axis=0)
    named = jnp.where(column_ref[:, 0:1].astype(jnp.int32) == centers_of(packed), 1.0, 0.0).astype(BF16)
    msg = put_rows(terms, named)
    low_ref[...] = msg[:32]
    high_ref[...] = msg[32:]
    scal_ref[0:3] = unit
    scal_ref[3:4] = radius
    scal_ref[4:5] = inv
    scal_ref[5:6] = cut
    scal_ref[6:7] = live * (-0.8) * scaled / (base * base * base)
    scal_ref[7:8] = live
    pre_ref[...] = pre
    av_ref[...] = av


def k_own_env(packed_ref, scal_ref, av_ref, ei_ref, ej_ref):
    packed = packed_ref[...]
    unit = scal_ref[0:3]
    a = av_ref[:CHAN]
    terms = jnp.concatenate([unit[k : k + 1] * a for k in range(3)], axis=0)
    at_center = match(centers_of(packed), ATOMS)
    env = put(terms, at_center)
    ei_ref[...] = pick(env, at_center)
    ej_ref[...] = pick(env, match(partners_of(packed), ATOMS))


def k_tangent(scal_ref, pre_ref, wb_ref, wav_ref, wm_ref, lat_ref, hid_ref, tan_ref, nav_ref):
    scal = scal_ref[...]
    radius, inv, cut, slope = scal[3:4], scal[4:5], scal[5:6], scal[6:7]
    pre = pre_ref[...]
    gate = jax.nn.sigmoid(pre)
    act = pre * gate
    latent = cut * act
    lat_ref[...] = latent
    hid_ref[...] = weighted(wm_ref[0:128], latent)
    orders = lax.broadcasted_iota(jnp.int32, (8, 1), 0).astype(F32) + 1.0
    angle = radius * orders * STEP
    change = (jnp.cos(angle) * (orders * STEP) - jnp.sin(angle) * inv) * inv
    tangent = slope * act + cut * (gate * (1.0 + pre * (1.0 - gate))) * weighted(wb_ref[0:8], change)
    tan_ref[...] = tangent
    nav_ref[...] = weighted(wav_ref[...], tangent)


def k_energy(
    packed_ref,
    scal_ref,
    av_ref,
    before_ref,
    after_ref,
    cells_ref,
    ei_ref,
    ejown_ref,
    hid_ref,
    wm_ref,
    wo_ref,
    to_before_ref,
    to_after_ref,
    to_cells_ref,
    ej_ref,
    h_ref,
    tb_ref,
):
    packed = packed_ref[...]
    scal = scal_ref[...]
    unit, cut = scal[0:3], scal[5:6]
    slots = match(ghost_slot(partners_of(packed)), 512)
    ghost = jnp.concatenate([before_ref[...], after_ref[...], cells_ref[...]], axis=0)
    ghost = jnp.concatenate([ghost, jnp.zeros((512, 64), F32)], axis=1).T[:192]
    ej = ejown_ref[...] + pick(ghost, slots)
    ei = ei_ref[...]
    coupling = 0.0
    for k in range(3):
        rows = slice(k * CHAN, (k + 1) * CHAN)
        coupling = coupling + ei[rows] * (unit[k : k + 1] + ej[rows])
    v = av_ref[CHAN:]
    mix = wm_ref[128:]
    h = hid_ref[...] + weighted(mix, v * coupling)
    gate = jax.nn.sigmoid(h)
    out = wo_ref[...]
    hbar = (cut * out) * (gate * (1.0 + h * (1.0 - gate)))
    tbar = weighted_t(mix, hbar)
    cbar = tbar * v
    back = jnp.concatenate([cbar * ei[k * CHAN : (k + 1) * CHAN] for k in range(3)], axis=0)
    msg = put_rows(back, slots)
    to_before_ref[...] = msg[:128]
    to_after_ref[...] = msg[128:256]
    to_cells_ref[...] = msg[256:]
    ej_ref[...] = ej
    h_ref[...] = h
    tb_ref[...] = tbar


def k_direct(
    packed_ref, scal_ref, av_ref, nav_ref, ei_ref, ej_ref, lat_ref, tan_ref, h_ref, tb_ref, wm_ref, wo_ref, part_ref, energy_ref
):
    packed = packed_ref[...]
    scal = scal_ref[...]
    unit, cut, slope = scal[0:3], scal[5:6], scal[6:7]
    at_center = match(centers_of(packed), ATOMS)
    at_partner = match(partners_of(packed), ATOMS)
    ei, ej = ei_ref[...], ej_ref[...]
    a, v = av_ref[:CHAN], av_ref[CHAN:]
    na, nv = nav_ref[:CHAN], nav_ref[CHAN:]
    tbar = tb_ref[...]
    cbar = tbar * v
    h = h_ref[...]
    gate = jax.nn.sigmoid(h)
    out = wo_ref[...]
    score = jnp.sum(out * (lat_ref[...] + h * gate), axis=0, keepdims=True)
    energy_ref[...] = put(jnp.concatenate([cut * score, jnp.zeros((7, PAIRS), F32)], axis=0), at_center)[0:4]
    ubar = cut * out
    hbar = ubar * (gate * (1.0 + h * (1.0 - gate)))
    lbar = ubar + weighted_t(wm_ref[0:128], hbar)
    coupling = 0.0
    to_center, to_partner, along = [], [], []
    for k in range(3):
        rows = slice(k * CHAN, (k + 1) * CHAN)
        mixed = unit[k : k + 1] + ej[rows]
        coupling = coupling + ei[rows] * mixed
        to_center.append(cbar * mixed)
        to_partner.append(cbar * ei[rows])
        along.append(jnp.sum(to_partner[k], axis=0, keepdims=True))
    vbar = tbar * coupling
    rbar = slope * score + jnp.sum(lbar * tan_ref[...], axis=0, keepdims=True) + jnp.sum(vbar * nv, axis=0, keepdims=True)
    grad = put(jnp.concatenate(to_center, axis=0), at_center) + put(jnp.concatenate(to_partner, axis=0), at_partner)
    gi = pick(grad, at_center)
    for k in range(3):
        rows = slice(k * CHAN, (k + 1) * CHAN)
        along[k] = along[k] + jnp.sum(a * gi[rows], axis=0, keepdims=True)
        rbar = rbar + unit[k : k + 1] * jnp.sum(na * gi[rows], axis=0, keepdims=True)
    part_ref[...] = jnp.concatenate(along + [rbar, jnp.zeros((4, PAIRS), F32)], axis=0)


def k_env_back(
    packed_ref,
    scal_ref,
    av_ref,
    nav_ref,
    part_ref,
    back_ref,
    column_ref,
    to_before_ref,
    to_after_ref,
    to_cells_ref,
    dbar_ref,
):
    packed = packed_ref[...]
    scal = scal_ref[...]
    unit, inv = scal[0:3], scal[4:5]
    part = part_ref[...]
    named = jnp.where(column_ref[:, 0:1].astype(jnp.int32) == centers_of(packed), 1.0, 0.0).astype(BF16)
    high, low = split2(back_ref[...])
    gi = dot(high, named, 0, 0) + dot(low, named, 0, 0)
    a, na = av_ref[:CHAN], nav_ref[:CHAN]
    along = []
    rbar = part[3:4]
    for k in range(3):
        rows = slice(k * CHAN, (k + 1) * CHAN)
        along.append(part[k : k + 1] + jnp.sum(a * gi[rows], axis=0, keepdims=True))
        rbar = rbar + unit[k : k + 1] * jnp.sum(na * gi[rows], axis=0, keepdims=True)
    for k in range(3):
        rbar = rbar - inv * along[k] * unit[k : k + 1]
    dbar = jnp.concatenate([along[k] * inv + rbar * unit[k : k + 1] for k in range(3)] + [jnp.zeros((5, PAIRS), F32)], axis=0)
    slots = match(ghost_slot(partners_of(packed)), 512)
    msg = put_rows(jnp.concatenate([dbar, jnp.zeros((120, PAIRS), F32)], axis=0), slots)
    to_before_ref[...] = msg[:128]
    to_after_ref[...] = msg[128:256]
    to_cells_ref[...] = msg[256:]
    dbar_ref[...] = dbar


def k_own_force(packed_ref, dbar_ref, out_ref):
    packed = packed_ref[...]
    dbar = dbar_ref[...]
    out_ref[...] = put(dbar, match(partners_of(packed), ATOMS)) - put(dbar, match(centers_of(packed), ATOMS))


def k_force(own_ref, back_ref, column_ref, energy_ref, out_ref):
    named = jnp.where(
        column_ref[:, 0:1].astype(jnp.int32) == lax.broadcasted_iota(jnp.int32, (LIST, ATOMS), 1), 1.0, 0.0
    ).astype(BF16)
    returned = pick(back_ref[...].T[0:8], named, 3)
    total = -(own_ref[0:3] + returned[0:3])
    energy = energy_ref[...]
    for k in range(3):
        for i in range(4):
            out_ref[4 * k + i : 4 * k + i + 1] = total[k : k + 1, 128 * i : 128 * i + 128]
    for i in range(4):
        out_ref[12 + i : 13 + i] = energy[0:1, 128 * i : 128 * i + 128]


def k_unpack(in_ref, force_ref, energy_ref):
    for k in range(3):
        for i in range(4):
            force_ref[k, 0, 0, 0:1, 128 * i : 128 * i + 128] = in_ref[4 * k + i : 4 * k + i + 1]
    for i in range(4):
        energy_ref[0, 0, 0:1, 128 * i : 128 * i + 128] = in_ref[12 + i : 13 + i]


def call(kernel, outs, *args):
    shapes = [jax.ShapeDtypeStruct(s, F32) for s in outs]
    spec = pl.BlockSpec(memory_space=pltpu.VMEM)
    return pl.pallas_call(
        kernel,
        out_shape=shapes,
        in_specs=[spec] * len(args),
        out_specs=[spec] * len(outs),
        compiler_params=pltpu.CompilerParams(vmem_limit_bytes=48 * 1024 * 1024),
        name=kernel.__name__,
    )(*args)


def shards(
    positions,
    species,
    send_lists,
    pair_center,
    pair_partner,
    pair_slot_live,
    w_basis,
    emb_center,
    emb_partner,
    w_env,
    w_value,
    w_mix,
    w_out,
):
    packed = pack(positions, species, send_lists, pair_center, pair_partner, pair_slot_live)
    here = spots()
    zeros = jnp.zeros((2, 128), F32)
    wb = jnp.concatenate([w_basis, emb_center, zeros, emb_partner, zeros], axis=0)
    wav = jnp.concatenate([w_env, w_value], axis=1)
    wo = w_out.reshape(128, 1)

    packed = send(packed, MOVE_IN)
    low, high, column = call(k_lists, [(32, 128), (32, 128), (LIST, 8)], packed)
    (part,) = call(k_own_pairs, [(8, PAIRS)], packed)
    low, high = low.reshape(1, 2, 2, 8, 128), high.reshape(1, 2, 2, 8, 128)
    ghosts, part, _ = spread(low, high, here, part, ())
    ghosts = [g.reshape(-1, 128) for g in ghosts]
    low, high, scal, pre, av = call(
        k_features,
        [(32, 192), (32, 192), (8, PAIRS), (128, PAIRS), (128, PAIRS)],
        packed,
        part,
        *ghosts,
        column,
        wb,
        wav,
    )
    own = call(k_own_env, [(192, PAIRS), (192, PAIRS)], packed, scal, av)
    rest = call(k_tangent, [(128, PAIRS)] * 4, scal, pre, wb, wav, w_mix)
    low, high = low.reshape(1, 2, 2, 8, 192), high.reshape(1, 2, 2, 8, 192)
    ghosts, (ei, ej), (latent, hid, tangent, nav) = spread(low, high, here, own, rest)
    ghosts = [g.reshape(-1, 192) for g in ghosts]
    before, after, cells, ej, h, tbar = call(
        k_energy,
        [(128, 192), (128, 192), (256, 192), (192, PAIRS), (128, PAIRS), (CHAN, PAIRS)],
        packed,
        scal,
        av,
        *ghosts,
        ei,
        ej,
        hid,
        w_mix,
        wo,
    )
    part, energy = call(
        k_direct,
        [(8, PAIRS), (4, ATOMS)],
        packed,
        scal,
        av,
        nav,
        ei,
        ej,
        latent,
        tangent,
        h,
        tbar,
        w_mix,
        wo,
    )
    before, after = before.reshape(4, 4, 8, 192), after.reshape(4, 4, 8, 192)
    back, (part, energy) = collect(before, after, cells.reshape(4, 4, 2, 8, 192), here, (part, energy))
    back = back.reshape(LIST, 192)
    before, after, cells, dbar = call(
        k_env_back, [(128, 128), (128, 128), (256, 128), (8, PAIRS)], packed, scal, av, nav, part, back, column
    )
    (own,) = call(k_own_force, [(8, ATOMS)], packed, dbar)
    before, after = before.reshape(4, 4, 8, 128), after.reshape(4, 4, 8, 128)
    back, own = collect(before, after, cells.reshape(4, 4, 2, 8, 128), here, own)
    back = back.reshape(LIST, 128)
    (out,) = call(k_force, [(16, 128)], own, back, column, energy)
    out = send(out, MOVE_OUT)
    return call(k_unpack, [(3, 1, 1, 1, ATOMS), (1, 1, 1, ATOMS)], out)


def solution(mesh):
    in_specs = (
        P(None, "gx", "gy", "gz", None),
        P("gx", "gy", "gz", None),
        P("gx", "gy", "gz", None),
        P("gx", "gy", "gz", None, None),
        P("gx", "gy", "gz", None, None),
        P("gx", "gy", "gz", None, None),
        P(),
        P(),
        P(),
        P(),
        P(),
        P(),
        P(),
    )
    out_specs = (P(None, "gx", "gy", "gz", None), P("gx", "gy", "gz", None))
    return jax.shard_map(shards, mesh=mesh, in_specs=in_specs, out_specs=out_specs, check_vma=False)
```

```python
import math

import jax
import jax.numpy as jnp

from jax import lax
from jax.experimental import pallas as pl
from jax.experimental.pallas import tpu as pltpu
from jax.sharding import PartitionSpec as P

AXES = ("gx", "gy", "gz")
SHAPE = (16, 4, 8)
ATOMS = 512
PAIRS = 1024
LIST = 64
CHAN = 64
STEP = math.pi / 12.0
F32 = jnp.float32
BF16 = jnp.bfloat16


def flat(x, y, z):
    return (x * SHAPE[1] + y) * SHAPE[2] + z


def device(chip_x, chip_y, chip_z, core):
    return flat((chip_z % 8) * 2 + core, chip_y, (chip_z // 8) * 4 + chip_x)


def home(x, y, z):
    x, y, z = x % SHAPE[0], y % SHAPE[1], z % SHAPE[2]
    return device(z // 2, y, x, z % 2)


CELLS = [(x, y, z) for x in range(SHAPE[0]) for y in range(SHAPE[1]) for z in range(SHAPE[2])]
CHIPS = [(x, y, z, c) for x in range(4) for y in range(4) for z in range(16) for c in range(2)]
MOVE_IN = [(flat(*c), home(*c)) for c in CELLS]
MOVE_OUT = [(b, a) for a, b in MOVE_IN]
UP = [(home(x, y, z), home(x, y, z + 1)) for x, y, z in CELLS]
DOWN = [(b, a) for a, b in UP]


def along(spot, axis, position, core):
    spot = list(spot)
    spot[axis], spot[3] = position, core
    return device(*spot)


def snake(axis, count):
    pairs = []
    for spot in CHIPS:
        at, core = spot[axis], spot[3]
        then = at + 1 - 2 * core
        goal = along(spot, axis, then, core) if 0 <= then < count else along(spot, axis, at, 1 - core)
        pairs.append((device(*spot), goal))
    return pairs


def ends(axis, count):
    return [(device(*s), along(s, axis, count - 1 - s[axis], s[3])) for s in CHIPS if s[axis] in (0, count - 1)]


RINGS = {0: (2, 16), 1: (1, 4)}
FORTH = {a: snake(*r) for a, r in RINGS.items()}
BACK = {a: [(j, i) for i, j in p] for a, p in FORTH.items()}
ENDS = {a: ends(*r) for a, r in RINGS.items()}


def send(x, pairs):
    return lax.ppermute(x, AXES, pairs)


def spots():
    gx, gy, gz = (lax.axis_index(a) for a in AXES)
    return {0: (gz // 4) * 8 + gx // 2, 1: gy, 2: gx % 2}


def swap(axis, first, last, here):
    at, upward, count = here[axis], here[2] == 0, RINGS[axis][1]
    forth = send(jnp.where(upward, last, first), FORTH[axis])
    ring = send(jnp.where(at == 0, first, last), ENDS[axis])
    back = send(jnp.where(upward, first, last), BACK[axis])
    start, end = at == 0, at == count - 1
    before = jnp.where(~start, jnp.where(upward, forth, back), jnp.where(start, ring, back))
    after = jnp.where(end, jnp.where(end, ring, back), jnp.where(~upward, forth, back))
    return before, after


def spread(low, high, here, first, second):
    before, after = swap(0, low, high, here)
    cells = jnp.concatenate([before, low, high, after], axis=0)
    cells, first = lax.optimization_barrier((cells, first))
    before, after = swap(1, cells[:, 0:1], cells[:, 1:2], here)
    cells = jnp.concatenate([before, cells, after], axis=1)
    cells, second = lax.optimization_barrier((cells, second))
    before = send(cells[:, :, 1], UP)
    after = send(cells[:, :, 0], DOWN)
    return (before, after, cells), first, second


def collect(before, after, cells, here, beside):
    first = send(after, UP)
    last = send(before, DOWN)
    cells = cells + jnp.stack([first, last], axis=2)
    cells, beside = lax.optimization_barrier((cells, beside))
    for axis in (1, 0):
        first = lax.slice_in_dim(cells, 0, 1, axis=axis)
        last = lax.slice_in_dim(cells, 3, 4, axis=axis)
        from_before, from_after = swap(axis, first, last, here)
        cells = lax.slice_in_dim(cells, 1, 3, axis=axis) + jnp.concatenate([from_before, from_after], axis=axis)
    return cells, beside


def split2(x):
    high = x.astype(BF16)
    low = (x - high.astype(F32)).astype(BF16)
    return high, low


def split3(x):
    high = x.astype(BF16)
    rest = x - high.astype(F32)
    mid = rest.astype(BF16)
    return high, mid, (rest - mid.astype(F32)).astype(BF16)


def dot(a, b, ca, cb):
    return lax.dot_general(a, b, (((ca,), (cb,)), ((), ())), preferred_element_type=F32)


def halves(x):
    high = x.astype(BF16).astype(F32)
    return high, x - high


def weighted(w, x):
    wh, wl = halves(w)
    xh, xl = halves(x)
    left = jnp.concatenate([wh, wl, wh], axis=0).astype(BF16)
    return dot(left, jnp.concatenate([xh, xh, xl], axis=0).astype(BF16), 0, 0)


def weighted_t(w, x):
    wh, wl = halves(w)
    xh, xl = halves(x)
    left = jnp.concatenate([wh, wl, wh], axis=1).astype(BF16)
    return dot(left, jnp.concatenate([xh, xh, xl], axis=0).astype(BF16), 1, 0)


def pick(table, onehot, parts=2):
    rows = table.shape[0]
    pieces = split3(table) if parts == 3 else split2(table)
    full = dot(jnp.concatenate(pieces, axis=0), onehot, 1, 0)
    out = full[:rows]
    for i in range(1, parts):
        out = out + full[rows * i : rows * (i + 1)]
    return out


def put(values, onehot, parts=2):
    rows = values.shape[0]
    pieces = split3(values) if parts == 3 else split2(values)
    full = dot(jnp.concatenate(pieces, axis=0), onehot, 1, 1)
    out = full[:rows]
    for i in range(1, parts):
        out = out + full[rows * i : rows * (i + 1)]
    return out


def put_rows(values, onehot):
    high, low = halves(values)
    if values.shape[0] % 128:
        gap = jnp.zeros((-values.shape[0] % 128, values.shape[1]), F32)
        high, low = jnp.concatenate([high, gap], axis=0), jnp.concatenate([low, gap], axis=0)
    rows = high.shape[0]
    full = dot(onehot, jnp.concatenate([high, low], axis=0).astype(BF16), 1, 1)
    return (full[:, :rows] + full[:, rows:])[:, : values.shape[0]]


def lanes(block):
    return jnp.concatenate([block[i : i + 1] for i in range(block.shape[0])], axis=1)


def match(index, count):
    ids = lax.broadcasted_iota(jnp.int32, (count, index.shape[1]), 0)
    return jnp.where(ids == index, 1.0, 0.0).astype(BF16)


def centers_of(packed):
    return lanes(packed[16:24]).astype(jnp.int32)


def partners_of(packed):
    return lanes(packed[24:32]).astype(jnp.int32)


def live_of(packed):
    return lanes(packed[32:40])


def own_table(packed):
    return jnp.concatenate([lanes(packed[4 * k : 4 * k + 4]) for k in range(4)], axis=0)


def ghost_cell(partners):
    rows = partners - ATOMS
    cell = rows >> 3
    skip = jnp.zeros_like(cell)
    for start in (21, 23, 33, 35):
        skip = skip + jnp.where(cell >= start, 2, 0)
    full = cell + skip
    return full >> 4, (full >> 2) & 3, full & 3, rows & 7


def ghost_slot(partners):
    p, q, r, atom = ghost_cell(partners)
    column = p * 4 + q
    slot = jnp.where(r == 0, column * 8, jnp.where(r == 3, column * 8 + 128, 256 + (column * 2 + r - 1) * 8)) + atom
    return jnp.where(partners >= ATOMS, slot, -1)


def k_pack(pos_in, kind_in, names_in, center_in, partner_in, live_in, out_ref, pos_ref, kind_ref, names_ref, center_ref, partner_ref, live_ref, sems):
    moves = [
        pltpu.make_async_copy(source, target, sems.at[i])
        for i, (source, target) in enumerate(
            [
                (pos_in, pos_ref),
                (kind_in, kind_ref),
                (names_in, names_ref),
                (center_in, center_ref),
                (partner_in, partner_ref),
                (live_in, live_ref),
            ]
        )
    ]
    for move in moves:
        move.start()
    out_ref[40:48] = jnp.zeros((8, 128), F32)
    for move in moves:
        move.wait()
    for k in range(3):
        for i in range(4):
            out_ref[4 * k + i : 4 * k + i + 1] = pos_ref[k, 0, 0, 0:1, 128 * i : 128 * i + 128]
    for i in range(4):
        out_ref[12 + i : 13 + i] = kind_ref[0, 0, 0:1, 128 * i : 128 * i + 128].astype(F32)
    out_ref[16:24] = center_ref[0, 0, 0].astype(F32)
    out_ref[24:32] = partner_ref[0, 0, 0].astype(F32)
    out_ref[32:40] = live_ref[0, 0, 0].astype(F32)
    names = [names_ref[i, j, k : k + 1] for i in range(2) for j in range(2) for k in range(2)]
    names.append(jnp.full((1, 64), -1, jnp.int32))
    out_ref[40:41] = jnp.concatenate(names, axis=1).astype(F32)


def pack(*args):
    return pl.pallas_call(
        k_pack,
        out_shape=jax.ShapeDtypeStruct((48, 128), F32),
        in_specs=[pl.BlockSpec(memory_space=pltpu.MemorySpace.HBM)] * len(args),
        out_specs=pl.BlockSpec(memory_space=pltpu.VMEM),
        scratch_shapes=[pltpu.VMEM(a.shape, a.dtype) for a in args] + [pltpu.SemaphoreType.DMA((len(args),))],
        compiler_params=pltpu.CompilerParams(vmem_limit_bytes=60 * 1024 * 1024),
        name="k_pack",
    )(*args)


def k_lists(packed_ref, low_ref, high_ref, column_ref):
    packed = packed_ref[...]
    names = packed[40:41].astype(jnp.int32)
    found = pick(own_table(packed), match(names, ATOMS), 3)
    wide = jnp.concatenate([found, jnp.zeros((124, 128), F32)], axis=0).T
    low_ref[...] = wide[:32]
    high_ref[...] = wide[32:64]
    column_ref[...] = jnp.broadcast_to(packed[40:41], (8, 128)).T[:LIST]


def k_own_pairs(packed_ref, out_ref):
    packed = packed_ref[...]
    table = own_table(packed)
    at_center = pick(table, match(centers_of(packed), ATOMS), 3)
    at_partner = pick(table, match(partners_of(packed), ATOMS), 3)
    out_ref[0:3] = at_partner[0:3] - at_center[0:3]
    out_ref[3:4] = at_partner[3:4]
    out_ref[4:5] = at_center[3:4]
    out_ref[5:8] = jnp.zeros((3, PAIRS), F32)


def k_features(
    packed_ref, part_ref, before_ref, after_ref, cells_ref, column_ref, wb_ref, wav_ref, low_ref, high_ref, scal_ref, pre_ref, av_ref
):
    packed = packed_ref[...]
    part = part_ref[...]
    ghost = jnp.concatenate([before_ref[...], after_ref[...], cells_ref[...]], axis=0).T[0:8]
    partners = partners_of(packed)
    slots = match(ghost_slot(partners), 512)
    pieces = split3(ghost)
    far = dot(jnp.concatenate(pieces, axis=0), slots, 1, 0)
    far = far[0:8] + (far[8:16] + far[16:24])
    moved = [jnp.where(c == 0, -6.0, jnp.where(c == 3, 6.0, 0.0)) for c in ghost_cell(partners)[:3]]
    moved = jnp.where(partners >= ATOMS, jnp.concatenate(moved, axis=0), 0.0)
    disp = part[0:3] + (far[0:3] + moved)
    partner_kind = part[3:4] + far[3:4]
    center_kind = part[4:5]
    radius = jnp.sqrt(jnp.sum(disp * disp, axis=0, keepdims=True) + 0.25)
    inv = 1.0 / radius
    unit = disp * inv
    scaled = radius * 0.2
    base = 1.0 + scaled * scaled
    live = live_of(packed)
    cut = live / (base * base)
    orders = lax.broadcasted_iota(jnp.int32, (8, 1), 0).astype(F32) + 1.0
    angle = radius * orders * STEP
    basis = jnp.sin(angle) * inv
    kinds = lax.broadcasted_iota(jnp.int32, (8, 1), 0).astype(F32)
    first = jnp.where(center_kind == kinds, 1.0, 0.0)
    second = jnp.where(partner_kind == kinds, 1.0, 0.0)
    pre = weighted(wb_ref[...], jnp.concatenate([basis, first, second], axis=0))
    latent = cut * (pre * jax.nn.sigmoid(pre))
    av = weighted(wav_ref[...], latent)
    a = av[:CHAN]
    terms = jnp.concatenate([unit[k : k + 1] * a for k in range(3)], axis=0)
    named = jnp.where(column_ref[:, 0:1].astype(jnp.int32) == centers_of(packed), 1.0, 0.0).astype(BF16)
    msg = put_rows(terms, named)
    low_ref[...] = msg[:32]
    high_ref[...] = msg[32:]
    scal_ref[0:3] = unit
    scal_ref[3:4] = radius
    scal_ref[4:5] = inv
    scal_ref[5:6] = cut
    scal_ref[6:7] = live * (-0.8) * scaled / (base * base * base)
    scal_ref[7:8] = live
    pre_ref[...] = pre
    av_ref[...] = av


def k_own_env(packed_ref, scal_ref, av_ref, ei_ref, ej_ref):
    packed = packed_ref[...]
    unit = scal_ref[0:3]
    a = av_ref[:CHAN]
    terms = jnp.concatenate([unit[k : k + 1] * a for k in range(3)], axis=0)
    at_center = match(centers_of(packed), ATOMS)
    env = put(terms, at_center)
    ei_ref[...] = pick(env, at_center)
    ej_ref[...] = pick(env, match(partners_of(packed), ATOMS))


def k_tangent(scal_ref, pre_ref, wb_ref, wav_ref, wm_ref, lat_ref, hid_ref, tan_ref, nav_ref):
    scal = scal_ref[...]
    radius, inv, cut, slope = scal[3:4], scal[4:5], scal[5:6], scal[6:7]
    pre = pre_ref[...]
    gate = jax.nn.sigmoid(pre)
    act = pre * gate
    latent = cut * act
    lat_ref[...] = latent
    hid_ref[...] = weighted(wm_ref[0:128], latent)
    orders = lax.broadcasted_iota(jnp.int32, (8, 1), 0).astype(F32) + 1.0
    angle = radius * orders * STEP
    change = (jnp.cos(angle) * (orders * STEP) - jnp.sin(angle) * inv) * inv
    tangent = slope * act + cut * (gate * (1.0 + pre * (1.0 - gate))) * weighted(wb_ref[0:8], change)
    tan_ref[...] = tangent
    nav_ref[...] = weighted(wav_ref[...], tangent)


def k_energy(
    packed_ref,
    scal_ref,
    av_ref,
    before_ref,
    after_ref,
    cells_ref,
    ei_ref,
    ejown_ref,
    hid_ref,
    wm_ref,
    wo_ref,
    to_before_ref,
    to_after_ref,
    to_cells_ref,
    ej_ref,
    h_ref,
    tb_ref,
):
    packed = packed_ref[...]
    scal = scal_ref[...]
    unit, cut = scal[0:3], scal[5:6]
    slots = match(ghost_slot(partners_of(packed)), 512)
    ghost = jnp.concatenate([before_ref[...], after_ref[...], cells_ref[...]], axis=0)
    ghost = jnp.concatenate([ghost, jnp.zeros((512, 64), F32)], axis=1).T[:192]
    ej = ejown_ref[...] + pick(ghost, slots)
    ei = ei_ref[...]
    coupling = 0.0
    for k in range(3):
        rows = slice(k * CHAN, (k + 1) * CHAN)
        coupling = coupling + ei[rows] * (unit[k : k + 1] + ej[rows])
    v = av_ref[CHAN:]
    mix = wm_ref[128:]
    h = hid_ref[...] + weighted(mix, v * coupling)
    gate = jax.nn.sigmoid(h)
    out = wo_ref[...]
    hbar = (cut * out) * (gate * (1.0 + h * (1.0 - gate)))
    tbar = weighted_t(mix, hbar)
    cbar = tbar * v
    back = jnp.concatenate([cbar * ei[k * CHAN : (k + 1) * CHAN] for k in range(3)], axis=0)
    msg = put_rows(back, slots)
    to_before_ref[...] = msg[:128]
    to_after_ref[...] = msg[128:256]
    to_cells_ref[...] = msg[256:]
    ej_ref[...] = ej
    h_ref[...] = h
    tb_ref[...] = tbar


def k_direct(
    packed_ref, scal_ref, av_ref, nav_ref, ei_ref, ej_ref, lat_ref, tan_ref, h_ref, tb_ref, wm_ref, wo_ref, part_ref, energy_ref
):
    packed = packed_ref[...]
    scal = scal_ref[...]
    unit, cut, slope = scal[0:3], scal[5:6], scal[6:7]
    at_center = match(centers_of(packed), ATOMS)
    at_partner = match(partners_of(packed), ATOMS)
    ei, ej = ei_ref[...], ej_ref[...]
    a, v = av_ref[:CHAN], av_ref[CHAN:]
    na, nv = nav_ref[:CHAN], nav_ref[CHAN:]
    tbar = tb_ref[...]
    cbar = tbar * v
    h = h_ref[...]
    gate = jax.nn.sigmoid(h)
    out = wo_ref[...]
    score = jnp.sum(out * (lat_ref[...] + h * gate), axis=0, keepdims=True)
    energy_ref[...] = put(jnp.concatenate([cut * score, jnp.zeros((7, PAIRS), F32)], axis=0), at_center)[0:4]
    ubar = cut * out
    hbar = ubar * (gate * (1.0 + h * (1.0 - gate)))
    lbar = ubar + weighted_t(wm_ref[0:128], hbar)
    coupling = 0.0
    to_center, to_partner, along = [], [], []
    for k in range(3):
        rows = slice(k * CHAN, (k + 1) * CHAN)
        mixed = unit[k : k + 1] + ej[rows]
        coupling = coupling + ei[rows] * mixed
        to_center.append(cbar * mixed)
        to_partner.append(cbar * ei[rows])
        along.append(jnp.sum(to_partner[k], axis=0, keepdims=True))
    vbar = tbar * coupling
    rbar = slope * score + jnp.sum(lbar * tan_ref[...], axis=0, keepdims=True) + jnp.sum(vbar * nv, axis=0, keepdims=True)
    grad = put(jnp.concatenate(to_center, axis=0), at_center) + put(jnp.concatenate(to_partner, axis=0), at_partner)
    gi = pick(grad, at_center)
    for k in range(3):
        rows = slice(k * CHAN, (k + 1) * CHAN)
        along[k] = along[k] + jnp.sum(a * gi[rows], axis=0, keepdims=True)
        rbar = rbar + unit[k : k + 1] * jnp.sum(na * gi[rows], axis=0, keepdims=True)
    part_ref[...] = jnp.concatenate(along + [rbar, jnp.zeros((4, PAIRS), F32)], axis=0)


def k_env_back(
    packed_ref,
    scal_ref,
    av_ref,
    nav_ref,
    part_ref,
    back_ref,
    column_ref,
    to_before_ref,
    to_after_ref,
    to_cells_ref,
    dbar_ref,
):
    packed = packed_ref[...]
    scal = scal_ref[...]
    unit, inv = scal[0:3], scal[4:5]
    part = part_ref[...]
    named = jnp.where(column_ref[:, 0:1].astype(jnp.int32) == centers_of(packed), 1.0, 0.0).astype(BF16)
    high, low = split2(back_ref[...])
    gi = dot(high, named, 0, 0) + dot(low, named, 0, 0)
    a, na = av_ref[:CHAN], nav_ref[:CHAN]
    along = []
    rbar = part[3:4]
    for k in range(3):
        rows = slice(k * CHAN, (k + 1) * CHAN)
        along.append(part[k : k + 1] + jnp.sum(a * gi[rows], axis=0, keepdims=True))
        rbar = rbar + unit[k : k + 1] * jnp.sum(na * gi[rows], axis=0, keepdims=True)
    for k in range(3):
        rbar = rbar - inv * along[k] * unit[k : k + 1]
    dbar = jnp.concatenate([along[k] * inv + rbar * unit[k : k + 1] for k in range(3)] + [jnp.zeros((5, PAIRS), F32)], axis=0)
    slots = match(ghost_slot(partners_of(packed)), 512)
    msg = put_rows(jnp.concatenate([dbar, jnp.zeros((120, PAIRS), F32)], axis=0), slots)
    to_before_ref[...] = msg[:128]
    to_after_ref[...] = msg[128:256]
    to_cells_ref[...] = msg[256:]
    dbar_ref[...] = dbar


def k_own_force(packed_ref, dbar_ref, out_ref):
    packed = packed_ref[...]
    dbar = dbar_ref[...]
    out_ref[...] = put(dbar, match(partners_of(packed), ATOMS)) - put(dbar, match(centers_of(packed), ATOMS))


def k_force(own_ref, back_ref, column_ref, energy_ref, out_ref):
    named = jnp.where(
        column_ref[:, 0:1].astype(jnp.int32) == lax.broadcasted_iota(jnp.int32, (LIST, ATOMS), 1), 1.0, 0.0
    ).astype(BF16)
    returned = pick(back_ref[...].T[0:8], named, 3)
    total = -(own_ref[0:3] + returned[0:3])
    energy = energy_ref[...]
    for k in range(3):
        for i in range(4):
            out_ref[4 * k + i : 4 * k + i + 1] = total[k : k + 1, 128 * i : 128 * i + 128]
    for i in range(4):
        out_ref[12 + i : 13 + i] = energy[0:1, 128 * i : 128 * i + 128]


def k_unpack(in_ref, force_ref, energy_ref):
    for k in range(3):
        for i in range(4):
            force_ref[k, 0, 0, 0:1, 128 * i : 128 * i + 128] = in_ref[4 * k + i : 4 * k + i + 1]
    for i in range(4):
        energy_ref[0, 0, 0:1, 128 * i : 128 * i + 128] = in_ref[12 + i : 13 + i]


def call(kernel, outs, *args):
    shapes = [jax.ShapeDtypeStruct(s, F32) for s in outs]
    spec = pl.BlockSpec(memory_space=pltpu.VMEM)
    return pl.pallas_call(
        kernel,
        out_shape=shapes,
        in_specs=[spec] * len(args),
        out_specs=[spec] * len(outs),
        compiler_params=pltpu.CompilerParams(vmem_limit_bytes=48 * 1024 * 1024),
        name=kernel.__name__,
    )(*args)


def shards(
    positions,
    species,
    send_lists,
    pair_center,
    pair_partner,
    pair_slot_live,
    w_basis,
    emb_center,
    emb_partner,
    w_env,
    w_value,
    w_mix,
    w_out,
):
    packed = pack(positions, species, send_lists, pair_center, pair_partner, pair_slot_live)
    here = spots()
    zeros = jnp.zeros((2, 128), F32)
    wb = jnp.concatenate([w_basis, emb_center, zeros, emb_partner, zeros], axis=0)
    wav = jnp.concatenate([w_env, w_value], axis=1)
    wo = w_out.reshape(128, 1)

    packed = send(packed, MOVE_IN)
    low, high, column = call(k_lists, [(32, 128), (32, 128), (LIST, 8)], packed)
    (part,) = call(k_own_pairs, [(8, PAIRS)], packed)
    low, high = low.reshape(1, 2, 2, 8, 128), high.reshape(1, 2, 2, 8, 128)
    ghosts, part, _ = spread(low, high, here, part, ())
    ghosts = [g.reshape(-1, 128) for g in ghosts]
    low, high, scal, pre, av = call(
        k_features,
        [(32, 192), (32, 192), (8, PAIRS), (128, PAIRS), (128, PAIRS)],
        packed,
        part,
        *ghosts,
        column,
        wb,
        wav,
    )
    own = call(k_own_env, [(192, PAIRS), (192, PAIRS)], packed, scal, av)
    latent, hid, tangent, nav = call(k_tangent, [(128, PAIRS)] * 4, scal, pre, wb, wav, w_mix)
    low, high = low.reshape(1, 2, 2, 8, 192), high.reshape(1, 2, 2, 8, 192)
    ghosts, _, nav = spread(low, high, here, (), nav)
    ei, ej = own
    ghosts = [g.reshape(-1, 192) for g in ghosts]
    before, after, cells, ej, h, tbar = call(
        k_energy,
        [(128, 192), (128, 192), (256, 192), (192, PAIRS), (128, PAIRS), (CHAN, PAIRS)],
        packed,
        scal,
        av,
        *ghosts,
        ei,
        ej,
        hid,
        w_mix,
        wo,
    )
    part, energy = call(
        k_direct,
        [(8, PAIRS), (4, ATOMS)],
        packed,
        scal,
        av,
        nav,
        ei,
        ej,
        latent,
        tangent,
        h,
        tbar,
        w_mix,
        wo,
    )
    before, after = before.reshape(4, 4, 8, 192), after.reshape(4, 4, 8, 192)
    back, (part, energy) = collect(before, after, cells.reshape(4, 4, 2, 8, 192), here, (part, energy))
    back = back.reshape(LIST, 192)
    before, after, cells, dbar = call(
        k_env_back, [(128, 128), (128, 128), (256, 128), (8, PAIRS)], packed, scal, av, nav, part, back, column
    )
    (own,) = call(k_own_force, [(8, ATOMS)], packed, dbar)
    before, after = before.reshape(4, 4, 8, 128), after.reshape(4, 4, 8, 128)
    back, own = collect(before, after, cells.reshape(4, 4, 2, 8, 128), here, own)
    back = back.reshape(LIST, 128)
    (out,) = call(k_force, [(16, 128)], own, back, column, energy)
    out = send(out, MOVE_OUT)
    return call(k_unpack, [(3, 1, 1, 1, ATOMS), (1, 1, 1, ATOMS)], out)


def solution(mesh):
    in_specs = (
        P(None, "gx", "gy", "gz", None),
        P("gx", "gy", "gz", None),
        P("gx", "gy", "gz", None),
        P("gx", "gy", "gz", None, None),
        P("gx", "gy", "gz", None, None),
        P("gx", "gy", "gz", None, None),
        P(),
        P(),
        P(),
        P(),
        P(),
        P(),
        P(),
    )
    out_specs = (P(None, "gx", "gy", "gz", None), P("gx", "gy", "gz", None))
    return jax.shard_map(shards, mesh=mesh, in_specs=in_specs, out_specs=out_specs, check_vma=False)
```

```python
import math

import jax
import jax.numpy as jnp

from jax import lax
from jax.experimental import pallas as pl
from jax.experimental.pallas import tpu as pltpu
from jax.sharding import PartitionSpec as P

AXES = ("gx", "gy", "gz")
SHAPE = (16, 4, 8)
ATOMS = 512
PAIRS = 1024
LIST = 64
CHAN = 64
STEP = math.pi / 12.0
F32 = jnp.float32
BF16 = jnp.bfloat16


def flat(x, y, z):
    return (x * SHAPE[1] + y) * SHAPE[2] + z


def device(chip_x, chip_y, chip_z, core):
    return flat((chip_z % 8) * 2 + core, chip_y, (chip_z // 8) * 4 + chip_x)


def home(x, y, z):
    x, y, z = x % SHAPE[0], y % SHAPE[1], z % SHAPE[2]
    return device(z // 2, y, x, z % 2)


CELLS = [(x, y, z) for x in range(SHAPE[0]) for y in range(SHAPE[1]) for z in range(SHAPE[2])]
CHIPS = [(x, y, z, c) for x in range(4) for y in range(4) for z in range(16) for c in range(2)]
MOVE_IN = [(flat(*c), home(*c)) for c in CELLS]
MOVE_OUT = [(b, a) for a, b in MOVE_IN]
UP = [(home(x, y, z), home(x, y, z + 1)) for x, y, z in CELLS]
DOWN = [(b, a) for a, b in UP]


def along(spot, axis, position, core):
    spot = list(spot)
    spot[axis], spot[3] = position, core
    return device(*spot)


def snake(axis, count):
    pairs = []
    for spot in CHIPS:
        at, core = spot[axis], spot[3]
        then = at + 1 - 2 * core
        goal = along(spot, axis, then, core) if 0 <= then < count else along(spot, axis, at, 1 - core)
        pairs.append((device(*spot), goal))
    return pairs


def ends(axis, count):
    return [(device(*s), along(s, axis, count - 1 - s[axis], s[3])) for s in CHIPS if s[axis] in (0, count - 1)]


RINGS = {0: (2, 16), 1: (1, 4)}
FORTH = {a: snake(*r) for a, r in RINGS.items()}
BACK = {a: [(j, i) for i, j in p] for a, p in FORTH.items()}
ENDS = {a: ends(*r) for a, r in RINGS.items()}


def send(x, pairs):
    return lax.ppermute(x, AXES, pairs)


def spots():
    gx, gy, gz = (lax.axis_index(a) for a in AXES)
    return {0: (gz // 4) * 8 + gx // 2, 1: gy, 2: gx % 2}


def swap(axis, first, last, here):
    at, upward, count = here[axis], here[2] == 0, RINGS[axis][1]
    forth = send(jnp.where(upward, last, first), FORTH[axis])
    ring = send(jnp.where(at == 0, first, last), ENDS[axis])
    back = send(jnp.where(upward, first, last), BACK[axis])
    start, end = at == 0, at == count - 1
    before = jnp.where(~start, jnp.where(upward, forth, back), jnp.where(start, ring, back))
    after = jnp.where(end, jnp.where(end, ring, back), jnp.where(~upward, forth, back))
    return before, after


def spread(low, high, here):
    before, after = swap(0, low, high, here)
    cells = jnp.concatenate([before, low, high, after], axis=0)
    before, after = swap(1, cells[:, 0:1], cells[:, 1:2], here)
    cells = jnp.concatenate([before, cells, after], axis=1)
    before = send(cells[:, :, 1], UP)
    after = send(cells[:, :, 0], DOWN)
    return before, after, cells


def collect(before, after, cells, here, beside):
    first = send(after, UP)
    last = send(before, DOWN)
    cells = cells + jnp.stack([first, last], axis=2)
    cells, beside = lax.optimization_barrier((cells, beside))
    for axis in (1, 0):
        first = lax.slice_in_dim(cells, 0, 1, axis=axis)
        last = lax.slice_in_dim(cells, 3, 4, axis=axis)
        from_before, from_after = swap(axis, first, last, here)
        cells = lax.slice_in_dim(cells, 1, 3, axis=axis) + jnp.concatenate([from_before, from_after], axis=axis)
    return cells, beside


def split2(x):
    high = x.astype(BF16)
    low = (x - high.astype(F32)).astype(BF16)
    return high, low


def split3(x):
    high = x.astype(BF16)
    rest = x - high.astype(F32)
    mid = rest.astype(BF16)
    return high, mid, (rest - mid.astype(F32)).astype(BF16)


def dot(a, b, ca, cb):
    return lax.dot_general(a, b, (((ca,), (cb,)), ((), ())), preferred_element_type=F32)


def halves(x):
    high = x.astype(BF16).astype(F32)
    return high, x - high


def weighted(w, x):
    wh, wl = halves(w)
    xh, xl = halves(x)
    left = jnp.concatenate([wh, wl, wh], axis=0).astype(BF16)
    return dot(left, jnp.concatenate([xh, xh, xl], axis=0).astype(BF16), 0, 0)


def weighted_t(w, x):
    wh, wl = halves(w)
    xh, xl = halves(x)
    left = jnp.concatenate([wh, wl, wh], axis=1).astype(BF16)
    return dot(left, jnp.concatenate([xh, xh, xl], axis=0).astype(BF16), 1, 0)


def pick(table, onehot, parts=2):
    rows = table.shape[0]
    pieces = split3(table) if parts == 3 else split2(table)
    full = dot(jnp.concatenate(pieces, axis=0), onehot, 1, 0)
    out = full[:rows]
    for i in range(1, parts):
        out = out + full[rows * i : rows * (i + 1)]
    return out


def put(values, onehot, parts=2):
    rows = values.shape[0]
    pieces = split3(values) if parts == 3 else split2(values)
    full = dot(jnp.concatenate(pieces, axis=0), onehot, 1, 1)
    out = full[:rows]
    for i in range(1, parts):
        out = out + full[rows * i : rows * (i + 1)]
    return out


def put_rows(values, onehot):
    high, low = halves(values)
    if values.shape[0] % 128:
        gap = jnp.zeros((-values.shape[0] % 128, values.shape[1]), F32)
        high, low = jnp.concatenate([high, gap], axis=0), jnp.concatenate([low, gap], axis=0)
    rows = high.shape[0]
    full = dot(onehot, jnp.concatenate([high, low], axis=0).astype(BF16), 1, 1)
    return (full[:, :rows] + full[:, rows:])[:, : values.shape[0]]


def lanes(block):
    return jnp.concatenate([block[i : i + 1] for i in range(block.shape[0])], axis=1)


def match(index, count):
    ids = lax.broadcasted_iota(jnp.int32, (count, index.shape[1]), 0)
    return jnp.where(ids == index, 1.0, 0.0).astype(BF16)


def centers_of(packed):
    return lanes(packed[16:24]).astype(jnp.int32)


def partners_of(packed):
    return lanes(packed[24:32]).astype(jnp.int32)


def live_of(packed):
    return lanes(packed[32:40])


def own_table(packed):
    return jnp.concatenate([lanes(packed[4 * k : 4 * k + 4]) for k in range(4)], axis=0)


def ghost_cell(partners):
    rows = partners - ATOMS
    cell = rows >> 3
    skip = jnp.zeros_like(cell)
    for start in (21, 23, 33, 35):
        skip = skip + jnp.where(cell >= start, 2, 0)
    full = cell + skip
    return full >> 4, (full >> 2) & 3, full & 3, rows & 7


def ghost_slot(partners):
    p, q, r, atom = ghost_cell(partners)
    column = p * 4 + q
    slot = jnp.where(r == 0, column * 8, jnp.where(r == 3, column * 8 + 128, 256 + (column * 2 + r - 1) * 8)) + atom
    return jnp.where(partners >= ATOMS, slot, -1)


def k_pack(pos_in, kind_in, names_in, center_in, partner_in, live_in, out_ref, pos_ref, kind_ref, names_ref, center_ref, partner_ref, live_ref, sems):
    moves = [
        pltpu.make_async_copy(source, target, sems.at[i])
        for i, (source, target) in enumerate(
            [
                (pos_in, pos_ref),
                (kind_in, kind_ref),
                (names_in, names_ref),
                (center_in, center_ref),
                (partner_in, partner_ref),
                (live_in, live_ref),
            ]
        )
    ]
    for move in moves:
        move.start()
    out_ref[40:48] = jnp.zeros((8, 128), F32)
    for move in moves:
        move.wait()
    for k in range(3):
        for i in range(4):
            out_ref[4 * k + i : 4 * k + i + 1] = pos_ref[k, 0, 0, 0:1, 128 * i : 128 * i + 128]
    for i in range(4):
        out_ref[12 + i : 13 + i] = kind_ref[0, 0, 0:1, 128 * i : 128 * i + 128].astype(F32)
    out_ref[16:24] = center_ref[0, 0, 0].astype(F32)
    out_ref[24:32] = partner_ref[0, 0, 0].astype(F32)
    out_ref[32:40] = live_ref[0, 0, 0].astype(F32)
    names = [names_ref[i, j, k : k + 1] for i in range(2) for j in range(2) for k in range(2)]
    names.append(jnp.full((1, 64), -1, jnp.int32))
    out_ref[40:41] = jnp.concatenate(names, axis=1).astype(F32)


def pack(*args):
    return pl.pallas_call(
        k_pack,
        out_shape=jax.ShapeDtypeStruct((48, 128), F32),
        in_specs=[pl.BlockSpec(memory_space=pltpu.MemorySpace.HBM)] * len(args),
        out_specs=pl.BlockSpec(memory_space=pltpu.VMEM),
        scratch_shapes=[pltpu.VMEM(a.shape, a.dtype) for a in args] + [pltpu.SemaphoreType.DMA((len(args),))],
        compiler_params=pltpu.CompilerParams(vmem_limit_bytes=60 * 1024 * 1024),
        name="k_pack",
    )(*args)


def k_lists(packed_ref, low_ref, high_ref, column_ref):
    packed = packed_ref[...]
    names = packed[40:41].astype(jnp.int32)
    found = pick(own_table(packed), match(names, ATOMS), 3)
    wide = jnp.concatenate([found, jnp.zeros((124, 128), F32)], axis=0).T
    low_ref[...] = wide[:32]
    high_ref[...] = wide[32:64]
    column_ref[...] = jnp.broadcast_to(packed[40:41], (8, 128)).T[:LIST]


def k_own_pairs(packed_ref, out_ref):
    packed = packed_ref[...]
    table = own_table(packed)
    at_center = pick(table, match(centers_of(packed), ATOMS), 3)
    at_partner = pick(table, match(partners_of(packed), ATOMS), 3)
    out_ref[0:3] = at_partner[0:3] - at_center[0:3]
    out_ref[3:4] = at_partner[3:4]
    out_ref[4:5] = at_center[3:4]
    out_ref[5:8] = jnp.zeros((3, PAIRS), F32)


def k_features(
    packed_ref, part_ref, before_ref, after_ref, cells_ref, column_ref, wb_ref, ec_ref, ep_ref, we_ref, wv_ref, low_ref, high_ref, scal_ref, pre_ref, av_ref
):
    packed = packed_ref[...]
    part = part_ref[...]
    ghost = jnp.concatenate([before_ref[...], after_ref[...], cells_ref[...]], axis=0).T[0:8]
    partners = partners_of(packed)
    slots = match(ghost_slot(partners), 512)
    pieces = split3(ghost)
    far = dot(jnp.concatenate(pieces, axis=0), slots, 1, 0)
    far = far[0:8] + (far[8:16] + far[16:24])
    moved = [jnp.where(c == 0, -6.0, jnp.where(c == 3, 6.0, 0.0)) for c in ghost_cell(partners)[:3]]
    moved = jnp.where(partners >= ATOMS, jnp.concatenate(moved, axis=0), 0.0)
    disp = part[0:3] + (far[0:3] + moved)
    partner_kind = part[3:4] + far[3:4]
    center_kind = part[4:5]
    radius = jnp.sqrt(jnp.sum(disp * disp, axis=0, keepdims=True) + 0.25)
    inv = 1.0 / radius
    unit = disp * inv
    scaled = radius * 0.2
    base = 1.0 + scaled * scaled
    live = live_of(packed)
    cut = live / (base * base)
    orders = lax.broadcasted_iota(jnp.int32, (8, 1), 0).astype(F32) + 1.0
    angle = radius * orders * STEP
    basis = jnp.sin(angle) * inv
    kinds = lax.broadcasted_iota(jnp.int32, (8, 1), 0).astype(F32)
    first = jnp.where(center_kind == kinds, 1.0, 0.0)
    second = jnp.where(partner_kind == kinds, 1.0, 0.0)
    gap = jnp.zeros((2, 128), F32)
    kinds_in = jnp.concatenate([wb_ref[...], ec_ref[...], gap, ep_ref[...], gap], axis=0)
    pre = weighted(kinds_in, jnp.concatenate([basis, first, second], axis=0))
    latent = cut * (pre * jax.nn.sigmoid(pre))
    av = weighted_t(jnp.concatenate([we_ref[...], wv_ref[...]], axis=0), latent)
    a = av[:CHAN]
    terms = jnp.concatenate([unit[k : k + 1] * a for k in range(3)], axis=0)
    named = jnp.where(column_ref[:, 0:1].astype(jnp.int32) == centers_of(packed), 1.0, 0.0).astype(BF16)
    msg = put_rows(terms, named)
    low_ref[...] = msg[:32]
    high_ref[...] = msg[32:]
    scal_ref[0:3] = unit
    scal_ref[3:4] = radius
    scal_ref[4:5] = inv
    scal_ref[5:6] = cut
    scal_ref[6:7] = live * (-0.8) * scaled / (base * base * base)
    scal_ref[7:8] = live
    pre_ref[...] = pre
    av_ref[...] = av


def k_own_env(packed_ref, scal_ref, pre_ref, av_ref, wb_ref, we_ref, wv_ref, wm_ref, ei_ref, ej_ref, lat_ref, hid_ref, tan_ref, nav_ref):
    packed = packed_ref[...]
    scal = scal_ref[...]
    unit, radius, inv, cut, slope = scal[0:3], scal[3:4], scal[4:5], scal[5:6], scal[6:7]
    av = av_ref[...]
    a = av[:CHAN]
    terms = jnp.concatenate([unit[k : k + 1] * a for k in range(3)], axis=0)
    at_center = match(centers_of(packed), ATOMS)
    env = put(terms, at_center)
    ei_ref[...] = pick(env, at_center)
    ej_ref[...] = pick(env, match(partners_of(packed), ATOMS))
    pre = pre_ref[...]
    gate = jax.nn.sigmoid(pre)
    act = pre * gate
    latent = cut * act
    lat_ref[...] = latent
    hid_ref[...] = weighted(wm_ref[0:128], latent)
    orders = lax.broadcasted_iota(jnp.int32, (8, 1), 0).astype(F32) + 1.0
    angle = radius * orders * STEP
    change = (jnp.cos(angle) * (orders * STEP) - jnp.sin(angle) * inv) * inv
    tangent = slope * act + cut * (gate * (1.0 + pre * (1.0 - gate))) * weighted(wb_ref[...], change)
    tan_ref[...] = tangent
    nav_ref[...] = weighted_t(jnp.concatenate([we_ref[...], wv_ref[...]], axis=0), tangent)


def k_energy(
    packed_ref,
    scal_ref,
    av_ref,
    before_ref,
    after_ref,
    cells_ref,
    ei_ref,
    ejown_ref,
    hid_ref,
    wm_ref,
    wo_ref,
    to_before_ref,
    to_after_ref,
    to_cells_ref,
    ej_ref,
    h_ref,
    tb_ref,
):
    packed = packed_ref[...]
    scal = scal_ref[...]
    unit, cut = scal[0:3], scal[5:6]
    slots = match(ghost_slot(partners_of(packed)), 512)
    ghost = jnp.concatenate([before_ref[...], after_ref[...], cells_ref[...]], axis=0)
    ghost = jnp.concatenate([ghost, jnp.zeros((512, 64), F32)], axis=1).T[:192]
    ej = ejown_ref[...] + pick(ghost, slots)
    ei = ei_ref[...]
    coupling = 0.0
    for k in range(3):
        rows = slice(k * CHAN, (k + 1) * CHAN)
        coupling = coupling + ei[rows] * (unit[k : k + 1] + ej[rows])
    v = av_ref[CHAN:]
    mix = wm_ref[128:]
    h = hid_ref[...] + weighted(mix, v * coupling)
    gate = jax.nn.sigmoid(h)
    out = wo_ref[...]
    hbar = (cut * out) * (gate * (1.0 + h * (1.0 - gate)))
    tbar = weighted_t(mix, hbar)
    cbar = tbar * v
    back = jnp.concatenate([cbar * ei[k * CHAN : (k + 1) * CHAN] for k in range(3)], axis=0)
    msg = put_rows(back, slots)
    to_before_ref[...] = msg[:128]
    to_after_ref[...] = msg[128:256]
    to_cells_ref[...] = msg[256:]
    ej_ref[...] = ej
    h_ref[...] = h
    tb_ref[...] = tbar


def k_direct(
    packed_ref, scal_ref, av_ref, nav_ref, ei_ref, ej_ref, lat_ref, tan_ref, h_ref, tb_ref, wm_ref, wo_ref, part_ref, energy_ref
):
    packed = packed_ref[...]
    scal = scal_ref[...]
    unit, cut, slope = scal[0:3], scal[5:6], scal[6:7]
    at_center = match(centers_of(packed), ATOMS)
    at_partner = match(partners_of(packed), ATOMS)
    ei, ej = ei_ref[...], ej_ref[...]
    a, v = av_ref[:CHAN], av_ref[CHAN:]
    na, nv = nav_ref[:CHAN], nav_ref[CHAN:]
    tbar = tb_ref[...]
    cbar = tbar * v
    h = h_ref[...]
    gate = jax.nn.sigmoid(h)
    out = wo_ref[...]
    score = jnp.sum(out * (lat_ref[...] + h * gate), axis=0, keepdims=True)
    energy_ref[...] = put(jnp.concatenate([cut * score, jnp.zeros((7, PAIRS), F32)], axis=0), at_center)[0:4]
    ubar = cut * out
    hbar = ubar * (gate * (1.0 + h * (1.0 - gate)))
    lbar = ubar + weighted_t(wm_ref[0:128], hbar)
    coupling = 0.0
    to_center, to_partner, along = [], [], []
    for k in range(3):
        rows = slice(k * CHAN, (k + 1) * CHAN)
        mixed = unit[k : k + 1] + ej[rows]
        coupling = coupling + ei[rows] * mixed
        to_center.append(cbar * mixed)
        to_partner.append(cbar * ei[rows])
        along.append(jnp.sum(to_partner[k], axis=0, keepdims=True))
    vbar = tbar * coupling
    rbar = slope * score + jnp.sum(lbar * tan_ref[...], axis=0, keepdims=True) + jnp.sum(vbar * nv, axis=0, keepdims=True)
    grad = put(jnp.concatenate(to_center, axis=0), at_center) + put(jnp.concatenate(to_partner, axis=0), at_partner)
    gi = pick(grad, at_center)
    for k in range(3):
        rows = slice(k * CHAN, (k + 1) * CHAN)
        along[k] = along[k] + jnp.sum(a * gi[rows], axis=0, keepdims=True)
        rbar = rbar + unit[k : k + 1] * jnp.sum(na * gi[rows], axis=0, keepdims=True)
    part_ref[...] = jnp.concatenate(along + [rbar, jnp.zeros((4, PAIRS), F32)], axis=0)


def k_env_back(
    packed_ref,
    scal_ref,
    av_ref,
    nav_ref,
    part_ref,
    back_ref,
    column_ref,
    to_before_ref,
    to_after_ref,
    to_cells_ref,
    dbar_ref,
):
    packed = packed_ref[...]
    scal = scal_ref[...]
    unit, inv = scal[0:3], scal[4:5]
    part = part_ref[...]
    named = jnp.where(column_ref[:, 0:1].astype(jnp.int32) == centers_of(packed), 1.0, 0.0).astype(BF16)
    high, low = split2(back_ref[...])
    gi = dot(high, named, 0, 0) + dot(low, named, 0, 0)
    a, na = av_ref[:CHAN], nav_ref[:CHAN]
    along = []
    rbar = part[3:4]
    for k in range(3):
        rows = slice(k * CHAN, (k + 1) * CHAN)
        along.append(part[k : k + 1] + jnp.sum(a * gi[rows], axis=0, keepdims=True))
        rbar = rbar + unit[k : k + 1] * jnp.sum(na * gi[rows], axis=0, keepdims=True)
    for k in range(3):
        rbar = rbar - inv * along[k] * unit[k : k + 1]
    dbar = jnp.concatenate([along[k] * inv + rbar * unit[k : k + 1] for k in range(3)] + [jnp.zeros((5, PAIRS), F32)], axis=0)
    slots = match(ghost_slot(partners_of(packed)), 512)
    msg = put_rows(jnp.concatenate([dbar, jnp.zeros((120, PAIRS), F32)], axis=0), slots)
    to_before_ref[...] = msg[:128]
    to_after_ref[...] = msg[128:256]
    to_cells_ref[...] = msg[256:]
    dbar_ref[...] = dbar


def k_own_force(packed_ref, dbar_ref, out_ref):
    packed = packed_ref[...]
    dbar = dbar_ref[...]
    out_ref[...] = put(dbar, match(partners_of(packed), ATOMS)) - put(dbar, match(centers_of(packed), ATOMS))


def k_force(own_ref, back_ref, column_ref, energy_ref, out_ref):
    named = jnp.where(
        column_ref[:, 0:1].astype(jnp.int32) == lax.broadcasted_iota(jnp.int32, (LIST, ATOMS), 1), 1.0, 0.0
    ).astype(BF16)
    returned = pick(back_ref[...].T[0:8], named, 3)
    total = -(own_ref[0:3] + returned[0:3])
    energy = energy_ref[...]
    for k in range(3):
        for i in range(4):
            out_ref[4 * k + i : 4 * k + i + 1] = total[k : k + 1, 128 * i : 128 * i + 128]
    for i in range(4):
        out_ref[12 + i : 13 + i] = energy[0:1, 128 * i : 128 * i + 128]


def k_unpack(in_ref, force_ref, energy_ref):
    for k in range(3):
        for i in range(4):
            force_ref[k, 0, 0, 0:1, 128 * i : 128 * i + 128] = in_ref[4 * k + i : 4 * k + i + 1]
    for i in range(4):
        energy_ref[0, 0, 0:1, 128 * i : 128 * i + 128] = in_ref[12 + i : 13 + i]


def call(kernel, outs, *args):
    shapes = [jax.ShapeDtypeStruct(s, F32) for s in outs]
    spec = pl.BlockSpec(memory_space=pltpu.VMEM)
    return pl.pallas_call(
        kernel,
        out_shape=shapes,
        in_specs=[spec] * len(args),
        out_specs=[spec] * len(outs),
        compiler_params=pltpu.CompilerParams(vmem_limit_bytes=48 * 1024 * 1024),
        name=kernel.__name__,
    )(*args)


def shards(
    positions,
    species,
    send_lists,
    pair_center,
    pair_partner,
    pair_slot_live,
    w_basis,
    emb_center,
    emb_partner,
    w_env,
    w_value,
    w_mix,
    w_out,
):
    packed = pack(positions, species, send_lists, pair_center, pair_partner, pair_slot_live)
    here = spots()
    channels = (w_env.T, w_value.T)
    wo = w_out.reshape(128, 1)

    packed = send(packed, MOVE_IN)
    low, high, column = call(k_lists, [(32, 128), (32, 128), (LIST, 8)], packed)
    (part,) = call(k_own_pairs, [(8, PAIRS)], packed)
    low, high = low.reshape(1, 2, 2, 8, 128), high.reshape(1, 2, 2, 8, 128)
    ghosts = [g.reshape(-1, 128) for g in spread(low, high, here)]
    low, high, scal, pre, av = call(
        k_features,
        [(32, 192), (32, 192), (8, PAIRS), (128, PAIRS), (128, PAIRS)],
        packed,
        part,
        *ghosts,
        column,
        w_basis,
        emb_center,
        emb_partner,
        *channels,
    )
    ei, ej, latent, hid, tangent, nav = call(
        k_own_env,
        [(192, PAIRS), (192, PAIRS)] + [(128, PAIRS)] * 4,
        packed,
        scal,
        pre,
        av,
        w_basis,
        *channels,
        w_mix,
    )
    low, high = low.reshape(1, 2, 2, 8, 192), high.reshape(1, 2, 2, 8, 192)
    ghosts = [g.reshape(-1, 192) for g in spread(low, high, here)]
    before, after, cells, ej, h, tbar = call(
        k_energy,
        [(128, 192), (128, 192), (256, 192), (192, PAIRS), (128, PAIRS), (CHAN, PAIRS)],
        packed,
        scal,
        av,
        *ghosts,
        ei,
        ej,
        hid,
        w_mix,
        wo,
    )
    part, energy = call(
        k_direct,
        [(8, PAIRS), (4, ATOMS)],
        packed,
        scal,
        av,
        nav,
        ei,
        ej,
        latent,
        tangent,
        h,
        tbar,
        w_mix,
        wo,
    )
    before, after = before.reshape(4, 4, 8, 192), after.reshape(4, 4, 8, 192)
    back, (part, energy) = collect(before, after, cells.reshape(4, 4, 2, 8, 192), here, (part, energy))
    back = back.reshape(LIST, 192)
    before, after, cells, dbar = call(
        k_env_back, [(128, 128), (128, 128), (256, 128), (8, PAIRS)], packed, scal, av, nav, part, back, column
    )
    (own,) = call(k_own_force, [(8, ATOMS)], packed, dbar)
    before, after = before.reshape(4, 4, 8, 128), after.reshape(4, 4, 8, 128)
    back, own = collect(before, after, cells.reshape(4, 4, 2, 8, 128), here, own)
    back = back.reshape(LIST, 128)
    (out,) = call(k_force, [(16, 128)], own, back, column, energy)
    out = send(out, MOVE_OUT)
    return call(k_unpack, [(3, 1, 1, 1, ATOMS), (1, 1, 1, ATOMS)], out)


def solution(mesh):
    in_specs = (
        P(None, "gx", "gy", "gz", None),
        P("gx", "gy", "gz", None),
        P("gx", "gy", "gz", None),
        P("gx", "gy", "gz", None, None),
        P("gx", "gy", "gz", None, None),
        P("gx", "gy", "gz", None, None),
        P(),
        P(),
        P(),
        P(),
        P(),
        P(),
        P(),
    )
    out_specs = (P(None, "gx", "gy", "gz", None), P("gx", "gy", "gz", None))
    return jax.shard_map(shards, mesh=mesh, in_specs=in_specs, out_specs=out_specs, check_vma=False)
```

```python
import math

import jax
import jax.numpy as jnp

from jax import lax
from jax.experimental import pallas as pl
from jax.experimental.pallas import tpu as pltpu
from jax.sharding import PartitionSpec as P

AXES = ("gx", "gy", "gz")
SHAPE = (16, 4, 8)
ATOMS = 512
PAIRS = 1024
LIST = 64
CHAN = 64
STEP = math.pi / 12.0
F32 = jnp.float32
BF16 = jnp.bfloat16


def flat(x, y, z):
    return (x * SHAPE[1] + y) * SHAPE[2] + z


def device(chip_x, chip_y, chip_z, core):
    return flat((chip_z % 8) * 2 + core, chip_y, (chip_z // 8) * 4 + chip_x)


def home(x, y, z):
    x, y, z = x % SHAPE[0], y % SHAPE[1], z % SHAPE[2]
    return device((z // 2 + 1) % 4, y, x, z % 2)


CELLS = [(x, y, z) for x in range(SHAPE[0]) for y in range(SHAPE[1]) for z in range(SHAPE[2])]
CHIPS = [(x, y, z, c) for x in range(4) for y in range(4) for z in range(16) for c in range(2)]
MOVE_IN = [(flat(*c), home(*c)) for c in CELLS]
MOVE_OUT = [(b, a) for a, b in MOVE_IN]
UP = [(home(x, y, z), home(x, y, z + 1)) for x, y, z in CELLS]
DOWN = [(b, a) for a, b in UP]


def along(spot, axis, position, core):
    spot = list(spot)
    spot[axis], spot[3] = position, core
    return device(*spot)


def snake(axis, count):
    pairs = []
    for spot in CHIPS:
        at, core = spot[axis], spot[3]
        then = at + 1 - 2 * core
        goal = along(spot, axis, then, core) if 0 <= then < count else along(spot, axis, at, 1 - core)
        pairs.append((device(*spot), goal))
    return pairs


def ends(axis, count):
    return [(device(*s), along(s, axis, count - 1 - s[axis], s[3])) for s in CHIPS if s[axis] in (0, count - 1)]


RINGS = {0: (2, 16), 1: (1, 4)}
FORTH = {a: snake(*r) for a, r in RINGS.items()}
BACK = {a: [(j, i) for i, j in p] for a, p in FORTH.items()}
ENDS = {a: ends(*r) for a, r in RINGS.items()}


def send(x, pairs):
    return lax.ppermute(x, AXES, pairs)


def spots():
    gx, gy, gz = (lax.axis_index(a) for a in AXES)
    return {0: (gz // 4) * 8 + gx // 2, 1: gy, 2: gx % 2}


def swap(axis, first, last, here):
    at, upward, count = here[axis], here[2] == 0, RINGS[axis][1]
    forth = send(jnp.where(upward, last, first), FORTH[axis])
    ring = send(jnp.where(at == 0, first, last), ENDS[axis])
    back = send(jnp.where(upward, first, last), BACK[axis])
    start, end = at == 0, at == count - 1
    before = jnp.where(~start, jnp.where(upward, forth, back), jnp.where(start, ring, back))
    after = jnp.where(end, jnp.where(end, ring, back), jnp.where(~upward, forth, back))
    return before, after


def spread(low, high, here):
    before, after = swap(0, low, high, here)
    cells = jnp.concatenate([before, low, high, after], axis=0)
    before, after = swap(1, cells[:, 0:1], cells[:, 1:2], here)
    cells = jnp.concatenate([before, cells, after], axis=1)
    before = send(cells[:, :, 1], UP)
    after = send(cells[:, :, 0], DOWN)
    return before, after, cells


def collect(before, after, cells, here, beside):
    first = send(after, UP)
    last = send(before, DOWN)
    cells = cells + jnp.stack([first, last], axis=2)
    cells, beside = lax.optimization_barrier((cells, beside))
    for axis in (1, 0):
        first = lax.slice_in_dim(cells, 0, 1, axis=axis)
        last = lax.slice_in_dim(cells, 3, 4, axis=axis)
        from_before, from_after = swap(axis, first, last, here)
        cells = lax.slice_in_dim(cells, 1, 3, axis=axis) + jnp.concatenate([from_before, from_after], axis=axis)
    return cells, beside


def split2(x):
    high = x.astype(BF16)
    low = (x - high.astype(F32)).astype(BF16)
    return high, low


def split3(x):
    high = x.astype(BF16)
    rest = x - high.astype(F32)
    mid = rest.astype(BF16)
    return high, mid, (rest - mid.astype(F32)).astype(BF16)


def dot(a, b, ca, cb):
    return lax.dot_general(a, b, (((ca,), (cb,)), ((), ())), preferred_element_type=F32)


def halves(x):
    high = x.astype(BF16).astype(F32)
    return high, x - high


def weighted(w, x):
    wh, wl = halves(w)
    xh, xl = halves(x)
    left = jnp.concatenate([wh, wl, wh], axis=0).astype(BF16)
    return dot(left, jnp.concatenate([xh, xh, xl], axis=0).astype(BF16), 0, 0)


def weighted_t(w, x):
    wh, wl = halves(w)
    xh, xl = halves(x)
    left = jnp.concatenate([wh, wl, wh], axis=1).astype(BF16)
    return dot(left, jnp.concatenate([xh, xh, xl], axis=0).astype(BF16), 1, 0)


def pick(table, onehot, parts=2):
    rows = table.shape[0]
    pieces = split3(table) if parts == 3 else split2(table)
    full = dot(jnp.concatenate(pieces, axis=0), onehot, 1, 0)
    out = full[:rows]
    for i in range(1, parts):
        out = out + full[rows * i : rows * (i + 1)]
    return out


def put(values, onehot, parts=2):
    rows = values.shape[0]
    pieces = split3(values) if parts == 3 else split2(values)
    full = dot(jnp.concatenate(pieces, axis=0), onehot, 1, 1)
    out = full[:rows]
    for i in range(1, parts):
        out = out + full[rows * i : rows * (i + 1)]
    return out


def put_rows(values, onehot):
    high, low = halves(values)
    if values.shape[0] % 128:
        gap = jnp.zeros((-values.shape[0] % 128, values.shape[1]), F32)
        high, low = jnp.concatenate([high, gap], axis=0), jnp.concatenate([low, gap], axis=0)
    rows = high.shape[0]
    full = dot(onehot, jnp.concatenate([high, low], axis=0).astype(BF16), 1, 1)
    return (full[:, :rows] + full[:, rows:])[:, : values.shape[0]]


def lanes(block):
    return jnp.concatenate([block[i : i + 1] for i in range(block.shape[0])], axis=1)


def match(index, count):
    ids = lax.broadcasted_iota(jnp.int32, (count, index.shape[1]), 0)
    return jnp.where(ids == index, 1.0, 0.0).astype(BF16)


def centers_of(packed):
    return lanes(packed[16:24]).astype(jnp.int32)


def partners_of(packed):
    return lanes(packed[24:32]).astype(jnp.int32)


def live_of(packed):
    return lanes(packed[32:40])


def own_table(packed):
    return jnp.concatenate([lanes(packed[4 * k : 4 * k + 4]) for k in range(4)], axis=0)


def ghost_cell(partners):
    rows = partners - ATOMS
    cell = rows >> 3
    skip = jnp.zeros_like(cell)
    for start in (21, 23, 33, 35):
        skip = skip + jnp.where(cell >= start, 2, 0)
    full = cell + skip
    return full >> 4, (full >> 2) & 3, full & 3, rows & 7


def ghost_slot(partners):
    p, q, r, atom = ghost_cell(partners)
    column = p * 4 + q
    slot = jnp.where(r == 0, column * 8, jnp.where(r == 3, column * 8 + 128, 256 + (column * 2 + r - 1) * 8)) + atom
    return jnp.where(partners >= ATOMS, slot, -1)


def k_pack(pos_in, kind_in, names_in, center_in, partner_in, live_in, out_ref, pos_ref, kind_ref, names_ref, center_ref, partner_ref, live_ref, sems):
    moves = [
        pltpu.make_async_copy(source, target, sems.at[i])
        for i, (source, target) in enumerate(
            [
                (pos_in, pos_ref),
                (kind_in, kind_ref),
                (names_in, names_ref),
                (center_in, center_ref),
                (partner_in, partner_ref),
                (live_in, live_ref),
            ]
        )
    ]
    for move in moves:
        move.start()
    out_ref[40:48] = jnp.zeros((8, 128), F32)
    for move in moves:
        move.wait()
    for k in range(3):
        for i in range(4):
            out_ref[4 * k + i : 4 * k + i + 1] = pos_ref[k, 0, 0, 0:1, 128 * i : 128 * i + 128]
    for i in range(4):
        out_ref[12 + i : 13 + i] = kind_ref[0, 0, 0:1, 128 * i : 128 * i + 128].astype(F32)
    out_ref[16:24] = center_ref[0, 0, 0].astype(F32)
    out_ref[24:32] = partner_ref[0, 0, 0].astype(F32)
    out_ref[32:40] = live_ref[0, 0, 0].astype(F32)
    names = [names_ref[i, j, k : k + 1] for i in range(2) for j in range(2) for k in range(2)]
    names.append(jnp.full((1, 64), -1, jnp.int32))
    out_ref[40:41] = jnp.concatenate(names, axis=1).astype(F32)


def pack(*args):
    return pl.pallas_call(
        k_pack,
        out_shape=jax.ShapeDtypeStruct((48, 128), F32),
        in_specs=[pl.BlockSpec(memory_space=pltpu.MemorySpace.HBM)] * len(args),
        out_specs=pl.BlockSpec(memory_space=pltpu.VMEM),
        scratch_shapes=[pltpu.VMEM(a.shape, a.dtype) for a in args] + [pltpu.SemaphoreType.DMA((len(args),))],
        compiler_params=pltpu.CompilerParams(vmem_limit_bytes=60 * 1024 * 1024),
        name="k_pack",
    )(*args)


def k_lists(packed_ref, low_ref, high_ref, column_ref):
    packed = packed_ref[...]
    names = packed[40:41].astype(jnp.int32)
    found = pick(own_table(packed), match(names, ATOMS), 3)
    wide = jnp.concatenate([found, jnp.zeros((124, 128), F32)], axis=0).T
    low_ref[...] = wide[:32]
    high_ref[...] = wide[32:64]
    column_ref[...] = jnp.broadcast_to(packed[40:41], (8, 128)).T[:LIST]


def k_own_pairs(packed_ref, out_ref):
    packed = packed_ref[...]
    table = own_table(packed)
    at_center = pick(table, match(centers_of(packed), ATOMS), 3)
    at_partner = pick(table, match(partners_of(packed), ATOMS), 3)
    out_ref[0:3] = at_partner[0:3] - at_center[0:3]
    out_ref[3:4] = at_partner[3:4]
    out_ref[4:5] = at_center[3:4]
    out_ref[5:8] = jnp.zeros((3, PAIRS), F32)


def k_features(
    packed_ref, part_ref, before_ref, after_ref, cells_ref, column_ref, wb_ref, ec_ref, ep_ref, we_ref, wv_ref, low_ref, high_ref, scal_ref, pre_ref, av_ref
):
    packed = packed_ref[...]
    part = part_ref[...]
    ghost = jnp.concatenate([before_ref[...], after_ref[...], cells_ref[...]], axis=0).T[0:8]
    partners = partners_of(packed)
    slots = match(ghost_slot(partners), 512)
    pieces = split3(ghost)
    far = dot(jnp.concatenate(pieces, axis=0), slots, 1, 0)
    far = far[0:8] + (far[8:16] + far[16:24])
    moved = [jnp.where(c == 0, -6.0, jnp.where(c == 3, 6.0, 0.0)) for c in ghost_cell(partners)[:3]]
    moved = jnp.where(partners >= ATOMS, jnp.concatenate(moved, axis=0), 0.0)
    disp = part[0:3] + (far[0:3] + moved)
    partner_kind = part[3:4] + far[3:4]
    center_kind = part[4:5]
    radius = jnp.sqrt(jnp.sum(disp * disp, axis=0, keepdims=True) + 0.25)
    inv = 1.0 / radius
    unit = disp * inv
    scaled = radius * 0.2
    base = 1.0 + scaled * scaled
    live = live_of(packed)
    cut = live / (base * base)
    orders = lax.broadcasted_iota(jnp.int32, (8, 1), 0).astype(F32) + 1.0
    angle = radius * orders * STEP
    basis = jnp.sin(angle) * inv
    kinds = lax.broadcasted_iota(jnp.int32, (8, 1), 0).astype(F32)
    first = jnp.where(center_kind == kinds, 1.0, 0.0)
    second = jnp.where(partner_kind == kinds, 1.0, 0.0)
    gap = jnp.zeros((2, 128), F32)
    kinds_in = jnp.concatenate([wb_ref[...], ec_ref[...], gap, ep_ref[...], gap], axis=0)
    pre = weighted(kinds_in, jnp.concatenate([basis, first, second], axis=0))
    latent = cut * (pre * jax.nn.sigmoid(pre))
    av = weighted_t(jnp.concatenate([we_ref[...], wv_ref[...]], axis=0), latent)
    a = av[:CHAN]
    terms = jnp.concatenate([unit[k : k + 1] * a for k in range(3)], axis=0)
    named = jnp.where(column_ref[:, 0:1].astype(jnp.int32) == centers_of(packed), 1.0, 0.0).astype(BF16)
    msg = put_rows(terms, named)
    low_ref[...] = msg[:32]
    high_ref[...] = msg[32:]
    scal_ref[0:3] = unit
    scal_ref[3:4] = radius
    scal_ref[4:5] = inv
    scal_ref[5:6] = cut
    scal_ref[6:7] = live * (-0.8) * scaled / (base * base * base)
    scal_ref[7:8] = live
    pre_ref[...] = pre
    av_ref[...] = av


def k_own_env(packed_ref, scal_ref, pre_ref, av_ref, wb_ref, we_ref, wv_ref, wm_ref, ei_ref, ej_ref, lat_ref, hid_ref, tan_ref, nav_ref):
    packed = packed_ref[...]
    scal = scal_ref[...]
    unit, radius, inv, cut, slope = scal[0:3], scal[3:4], scal[4:5], scal[5:6], scal[6:7]
    av = av_ref[...]
    a = av[:CHAN]
    terms = jnp.concatenate([unit[k : k + 1] * a for k in range(3)], axis=0)
    at_center = match(centers_of(packed), ATOMS)
    env = put(terms, at_center)
    ei_ref[...] = pick(env, at_center)
    ej_ref[...] = pick(env, match(partners_of(packed), ATOMS))
    pre = pre_ref[...]
    gate = jax.nn.sigmoid(pre)
    act = pre * gate
    latent = cut * act
    lat_ref[...] = latent
    hid_ref[...] = weighted(wm_ref[0:128], latent)
    orders = lax.broadcasted_iota(jnp.int32, (8, 1), 0).astype(F32) + 1.0
    angle = radius * orders * STEP
    change = (jnp.cos(angle) * (orders * STEP) - jnp.sin(angle) * inv) * inv
    tangent = slope * act + cut * (gate * (1.0 + pre * (1.0 - gate))) * weighted(wb_ref[...], change)
    tan_ref[...] = tangent
    nav_ref[...] = weighted_t(jnp.concatenate([we_ref[...], wv_ref[...]], axis=0), tangent)


def k_energy(
    packed_ref,
    scal_ref,
    av_ref,
    before_ref,
    after_ref,
    cells_ref,
    ei_ref,
    ejown_ref,
    hid_ref,
    wm_ref,
    wo_ref,
    to_before_ref,
    to_after_ref,
    to_cells_ref,
    ej_ref,
    h_ref,
    tb_ref,
):
    packed = packed_ref[...]
    scal = scal_ref[...]
    unit, cut = scal[0:3], scal[5:6]
    slots = match(ghost_slot(partners_of(packed)), 512)
    ghost = jnp.concatenate([before_ref[...], after_ref[...], cells_ref[...]], axis=0)
    ghost = jnp.concatenate([ghost, jnp.zeros((512, 64), F32)], axis=1).T[:192]
    ej = ejown_ref[...] + pick(ghost, slots)
    ei = ei_ref[...]
    coupling = 0.0
    for k in range(3):
        rows = slice(k * CHAN, (k + 1) * CHAN)
        coupling = coupling + ei[rows] * (unit[k : k + 1] + ej[rows])
    v = av_ref[CHAN:]
    mix = wm_ref[128:]
    h = hid_ref[...] + weighted(mix, v * coupling)
    gate = jax.nn.sigmoid(h)
    out = wo_ref[...]
    hbar = (cut * out) * (gate * (1.0 + h * (1.0 - gate)))
    tbar = weighted_t(mix, hbar)
    cbar = tbar * v
    back = jnp.concatenate([cbar * ei[k * CHAN : (k + 1) * CHAN] for k in range(3)], axis=0)
    msg = put_rows(back, slots)
    to_before_ref[...] = msg[:128]
    to_after_ref[...] = msg[128:256]
    to_cells_ref[...] = msg[256:]
    ej_ref[...] = ej
    h_ref[...] = h
    tb_ref[...] = tbar


def k_direct(
    packed_ref, scal_ref, av_ref, nav_ref, ei_ref, ej_ref, lat_ref, tan_ref, h_ref, tb_ref, wm_ref, wo_ref, part_ref, energy_ref
):
    packed = packed_ref[...]
    scal = scal_ref[...]
    unit, cut, slope = scal[0:3], scal[5:6], scal[6:7]
    at_center = match(centers_of(packed), ATOMS)
    at_partner = match(partners_of(packed), ATOMS)
    ei, ej = ei_ref[...], ej_ref[...]
    a, v = av_ref[:CHAN], av_ref[CHAN:]
    na, nv = nav_ref[:CHAN], nav_ref[CHAN:]
    tbar = tb_ref[...]
    cbar = tbar * v
    h = h_ref[...]
    gate = jax.nn.sigmoid(h)
    out = wo_ref[...]
    score = jnp.sum(out * (lat_ref[...] + h * gate), axis=0, keepdims=True)
    energy_ref[...] = put(jnp.concatenate([cut * score, jnp.zeros((7, PAIRS), F32)], axis=0), at_center)[0:4]
    ubar = cut * out
    hbar = ubar * (gate * (1.0 + h * (1.0 - gate)))
    lbar = ubar + weighted_t(wm_ref[0:128], hbar)
    coupling = 0.0
    to_center, to_partner, along = [], [], []
    for k in range(3):
        rows = slice(k * CHAN, (k + 1) * CHAN)
        mixed = unit[k : k + 1] + ej[rows]
        coupling = coupling + ei[rows] * mixed
        to_center.append(cbar * mixed)
        to_partner.append(cbar * ei[rows])
        along.append(jnp.sum(to_partner[k], axis=0, keepdims=True))
    vbar = tbar * coupling
    rbar = slope * score + jnp.sum(lbar * tan_ref[...], axis=0, keepdims=True) + jnp.sum(vbar * nv, axis=0, keepdims=True)
    grad = put(jnp.concatenate(to_center, axis=0), at_center) + put(jnp.concatenate(to_partner, axis=0), at_partner)
    gi = pick(grad, at_center)
    for k in range(3):
        rows = slice(k * CHAN, (k + 1) * CHAN)
        along[k] = along[k] + jnp.sum(a * gi[rows], axis=0, keepdims=True)
        rbar = rbar + unit[k : k + 1] * jnp.sum(na * gi[rows], axis=0, keepdims=True)
    part_ref[...] = jnp.concatenate(along + [rbar, jnp.zeros((4, PAIRS), F32)], axis=0)


def k_env_back(
    packed_ref,
    scal_ref,
    av_ref,
    nav_ref,
    part_ref,
    back_ref,
    column_ref,
    to_before_ref,
    to_after_ref,
    to_cells_ref,
    dbar_ref,
):
    packed = packed_ref[...]
    scal = scal_ref[...]
    unit, inv = scal[0:3], scal[4:5]
    part = part_ref[...]
    named = jnp.where(column_ref[:, 0:1].astype(jnp.int32) == centers_of(packed), 1.0, 0.0).astype(BF16)
    high, low = split2(back_ref[...])
    gi = dot(high, named, 0, 0) + dot(low, named, 0, 0)
    a, na = av_ref[:CHAN], nav_ref[:CHAN]
    along = []
    rbar = part[3:4]
    for k in range(3):
        rows = slice(k * CHAN, (k + 1) * CHAN)
        along.append(part[k : k + 1] + jnp.sum(a * gi[rows], axis=0, keepdims=True))
        rbar = rbar + unit[k : k + 1] * jnp.sum(na * gi[rows], axis=0, keepdims=True)
    for k in range(3):
        rbar = rbar - inv * along[k] * unit[k : k + 1]
    dbar = jnp.concatenate([along[k] * inv + rbar * unit[k : k + 1] for k in range(3)] + [jnp.zeros((5, PAIRS), F32)], axis=0)
    slots = match(ghost_slot(partners_of(packed)), 512)
    msg = put_rows(jnp.concatenate([dbar, jnp.zeros((120, PAIRS), F32)], axis=0), slots)
    to_before_ref[...] = msg[:128]
    to_after_ref[...] = msg[128:256]
    to_cells_ref[...] = msg[256:]
    dbar_ref[...] = dbar


def k_own_force(packed_ref, dbar_ref, out_ref):
    packed = packed_ref[...]
    dbar = dbar_ref[...]
    out_ref[...] = put(dbar, match(partners_of(packed), ATOMS)) - put(dbar, match(centers_of(packed), ATOMS))


def k_force(own_ref, back_ref, column_ref, energy_ref, out_ref):
    named = jnp.where(
        column_ref[:, 0:1].astype(jnp.int32) == lax.broadcasted_iota(jnp.int32, (LIST, ATOMS), 1), 1.0, 0.0
    ).astype(BF16)
    returned = pick(back_ref[...].T[0:8], named, 3)
    total = -(own_ref[0:3] + returned[0:3])
    energy = energy_ref[...]
    for k in range(3):
        for i in range(4):
            out_ref[4 * k + i : 4 * k + i + 1] = total[k : k + 1, 128 * i : 128 * i + 128]
    for i in range(4):
        out_ref[12 + i : 13 + i] = energy[0:1, 128 * i : 128 * i + 128]


def k_unpack(in_ref, force_ref, energy_ref):
    for k in range(3):
        for i in range(4):
            force_ref[k, 0, 0, 0:1, 128 * i : 128 * i + 128] = in_ref[4 * k + i : 4 * k + i + 1]
    for i in range(4):
        energy_ref[0, 0, 0:1, 128 * i : 128 * i + 128] = in_ref[12 + i : 13 + i]


def call(kernel, outs, *args):
    shapes = [jax.ShapeDtypeStruct(s, F32) for s in outs]
    spec = pl.BlockSpec(memory_space=pltpu.VMEM)
    return pl.pallas_call(
        kernel,
        out_shape=shapes,
        in_specs=[spec] * len(args),
        out_specs=[spec] * len(outs),
        compiler_params=pltpu.CompilerParams(vmem_limit_bytes=48 * 1024 * 1024),
        name=kernel.__name__,
    )(*args)


def shards(
    positions,
    species,
    send_lists,
    pair_center,
    pair_partner,
    pair_slot_live,
    w_basis,
    emb_center,
    emb_partner,
    w_env,
    w_value,
    w_mix,
    w_out,
):
    packed = pack(positions, species, send_lists, pair_center, pair_partner, pair_slot_live)
    here = spots()
    channels = (w_env.T, w_value.T)
    wo = w_out.reshape(128, 1)

    packed = send(packed, MOVE_IN)
    low, high, column = call(k_lists, [(32, 128), (32, 128), (LIST, 8)], packed)
    (part,) = call(k_own_pairs, [(8, PAIRS)], packed)
    low, high = low.reshape(1, 2, 2, 8, 128), high.reshape(1, 2, 2, 8, 128)
    ghosts = [g.reshape(-1, 128) for g in spread(low, high, here)]
    low, high, scal, pre, av = call(
        k_features,
        [(32, 192), (32, 192), (8, PAIRS), (128, PAIRS), (128, PAIRS)],
        packed,
        part,
        *ghosts,
        column,
        w_basis,
        emb_center,
        emb_partner,
        *channels,
    )
    ei, ej, latent, hid, tangent, nav = call(
        k_own_env,
        [(192, PAIRS), (192, PAIRS)] + [(128, PAIRS)] * 4,
        packed,
        scal,
        pre,
        av,
        w_basis,
        *channels,
        w_mix,
    )
    low, high = low.reshape(1, 2, 2, 8, 192), high.reshape(1, 2, 2, 8, 192)
    ghosts = [g.reshape(-1, 192) for g in spread(low, high, here)]
    before, after, cells, ej, h, tbar = call(
        k_energy,
        [(128, 192), (128, 192), (256, 192), (192, PAIRS), (128, PAIRS), (CHAN, PAIRS)],
        packed,
        scal,
        av,
        *ghosts,
        ei,
        ej,
        hid,
        w_mix,
        wo,
    )
    part, energy = call(
        k_direct,
        [(8, PAIRS), (4, ATOMS)],
        packed,
        scal,
        av,
        nav,
        ei,
        ej,
        latent,
        tangent,
        h,
        tbar,
        w_mix,
        wo,
    )
    before, after = before.reshape(4, 4, 8, 192), after.reshape(4, 4, 8, 192)
    back, (part, energy) = collect(before, after, cells.reshape(4, 4, 2, 8, 192), here, (part, energy))
    back = back.reshape(LIST, 192)
    before, after, cells, dbar = call(
        k_env_back, [(128, 128), (128, 128), (256, 128), (8, PAIRS)], packed, scal, av, nav, part, back, column
    )
    (own,) = call(k_own_force, [(8, ATOMS)], packed, dbar)
    before, after = before.reshape(4, 4, 8, 128), after.reshape(4, 4, 8, 128)
    back, own = collect(before, after, cells.reshape(4, 4, 2, 8, 128), here, own)
    back = back.reshape(LIST, 128)
    (out,) = call(k_force, [(16, 128)], own, back, column, energy)
    out = send(out, MOVE_OUT)
    return call(k_unpack, [(3, 1, 1, 1, ATOMS), (1, 1, 1, ATOMS)], out)


def solution(mesh):
    in_specs = (
        P(None, "gx", "gy", "gz", None),
        P("gx", "gy", "gz", None),
        P("gx", "gy", "gz", None),
        P("gx", "gy", "gz", None, None),
        P("gx", "gy", "gz", None, None),
        P("gx", "gy", "gz", None, None),
        P(),
        P(),
        P(),
        P(),
        P(),
        P(),
        P(),
    )
    out_specs = (P(None, "gx", "gy", "gz", None), P("gx", "gy", "gz", None))
    return jax.shard_map(shards, mesh=mesh, in_specs=in_specs, out_specs=out_specs, check_vma=False)
```

```python
import math

import jax
import jax.numpy as jnp

from jax import lax
from jax.experimental import pallas as pl
from jax.experimental.pallas import tpu as pltpu
from jax.sharding import PartitionSpec as P

AXES = ("gx", "gy", "gz")
SHAPE = (16, 4, 8)
ATOMS = 512
PAIRS = 1024
LIST = 64
CHAN = 64
STEP = math.pi / 12.0
F32 = jnp.float32
BF16 = jnp.bfloat16


def flat(x, y, z):
    return (x * SHAPE[1] + y) * SHAPE[2] + z


def device(chip_x, chip_y, chip_z, core):
    return flat((chip_z % 8) * 2 + core, chip_y, (chip_z // 8) * 4 + chip_x)


def home(x, y, z):
    x, y, z = x % SHAPE[0], y % SHAPE[1], z % SHAPE[2]
    return device((z // 2 + 1) % 4, y, -x % 16, z % 2)


CELLS = [(x, y, z) for x in range(SHAPE[0]) for y in range(SHAPE[1]) for z in range(SHAPE[2])]
CHIPS = [(x, y, z, c) for x in range(4) for y in range(4) for z in range(16) for c in range(2)]
MOVE_IN = [(flat(*c), home(*c)) for c in CELLS]
MOVE_OUT = [(b, a) for a, b in MOVE_IN]
UP = [(home(x, y, z), home(x, y, z + 1)) for x, y, z in CELLS]
DOWN = [(b, a) for a, b in UP]


def along(spot, axis, position, core):
    spot = list(spot)
    spot[axis], spot[3] = position, core
    return device(*spot)


def snake(axis, count):
    pairs = []
    for spot in CHIPS:
        at, core = spot[axis], spot[3]
        then = at + 1 - 2 * core
        goal = along(spot, axis, then, core) if 0 <= then < count else along(spot, axis, at, 1 - core)
        pairs.append((device(*spot), goal))
    return pairs


def ends(axis, count):
    return [(device(*s), along(s, axis, count - 1 - s[axis], s[3])) for s in CHIPS if s[axis] in (0, count - 1)]


RINGS = {0: (2, 16), 1: (1, 4)}
FORTH = {a: snake(*r) for a, r in RINGS.items()}
BACK = {a: [(j, i) for i, j in p] for a, p in FORTH.items()}
ENDS = {a: ends(*r) for a, r in RINGS.items()}


def send(x, pairs):
    return lax.ppermute(x, AXES, pairs)


def spots():
    gx, gy, gz = (lax.axis_index(a) for a in AXES)
    return {0: (gz // 4) * 8 + gx // 2, 1: gy, 2: gx % 2}


def swap(axis, first, last, here):
    if axis == 0:
        return trade(axis, last, first, here)[::-1]
    return trade(axis, first, last, here)


def trade(axis, first, last, here):
    at, upward, count = here[axis], here[2] == 0, RINGS[axis][1]
    forth = send(jnp.where(upward, last, first), FORTH[axis])
    ring = send(jnp.where(at == 0, first, last), ENDS[axis])
    back = send(jnp.where(upward, first, last), BACK[axis])
    start, end = at == 0, at == count - 1
    if axis == 0:
        after = jnp.where(~end, jnp.where(~upward, forth, back), jnp.where(end, ring, back))
        before = jnp.where(start, jnp.where(start, ring, back), jnp.where(upward, forth, back))
    else:
        before = jnp.where(~start, jnp.where(upward, forth, back), jnp.where(start, ring, back))
        after = jnp.where(end, jnp.where(end, ring, back), jnp.where(~upward, forth, back))
    return before, after


def spread(low, high, here):
    before, after = swap(0, low, high, here)
    cells = jnp.concatenate([before, low, high, after], axis=0)
    before, after = swap(1, cells[:, 0:1], cells[:, 1:2], here)
    cells = jnp.concatenate([before, cells, after], axis=1)
    before = send(cells[:, :, 1], UP)
    after = send(cells[:, :, 0], DOWN)
    return before, after, cells


def collect(before, after, cells, here, beside):
    first = send(after, UP)
    last = send(before, DOWN)
    cells = cells + jnp.stack([first, last], axis=2)
    cells, beside = lax.optimization_barrier((cells, beside))
    for axis in (1, 0):
        first = lax.slice_in_dim(cells, 0, 1, axis=axis)
        last = lax.slice_in_dim(cells, 3, 4, axis=axis)
        from_before, from_after = swap(axis, first, last, here)
        cells = lax.slice_in_dim(cells, 1, 3, axis=axis) + jnp.concatenate([from_before, from_after], axis=axis)
    return cells, beside


def split2(x):
    high = x.astype(BF16)
    low = (x - high.astype(F32)).astype(BF16)
    return high, low


def split3(x):
    high = x.astype(BF16)
    rest = x - high.astype(F32)
    mid = rest.astype(BF16)
    return high, mid, (rest - mid.astype(F32)).astype(BF16)


def dot(a, b, ca, cb):
    return lax.dot_general(a, b, (((ca,), (cb,)), ((), ())), preferred_element_type=F32)


def halves(x):
    high = x.astype(BF16).astype(F32)
    return high, x - high


def weighted(w, x):
    wh, wl = halves(w)
    xh, xl = halves(x)
    left = jnp.concatenate([wh, wl, wh], axis=0).astype(BF16)
    return dot(left, jnp.concatenate([xh, xh, xl], axis=0).astype(BF16), 0, 0)


def weighted_t(w, x):
    wh, wl = halves(w)
    xh, xl = halves(x)
    left = jnp.concatenate([wh, wl, wh], axis=1).astype(BF16)
    return dot(left, jnp.concatenate([xh, xh, xl], axis=0).astype(BF16), 1, 0)


def pick(table, onehot, parts=2):
    rows = table.shape[0]
    pieces = split3(table) if parts == 3 else split2(table)
    full = dot(jnp.concatenate(pieces, axis=0), onehot, 1, 0)
    out = full[:rows]
    for i in range(1, parts):
        out = out + full[rows * i : rows * (i + 1)]
    return out


def put(values, onehot, parts=2):
    rows = values.shape[0]
    pieces = split3(values) if parts == 3 else split2(values)
    full = dot(jnp.concatenate(pieces, axis=0), onehot, 1, 1)
    out = full[:rows]
    for i in range(1, parts):
        out = out + full[rows * i : rows * (i + 1)]
    return out


def put_rows(values, onehot):
    high, low = halves(values)
    if values.shape[0] % 128:
        gap = jnp.zeros((-values.shape[0] % 128, values.shape[1]), F32)
        high, low = jnp.concatenate([high, gap], axis=0), jnp.concatenate([low, gap], axis=0)
    rows = high.shape[0]
    full = dot(onehot, jnp.concatenate([high, low], axis=0).astype(BF16), 1, 1)
    return (full[:, :rows] + full[:, rows:])[:, : values.shape[0]]


def lanes(block):
    return jnp.concatenate([block[i : i + 1] for i in range(block.shape[0])], axis=1)


def match(index, count):
    ids = lax.broadcasted_iota(jnp.int32, (count, index.shape[1]), 0)
    return jnp.where(ids == index, 1.0, 0.0).astype(BF16)


def centers_of(packed):
    return lanes(packed[16:24]).astype(jnp.int32)


def partners_of(packed):
    return lanes(packed[24:32]).astype(jnp.int32)


def live_of(packed):
    return lanes(packed[32:40])


def own_table(packed):
    return jnp.concatenate([lanes(packed[4 * k : 4 * k + 4]) for k in range(4)], axis=0)


def ghost_cell(partners):
    rows = partners - ATOMS
    cell = rows >> 3
    skip = jnp.zeros_like(cell)
    for start in (21, 23, 33, 35):
        skip = skip + jnp.where(cell >= start, 2, 0)
    full = cell + skip
    return full >> 4, (full >> 2) & 3, full & 3, rows & 7


def ghost_slot(partners):
    p, q, r, atom = ghost_cell(partners)
    column = p * 4 + q
    slot = jnp.where(r == 0, column * 8, jnp.where(r == 3, column * 8 + 128, 256 + (column * 2 + r - 1) * 8)) + atom
    return jnp.where(partners >= ATOMS, slot, -1)


def k_pack(pos_in, kind_in, names_in, center_in, partner_in, live_in, out_ref, pos_ref, kind_ref, names_ref, center_ref, partner_ref, live_ref, sems):
    moves = [
        pltpu.make_async_copy(source, target, sems.at[i])
        for i, (source, target) in enumerate(
            [
                (pos_in, pos_ref),
                (kind_in, kind_ref),
                (names_in, names_ref),
                (center_in, center_ref),
                (partner_in, partner_ref),
                (live_in, live_ref),
            ]
        )
    ]
    for move in moves:
        move.start()
    out_ref[40:48] = jnp.zeros((8, 128), F32)
    for move in moves:
        move.wait()
    for k in range(3):
        for i in range(4):
            out_ref[4 * k + i : 4 * k + i + 1] = pos_ref[k, 0, 0, 0:1, 128 * i : 128 * i + 128]
    for i in range(4):
        out_ref[12 + i : 13 + i] = kind_ref[0, 0, 0:1, 128 * i : 128 * i + 128].astype(F32)
    out_ref[16:24] = center_ref[0, 0, 0].astype(F32)
    out_ref[24:32] = partner_ref[0, 0, 0].astype(F32)
    out_ref[32:40] = live_ref[0, 0, 0].astype(F32)
    names = [names_ref[i, j, k : k + 1] for i in range(2) for j in range(2) for k in range(2)]
    names.append(jnp.full((1, 64), -1, jnp.int32))
    out_ref[40:41] = jnp.concatenate(names, axis=1).astype(F32)


def pack(*args):
    return pl.pallas_call(
        k_pack,
        out_shape=jax.ShapeDtypeStruct((48, 128), F32),
        in_specs=[pl.BlockSpec(memory_space=pltpu.MemorySpace.HBM)] * len(args),
        out_specs=pl.BlockSpec(memory_space=pltpu.VMEM),
        scratch_shapes=[pltpu.VMEM(a.shape, a.dtype) for a in args] + [pltpu.SemaphoreType.DMA((len(args),))],
        compiler_params=pltpu.CompilerParams(vmem_limit_bytes=60 * 1024 * 1024),
        name="k_pack",
    )(*args)


def k_lists(packed_ref, low_ref, high_ref, column_ref):
    packed = packed_ref[...]
    names = packed[40:41].astype(jnp.int32)
    found = pick(own_table(packed), match(names, ATOMS), 3)
    wide = jnp.concatenate([found, jnp.zeros((124, 128), F32)], axis=0).T
    low_ref[...] = wide[:32]
    high_ref[...] = wide[32:64]
    column_ref[...] = jnp.broadcast_to(packed[40:41], (8, 128)).T[:LIST]


def k_own_pairs(packed_ref, out_ref):
    packed = packed_ref[...]
    table = own_table(packed)
    at_center = pick(table, match(centers_of(packed), ATOMS), 3)
    at_partner = pick(table, match(partners_of(packed), ATOMS), 3)
    out_ref[0:3] = at_partner[0:3] - at_center[0:3]
    out_ref[3:4] = at_partner[3:4]
    out_ref[4:5] = at_center[3:4]
    out_ref[5:8] = jnp.zeros((3, PAIRS), F32)


def k_features(
    packed_ref, part_ref, before_ref, after_ref, cells_ref, column_ref, wb_ref, ec_ref, ep_ref, we_ref, wv_ref, low_ref, high_ref, scal_ref, pre_ref, av_ref
):
    packed = packed_ref[...]
    part = part_ref[...]
    ghost = jnp.concatenate([before_ref[...], after_ref[...], cells_ref[...]], axis=0).T[0:8]
    partners = partners_of(packed)
    slots = match(ghost_slot(partners), 512)
    pieces = split3(ghost)
    far = dot(jnp.concatenate(pieces, axis=0), slots, 1, 0)
    far = far[0:8] + (far[8:16] + far[16:24])
    moved = [jnp.where(c == 0, -6.0, jnp.where(c == 3, 6.0, 0.0)) for c in ghost_cell(partners)[:3]]
    moved = jnp.where(partners >= ATOMS, jnp.concatenate(moved, axis=0), 0.0)
    disp = part[0:3] + (far[0:3] + moved)
    partner_kind = part[3:4] + far[3:4]
    center_kind = part[4:5]
    radius = jnp.sqrt(jnp.sum(disp * disp, axis=0, keepdims=True) + 0.25)
    inv = 1.0 / radius
    unit = disp * inv
    scaled = radius * 0.2
    base = 1.0 + scaled * scaled
    live = live_of(packed)
    cut = live / (base * base)
    orders = lax.broadcasted_iota(jnp.int32, (8, 1), 0).astype(F32) + 1.0
    angle = radius * orders * STEP
    basis = jnp.sin(angle) * inv
    kinds = lax.broadcasted_iota(jnp.int32, (8, 1), 0).astype(F32)
    first = jnp.where(center_kind == kinds, 1.0, 0.0)
    second = jnp.where(partner_kind == kinds, 1.0, 0.0)
    gap = jnp.zeros((2, 128), F32)
    kinds_in = jnp.concatenate([wb_ref[...], ec_ref[...], gap, ep_ref[...], gap], axis=0)
    pre = weighted(kinds_in, jnp.concatenate([basis, first, second], axis=0))
    latent = cut * (pre * jax.nn.sigmoid(pre))
    av = weighted_t(jnp.concatenate([we_ref[...], wv_ref[...]], axis=0), latent)
    a = av[:CHAN]
    terms = jnp.concatenate([unit[k : k + 1] * a for k in range(3)], axis=0)
    named = jnp.where(column_ref[:, 0:1].astype(jnp.int32) == centers_of(packed), 1.0, 0.0).astype(BF16)
    msg = put_rows(terms, named)
    low_ref[...] = msg[:32]
    high_ref[...] = msg[32:]
    scal_ref[0:3] = unit
    scal_ref[3:4] = radius
    scal_ref[4:5] = inv
    scal_ref[5:6] = cut
    scal_ref[6:7] = live * (-0.8) * scaled / (base * base * base)
    scal_ref[7:8] = live
    pre_ref[...] = pre
    av_ref[...] = av


def k_own_env(packed_ref, scal_ref, pre_ref, av_ref, wb_ref, we_ref, wv_ref, wm_ref, ei_ref, ej_ref, lat_ref, hid_ref, tan_ref, nav_ref):
    packed = packed_ref[...]
    scal = scal_ref[...]
    unit, radius, inv, cut, slope = scal[0:3], scal[3:4], scal[4:5], scal[5:6], scal[6:7]
    av = av_ref[...]
    a = av[:CHAN]
    terms = jnp.concatenate([unit[k : k + 1] * a for k in range(3)], axis=0)
    at_center = match(centers_of(packed), ATOMS)
    env = put(terms, at_center)
    ei_ref[...] = pick(env, at_center)
    ej_ref[...] = pick(env, match(partners_of(packed), ATOMS))
    pre = pre_ref[...]
    gate = jax.nn.sigmoid(pre)
    act = pre * gate
    latent = cut * act
    lat_ref[...] = latent
    hid_ref[...] = weighted(wm_ref[0:128], latent)
    orders = lax.broadcasted_iota(jnp.int32, (8, 1), 0).astype(F32) + 1.0
    angle = radius * orders * STEP
    change = (jnp.cos(angle) * (orders * STEP) - jnp.sin(angle) * inv) * inv
    tangent = slope * act + cut * (gate * (1.0 + pre * (1.0 - gate))) * weighted(wb_ref[...], change)
    tan_ref[...] = tangent
    nav_ref[...] = weighted_t(jnp.concatenate([we_ref[...], wv_ref[...]], axis=0), tangent)


def k_energy(
    packed_ref,
    scal_ref,
    av_ref,
    before_ref,
    after_ref,
    cells_ref,
    ei_ref,
    ejown_ref,
    hid_ref,
    wm_ref,
    wo_ref,
    to_before_ref,
    to_after_ref,
    to_cells_ref,
    ej_ref,
    h_ref,
    tb_ref,
):
    packed = packed_ref[...]
    scal = scal_ref[...]
    unit, cut = scal[0:3], scal[5:6]
    slots = match(ghost_slot(partners_of(packed)), 512)
    ghost = jnp.concatenate([before_ref[...], after_ref[...], cells_ref[...]], axis=0)
    ghost = jnp.concatenate([ghost, jnp.zeros((512, 64), F32)], axis=1).T[:192]
    ej = ejown_ref[...] + pick(ghost, slots)
    ei = ei_ref[...]
    coupling = 0.0
    for k in range(3):
        rows = slice(k * CHAN, (k + 1) * CHAN)
        coupling = coupling + ei[rows] * (unit[k : k + 1] + ej[rows])
    v = av_ref[CHAN:]
    mix = wm_ref[128:]
    h = hid_ref[...] + weighted(mix, v * coupling)
    gate = jax.nn.sigmoid(h)
    out = wo_ref[...]
    hbar = (cut * out) * (gate * (1.0 + h * (1.0 - gate)))
    tbar = weighted_t(mix, hbar)
    cbar = tbar * v
    back = jnp.concatenate([cbar * ei[k * CHAN : (k + 1) * CHAN] for k in range(3)], axis=0)
    msg = put_rows(back, slots)
    to_before_ref[...] = msg[:128]
    to_after_ref[...] = msg[128:256]
    to_cells_ref[...] = msg[256:]
    ej_ref[...] = ej
    h_ref[...] = h
    tb_ref[...] = tbar


def k_direct(
    packed_ref, scal_ref, av_ref, nav_ref, ei_ref, ej_ref, lat_ref, tan_ref, h_ref, tb_ref, wm_ref, wo_ref, part_ref, energy_ref
):
    packed = packed_ref[...]
    scal = scal_ref[...]
    unit, cut, slope = scal[0:3], scal[5:6], scal[6:7]
    at_center = match(centers_of(packed), ATOMS)
    at_partner = match(partners_of(packed), ATOMS)
    ei, ej = ei_ref[...], ej_ref[...]
    a, v = av_ref[:CHAN], av_ref[CHAN:]
    na, nv = nav_ref[:CHAN], nav_ref[CHAN:]
    tbar = tb_ref[...]
    cbar = tbar * v
    h = h_ref[...]
    gate = jax.nn.sigmoid(h)
    out = wo_ref[...]
    score = jnp.sum(out * (lat_ref[...] + h * gate), axis=0, keepdims=True)
    energy_ref[...] = put(jnp.concatenate([cut * score, jnp.zeros((7, PAIRS), F32)], axis=0), at_center)[0:4]
    ubar = cut * out
    hbar = ubar * (gate * (1.0 + h * (1.0 - gate)))
    lbar = ubar + weighted_t(wm_ref[0:128], hbar)
    coupling = 0.0
    to_center, to_partner, along = [], [], []
    for k in range(3):
        rows = slice(k * CHAN, (k + 1) * CHAN)
        mixed = unit[k : k + 1] + ej[rows]
        coupling = coupling + ei[rows] * mixed
        to_center.append(cbar * mixed)
        to_partner.append(cbar * ei[rows])
        along.append(jnp.sum(to_partner[k], axis=0, keepdims=True))
    vbar = tbar * coupling
    rbar = slope * score + jnp.sum(lbar * tan_ref[...], axis=0, keepdims=True) + jnp.sum(vbar * nv, axis=0, keepdims=True)
    grad = put(jnp.concatenate(to_center, axis=0), at_center) + put(jnp.concatenate(to_partner, axis=0), at_partner)
    gi = pick(grad, at_center)
    for k in range(3):
        rows = slice(k * CHAN, (k + 1) * CHAN)
        along[k] = along[k] + jnp.sum(a * gi[rows], axis=0, keepdims=True)
        rbar = rbar + unit[k : k + 1] * jnp.sum(na * gi[rows], axis=0, keepdims=True)
    part_ref[...] = jnp.concatenate(along + [rbar, jnp.zeros((4, PAIRS), F32)], axis=0)


def k_env_back(
    packed_ref,
    scal_ref,
    av_ref,
    nav_ref,
    part_ref,
    back_ref,
    column_ref,
    to_before_ref,
    to_after_ref,
    to_cells_ref,
    dbar_ref,
):
    packed = packed_ref[...]
    scal = scal_ref[...]
    unit, inv = scal[0:3], scal[4:5]
    part = part_ref[...]
    named = jnp.where(column_ref[:, 0:1].astype(jnp.int32) == centers_of(packed), 1.0, 0.0).astype(BF16)
    high, low = split2(back_ref[...])
    gi = dot(high, named, 0, 0) + dot(low, named, 0, 0)
    a, na = av_ref[:CHAN], nav_ref[:CHAN]
    along = []
    rbar = part[3:4]
    for k in range(3):
        rows = slice(k * CHAN, (k + 1) * CHAN)
        along.append(part[k : k + 1] + jnp.sum(a * gi[rows], axis=0, keepdims=True))
        rbar = rbar + unit[k : k + 1] * jnp.sum(na * gi[rows], axis=0, keepdims=True)
    for k in range(3):
        rbar = rbar - inv * along[k] * unit[k : k + 1]
    dbar = jnp.concatenate([along[k] * inv + rbar * unit[k : k + 1] for k in range(3)] + [jnp.zeros((5, PAIRS), F32)], axis=0)
    slots = match(ghost_slot(partners_of(packed)), 512)
    msg = put_rows(jnp.concatenate([dbar, jnp.zeros((120, PAIRS), F32)], axis=0), slots)
    to_before_ref[...] = msg[:128]
    to_after_ref[...] = msg[128:256]
    to_cells_ref[...] = msg[256:]
    dbar_ref[...] = dbar


def k_own_force(packed_ref, dbar_ref, out_ref):
    packed = packed_ref[...]
    dbar = dbar_ref[...]
    out_ref[...] = put(dbar, match(partners_of(packed), ATOMS)) - put(dbar, match(centers_of(packed), ATOMS))


def k_force(own_ref, back_ref, column_ref, energy_ref, out_ref):
    named = jnp.where(
        column_ref[:, 0:1].astype(jnp.int32) == lax.broadcasted_iota(jnp.int32, (LIST, ATOMS), 1), 1.0, 0.0
    ).astype(BF16)
    returned = pick(back_ref[...].T[0:8], named, 3)
    total = -(own_ref[0:3] + returned[0:3])
    energy = energy_ref[...]
    for k in range(3):
        for i in range(4):
            out_ref[4 * k + i : 4 * k + i + 1] = total[k : k + 1, 128 * i : 128 * i + 128]
    for i in range(4):
        out_ref[12 + i : 13 + i] = energy[0:1, 128 * i : 128 * i + 128]


def k_unpack(in_ref, force_ref, energy_ref):
    for k in range(3):
        for i in range(4):
            force_ref[k, 0, 0, 0:1, 128 * i : 128 * i + 128] = in_ref[4 * k + i : 4 * k + i + 1]
    for i in range(4):
        energy_ref[0, 0, 0:1, 128 * i : 128 * i + 128] = in_ref[12 + i : 13 + i]


def call(kernel, outs, *args):
    shapes = [jax.ShapeDtypeStruct(s, F32) for s in outs]
    spec = pl.BlockSpec(memory_space=pltpu.VMEM)
    return pl.pallas_call(
        kernel,
        out_shape=shapes,
        in_specs=[spec] * len(args),
        out_specs=[spec] * len(outs),
        compiler_params=pltpu.CompilerParams(vmem_limit_bytes=48 * 1024 * 1024),
        name=kernel.__name__,
    )(*args)


def shards(
    positions,
    species,
    send_lists,
    pair_center,
    pair_partner,
    pair_slot_live,
    w_basis,
    emb_center,
    emb_partner,
    w_env,
    w_value,
    w_mix,
    w_out,
):
    packed = pack(positions, species, send_lists, pair_center, pair_partner, pair_slot_live)
    here = spots()
    channels = (w_env.T, w_value.T)
    wo = w_out.reshape(128, 1)

    packed = send(packed, MOVE_IN)
    low, high, column = call(k_lists, [(32, 128), (32, 128), (LIST, 8)], packed)
    (part,) = call(k_own_pairs, [(8, PAIRS)], packed)
    low, high = low.reshape(1, 2, 2, 8, 128), high.reshape(1, 2, 2, 8, 128)
    ghosts = [g.reshape(-1, 128) for g in spread(low, high, here)]
    low, high, scal, pre, av = call(
        k_features,
        [(32, 192), (32, 192), (8, PAIRS), (128, PAIRS), (128, PAIRS)],
        packed,
        part,
        *ghosts,
        column,
        w_basis,
        emb_center,
        emb_partner,
        *channels,
    )
    ei, ej, latent, hid, tangent, nav = call(
        k_own_env,
        [(192, PAIRS), (192, PAIRS)] + [(128, PAIRS)] * 4,
        packed,
        scal,
        pre,
        av,
        w_basis,
        *channels,
        w_mix,
    )
    low, high = low.reshape(1, 2, 2, 8, 192), high.reshape(1, 2, 2, 8, 192)
    ghosts = [g.reshape(-1, 192) for g in spread(low, high, here)]
    before, after, cells, ej, h, tbar = call(
        k_energy,
        [(128, 192), (128, 192), (256, 192), (192, PAIRS), (128, PAIRS), (CHAN, PAIRS)],
        packed,
        scal,
        av,
        *ghosts,
        ei,
        ej,
        hid,
        w_mix,
        wo,
    )
    part, energy = call(
        k_direct,
        [(8, PAIRS), (4, ATOMS)],
        packed,
        scal,
        av,
        nav,
        ei,
        ej,
        latent,
        tangent,
        h,
        tbar,
        w_mix,
        wo,
    )
    before, after = before.reshape(4, 4, 8, 192), after.reshape(4, 4, 8, 192)
    back, (part, energy) = collect(before, after, cells.reshape(4, 4, 2, 8, 192), here, (part, energy))
    back = back.reshape(LIST, 192)
    before, after, cells, dbar = call(
        k_env_back, [(128, 128), (128, 128), (256, 128), (8, PAIRS)], packed, scal, av, nav, part, back, column
    )
    (own,) = call(k_own_force, [(8, ATOMS)], packed, dbar)
    before, after = before.reshape(4, 4, 8, 128), after.reshape(4, 4, 8, 128)
    back, own = collect(before, after, cells.reshape(4, 4, 2, 8, 128), here, own)
    back = back.reshape(LIST, 128)
    (out,) = call(k_force, [(16, 128)], own, back, column, energy)
    out = send(out, MOVE_OUT)
    return call(k_unpack, [(3, 1, 1, 1, ATOMS), (1, 1, 1, ATOMS)], out)


def solution(mesh):
    in_specs = (
        P(None, "gx", "gy", "gz", None),
        P("gx", "gy", "gz", None),
        P("gx", "gy", "gz", None),
        P("gx", "gy", "gz", None, None),
        P("gx", "gy", "gz", None, None),
        P("gx", "gy", "gz", None, None),
        P(),
        P(),
        P(),
        P(),
        P(),
        P(),
        P(),
    )
    out_specs = (P(None, "gx", "gy", "gz", None), P("gx", "gy", "gz", None))
    return jax.shard_map(shards, mesh=mesh, in_specs=in_specs, out_specs=out_specs, check_vma=False)
```

```python
import math

import jax
import jax.numpy as jnp

from jax import lax
from jax.experimental import pallas as pl
from jax.experimental.pallas import tpu as pltpu
from jax.sharding import PartitionSpec as P

AXES = ("gx", "gy", "gz")
SHAPE = (16, 4, 8)
ATOMS = 512
PAIRS = 1024
LIST = 64
CHAN = 64
STEP = math.pi / 12.0
F32 = jnp.float32
BF16 = jnp.bfloat16


def flat(x, y, z):
    return (x * SHAPE[1] + y) * SHAPE[2] + z


def device(chip_x, chip_y, chip_z, core):
    return flat((chip_z % 8) * 2 + core, chip_y, (chip_z // 8) * 4 + chip_x)


def home(x, y, z):
    x, y, z = x % SHAPE[0], y % SHAPE[1], z % SHAPE[2]
    return device((z // 2 + 1) % 4, y, x, z % 2)


CELLS = [(x, y, z) for x in range(SHAPE[0]) for y in range(SHAPE[1]) for z in range(SHAPE[2])]
CHIPS = [(x, y, z, c) for x in range(4) for y in range(4) for z in range(16) for c in range(2)]
MOVE_IN = [(flat(*c), home(*c)) for c in CELLS]
MOVE_OUT = [(b, a) for a, b in MOVE_IN]
UP = [(home(x, y, z), home(x, y, z + 1)) for x, y, z in CELLS]
DOWN = [(b, a) for a, b in UP]


def along(spot, axis, position, core):
    spot = list(spot)
    spot[axis], spot[3] = position, core
    return device(*spot)


def snake(axis, count):
    pairs = []
    for spot in CHIPS:
        at, core = spot[axis], spot[3]
        then = at + 1 - 2 * core
        goal = along(spot, axis, then, core) if 0 <= then < count else along(spot, axis, at, 1 - core)
        pairs.append((device(*spot), goal))
    return pairs


def ends(axis, count):
    return [(device(*s), along(s, axis, count - 1 - s[axis], s[3])) for s in CHIPS if s[axis] in (0, count - 1)]


RINGS = {0: (2, 16), 1: (1, 4)}
FORTH = {a: snake(*r) for a, r in RINGS.items()}
BACK = {a: [(j, i) for i, j in p] for a, p in FORTH.items()}
ENDS = {a: ends(*r) for a, r in RINGS.items()}


def send(x, pairs):
    return lax.ppermute(x, AXES, pairs)


def spots():
    gx, gy, gz = (lax.axis_index(a) for a in AXES)
    return {0: (gz // 4) * 8 + gx // 2, 1: gy, 2: gx % 2}


def swap(axis, first, last, here):
    at, upward, count = here[axis], here[2] == 0, RINGS[axis][1]
    forth = send(jnp.where(upward, last, first), FORTH[axis])
    ring = send(jnp.where(at == 0, first, last), ENDS[axis])
    back = send(jnp.where(upward, first, last), BACK[axis])
    start, end = at == 0, at == count - 1
    before = jnp.where(~start, jnp.where(upward, forth, back), jnp.where(start, ring, back))
    after = jnp.where(end, jnp.where(end, ring, back), jnp.where(~upward, forth, back))
    return before, after


def spread(low, high, here):
    before, after = swap(0, low, high, here)
    cells = jnp.concatenate([before, low, high, after], axis=0)
    before, after = swap(1, cells[:, 0:1], cells[:, 1:2], here)
    cells = jnp.concatenate([before, cells, after], axis=1)
    before = send(cells[:, :, 1], UP)
    after = send(cells[:, :, 0], DOWN)
    return before, after, cells


def collect(before, after, cells, here, beside):
    first = send(after, UP)
    last = send(before, DOWN)
    cells = cells + jnp.stack([first, last], axis=2)
    cells, beside = lax.optimization_barrier((cells, beside))
    for axis in (0, 1):
        first = lax.slice_in_dim(cells, 0, 1, axis=axis)
        last = lax.slice_in_dim(cells, 3, 4, axis=axis)
        from_before, from_after = swap(axis, first, last, here)
        cells = lax.slice_in_dim(cells, 1, 3, axis=axis) + jnp.concatenate([from_before, from_after], axis=axis)
    return cells, beside


def split2(x):
    high = x.astype(BF16)
    low = (x - high.astype(F32)).astype(BF16)
    return high, low


def split3(x):
    high = x.astype(BF16)
    rest = x - high.astype(F32)
    mid = rest.astype(BF16)
    return high, mid, (rest - mid.astype(F32)).astype(BF16)


def dot(a, b, ca, cb):
    return lax.dot_general(a, b, (((ca,), (cb,)), ((), ())), preferred_element_type=F32)


def halves(x):
    high = x.astype(BF16).astype(F32)
    return high, x - high


def weighted(w, x):
    wh, wl = halves(w)
    xh, xl = halves(x)
    left = jnp.concatenate([wh, wl, wh], axis=0).astype(BF16)
    return dot(left, jnp.concatenate([xh, xh, xl], axis=0).astype(BF16), 0, 0)


def weighted_t(w, x):
    wh, wl = halves(w)
    xh, xl = halves(x)
    left = jnp.concatenate([wh, wl, wh], axis=1).astype(BF16)
    return dot(left, jnp.concatenate([xh, xh, xl], axis=0).astype(BF16), 1, 0)


def pick(table, onehot, parts=2):
    rows = table.shape[0]
    pieces = split3(table) if parts == 3 else split2(table)
    full = dot(jnp.concatenate(pieces, axis=0), onehot, 1, 0)
    out = full[:rows]
    for i in range(1, parts):
        out = out + full[rows * i : rows * (i + 1)]
    return out


def put(values, onehot, parts=2):
    rows = values.shape[0]
    pieces = split3(values) if parts == 3 else split2(values)
    full = dot(jnp.concatenate(pieces, axis=0), onehot, 1, 1)
    out = full[:rows]
    for i in range(1, parts):
        out = out + full[rows * i : rows * (i + 1)]
    return out


def put_rows(values, onehot):
    high, low = halves(values)
    if values.shape[0] % 128:
        gap = jnp.zeros((-values.shape[0] % 128, values.shape[1]), F32)
        high, low = jnp.concatenate([high, gap], axis=0), jnp.concatenate([low, gap], axis=0)
    rows = high.shape[0]
    full = dot(onehot, jnp.concatenate([high, low], axis=0).astype(BF16), 1, 1)
    return (full[:, :rows] + full[:, rows:])[:, : values.shape[0]]


def lanes(block):
    return jnp.concatenate([block[i : i + 1] for i in range(block.shape[0])], axis=1)


def match(index, count):
    ids = lax.broadcasted_iota(jnp.int32, (count, index.shape[1]), 0)
    return jnp.where(ids == index, 1.0, 0.0).astype(BF16)


def centers_of(packed):
    return lanes(packed[16:24]).astype(jnp.int32)


def partners_of(packed):
    return lanes(packed[24:32]).astype(jnp.int32)


def live_of(packed):
    return lanes(packed[32:40])


def own_table(packed):
    return jnp.concatenate([lanes(packed[4 * k : 4 * k + 4]) for k in range(4)], axis=0)


def ghost_cell(partners):
    rows = partners - ATOMS
    cell = rows >> 3
    skip = jnp.zeros_like(cell)
    for start in (21, 23, 33, 35):
        skip = skip + jnp.where(cell >= start, 2, 0)
    full = cell + skip
    return full >> 4, (full >> 2) & 3, full & 3, rows & 7


def ghost_slot(partners):
    p, q, r, atom = ghost_cell(partners)
    column = p * 4 + q
    slot = jnp.where(r == 0, column * 8, jnp.where(r == 3, column * 8 + 128, 256 + (column * 2 + r - 1) * 8)) + atom
    return jnp.where(partners >= ATOMS, slot, -1)


def k_pack(pos_in, kind_in, names_in, center_in, partner_in, live_in, out_ref, pos_ref, kind_ref, names_ref, center_ref, partner_ref, live_ref, sems):
    moves = [
        pltpu.make_async_copy(source, target, sems.at[i])
        for i, (source, target) in enumerate(
            [
                (pos_in, pos_ref),
                (kind_in, kind_ref),
                (names_in, names_ref),
                (center_in, center_ref),
                (partner_in, partner_ref),
                (live_in, live_ref),
            ]
        )
    ]
    for move in moves:
        move.start()
    out_ref[40:48] = jnp.zeros((8, 128), F32)
    for move in moves:
        move.wait()
    for k in range(3):
        for i in range(4):
            out_ref[4 * k + i : 4 * k + i + 1] = pos_ref[k, 0, 0, 0:1, 128 * i : 128 * i + 128]
    for i in range(4):
        out_ref[12 + i : 13 + i] = kind_ref[0, 0, 0:1, 128 * i : 128 * i + 128].astype(F32)
    out_ref[16:24] = center_ref[0, 0, 0].astype(F32)
    out_ref[24:32] = partner_ref[0, 0, 0].astype(F32)
    out_ref[32:40] = live_ref[0, 0, 0].astype(F32)
    names = [names_ref[i, j, k : k + 1] for i in range(2) for j in range(2) for k in range(2)]
    names.append(jnp.full((1, 64), -1, jnp.int32))
    out_ref[40:41] = jnp.concatenate(names, axis=1).astype(F32)


def pack(*args):
    return pl.pallas_call(
        k_pack,
        out_shape=jax.ShapeDtypeStruct((48, 128), F32),
        in_specs=[pl.BlockSpec(memory_space=pltpu.MemorySpace.HBM)] * len(args),
        out_specs=pl.BlockSpec(memory_space=pltpu.VMEM),
        scratch_shapes=[pltpu.VMEM(a.shape, a.dtype) for a in args] + [pltpu.SemaphoreType.DMA((len(args),))],
        compiler_params=pltpu.CompilerParams(vmem_limit_bytes=60 * 1024 * 1024),
        name="k_pack",
    )(*args)


def k_lists(packed_ref, low_ref, high_ref, column_ref):
    packed = packed_ref[...]
    names = packed[40:41].astype(jnp.int32)
    found = pick(own_table(packed), match(names, ATOMS), 3)
    wide = jnp.concatenate([found, jnp.zeros((124, 128), F32)], axis=0).T
    low_ref[...] = wide[:32]
    high_ref[...] = wide[32:64]
    column_ref[...] = jnp.broadcast_to(packed[40:41], (8, 128)).T[:LIST]


def k_own_pairs(packed_ref, out_ref):
    packed = packed_ref[...]
    table = own_table(packed)
    at_center = pick(table, match(centers_of(packed), ATOMS), 3)
    at_partner = pick(table, match(partners_of(packed), ATOMS), 3)
    out_ref[0:3] = at_partner[0:3] - at_center[0:3]
    out_ref[3:4] = at_partner[3:4]
    out_ref[4:5] = at_center[3:4]
    out_ref[5:8] = jnp.zeros((3, PAIRS), F32)


def k_features(
    packed_ref, part_ref, before_ref, after_ref, cells_ref, column_ref, wb_ref, ec_ref, ep_ref, we_ref, wv_ref, low_ref, high_ref, scal_ref, pre_ref, av_ref
):
    packed = packed_ref[...]
    part = part_ref[...]
    ghost = jnp.concatenate([before_ref[...], after_ref[...], cells_ref[...]], axis=0).T[0:8]
    partners = partners_of(packed)
    slots = match(ghost_slot(partners), 512)
    pieces = split3(ghost)
    far = dot(jnp.concatenate(pieces, axis=0), slots, 1, 0)
    far = far[0:8] + (far[8:16] + far[16:24])
    moved = [jnp.where(c == 0, -6.0, jnp.where(c == 3, 6.0, 0.0)) for c in ghost_cell(partners)[:3]]
    moved = jnp.where(partners >= ATOMS, jnp.concatenate(moved, axis=0), 0.0)
    disp = part[0:3] + (far[0:3] + moved)
    partner_kind = part[3:4] + far[3:4]
    center_kind = part[4:5]
    radius = jnp.sqrt(jnp.sum(disp * disp, axis=0, keepdims=True) + 0.25)
    inv = 1.0 / radius
    unit = disp * inv
    scaled = radius * 0.2
    base = 1.0 + scaled * scaled
    live = live_of(packed)
    cut = live / (base * base)
    orders = lax.broadcasted_iota(jnp.int32, (8, 1), 0).astype(F32) + 1.0
    angle = radius * orders * STEP
    basis = jnp.sin(angle) * inv
    kinds = lax.broadcasted_iota(jnp.int32, (8, 1), 0).astype(F32)
    first = jnp.where(center_kind == kinds, 1.0, 0.0)
    second = jnp.where(partner_kind == kinds, 1.0, 0.0)
    gap = jnp.zeros((2, 128), F32)
    kinds_in = jnp.concatenate([wb_ref[...], ec_ref[...], gap, ep_ref[...], gap], axis=0)
    pre = weighted(kinds_in, jnp.concatenate([basis, first, second], axis=0))
    latent = cut * (pre * jax.nn.sigmoid(pre))
    av = weighted_t(jnp.concatenate([we_ref[...], wv_ref[...]], axis=0), latent)
    a = av[:CHAN]
    terms = jnp.concatenate([unit[k : k + 1] * a for k in range(3)], axis=0)
    named = jnp.where(column_ref[:, 0:1].astype(jnp.int32) == centers_of(packed), 1.0, 0.0).astype(BF16)
    msg = put_rows(terms, named)
    low_ref[...] = msg[:32]
    high_ref[...] = msg[32:]
    scal_ref[0:3] = unit
    scal_ref[3:4] = radius
    scal_ref[4:5] = inv
    scal_ref[5:6] = cut
    scal_ref[6:7] = live * (-0.8) * scaled / (base * base * base)
    scal_ref[7:8] = live
    pre_ref[...] = pre
    av_ref[...] = av


def k_own_env(packed_ref, scal_ref, pre_ref, av_ref, wb_ref, we_ref, wv_ref, wm_ref, ei_ref, ej_ref, lat_ref, hid_ref, tan_ref, nav_ref):
    packed = packed_ref[...]
    scal = scal_ref[...]
    unit, radius, inv, cut, slope = scal[0:3], scal[3:4], scal[4:5], scal[5:6], scal[6:7]
    av = av_ref[...]
    a = av[:CHAN]
    terms = jnp.concatenate([unit[k : k + 1] * a for k in range(3)], axis=0)
    at_center = match(centers_of(packed), ATOMS)
    env = put(terms, at_center)
    ei_ref[...] = pick(env, at_center)
    ej_ref[...] = pick(env, match(partners_of(packed), ATOMS))
    pre = pre_ref[...]
    gate = jax.nn.sigmoid(pre)
    act = pre * gate
    latent = cut * act
    lat_ref[...] = latent
    hid_ref[...] = weighted(wm_ref[0:128], latent)
    orders = lax.broadcasted_iota(jnp.int32, (8, 1), 0).astype(F32) + 1.0
    angle = radius * orders * STEP
    change = (jnp.cos(angle) * (orders * STEP) - jnp.sin(angle) * inv) * inv
    tangent = slope * act + cut * (gate * (1.0 + pre * (1.0 - gate))) * weighted(wb_ref[...], change)
    tan_ref[...] = tangent
    nav_ref[...] = weighted_t(jnp.concatenate([we_ref[...], wv_ref[...]], axis=0), tangent)


def k_energy(
    packed_ref,
    scal_ref,
    av_ref,
    before_ref,
    after_ref,
    cells_ref,
    ei_ref,
    ejown_ref,
    hid_ref,
    wm_ref,
    wo_ref,
    to_before_ref,
    to_after_ref,
    to_cells_ref,
    ej_ref,
    h_ref,
    tb_ref,
):
    packed = packed_ref[...]
    scal = scal_ref[...]
    unit, cut = scal[0:3], scal[5:6]
    slots = match(ghost_slot(partners_of(packed)), 512)
    ghost = jnp.concatenate([before_ref[...], after_ref[...], cells_ref[...]], axis=0)
    ghost = jnp.concatenate([ghost, jnp.zeros((512, 64), F32)], axis=1).T[:192]
    ej = ejown_ref[...] + pick(ghost, slots)
    ei = ei_ref[...]
    coupling = 0.0
    for k in range(3):
        rows = slice(k * CHAN, (k + 1) * CHAN)
        coupling = coupling + ei[rows] * (unit[k : k + 1] + ej[rows])
    v = av_ref[CHAN:]
    mix = wm_ref[128:]
    h = hid_ref[...] + weighted(mix, v * coupling)
    gate = jax.nn.sigmoid(h)
    out = wo_ref[...]
    hbar = (cut * out) * (gate * (1.0 + h * (1.0 - gate)))
    tbar = weighted_t(mix, hbar)
    cbar = tbar * v
    back = jnp.concatenate([cbar * ei[k * CHAN : (k + 1) * CHAN] for k in range(3)], axis=0)
    msg = put_rows(back, slots)
    to_before_ref[...] = msg[:128]
    to_after_ref[...] = msg[128:256]
    to_cells_ref[...] = msg[256:]
    ej_ref[...] = ej
    h_ref[...] = h
    tb_ref[...] = tbar


def k_direct(
    packed_ref, scal_ref, av_ref, nav_ref, ei_ref, ej_ref, lat_ref, tan_ref, h_ref, tb_ref, wm_ref, wo_ref, part_ref, energy_ref
):
    packed = packed_ref[...]
    scal = scal_ref[...]
    unit, cut, slope = scal[0:3], scal[5:6], scal[6:7]
    at_center = match(centers_of(packed), ATOMS)
    at_partner = match(partners_of(packed), ATOMS)
    ei, ej = ei_ref[...], ej_ref[...]
    a, v = av_ref[:CHAN], av_ref[CHAN:]
    na, nv = nav_ref[:CHAN], nav_ref[CHAN:]
    tbar = tb_ref[...]
    cbar = tbar * v
    h = h_ref[...]
    gate = jax.nn.sigmoid(h)
    out = wo_ref[...]
    score = jnp.sum(out * (lat_ref[...] + h * gate), axis=0, keepdims=True)
    energy_ref[...] = put(jnp.concatenate([cut * score, jnp.zeros((7, PAIRS), F32)], axis=0), at_center)[0:4]
    ubar = cut * out
    hbar = ubar * (gate * (1.0 + h * (1.0 - gate)))
    lbar = ubar + weighted_t(wm_ref[0:128], hbar)
    coupling = 0.0
    to_center, to_partner, along = [], [], []
    for k in range(3):
        rows = slice(k * CHAN, (k + 1) * CHAN)
        mixed = unit[k : k + 1] + ej[rows]
        coupling = coupling + ei[rows] * mixed
        to_center.append(cbar * mixed)
        to_partner.append(cbar * ei[rows])
        along.append(jnp.sum(to_partner[k], axis=0, keepdims=True))
    vbar = tbar * coupling
    rbar = slope * score + jnp.sum(lbar * tan_ref[...], axis=0, keepdims=True) + jnp.sum(vbar * nv, axis=0, keepdims=True)
    grad = put(jnp.concatenate(to_center, axis=0), at_center) + put(jnp.concatenate(to_partner, axis=0), at_partner)
    gi = pick(grad, at_center)
    for k in range(3):
        rows = slice(k * CHAN, (k + 1) * CHAN)
        along[k] = along[k] + jnp.sum(a * gi[rows], axis=0, keepdims=True)
        rbar = rbar + unit[k : k + 1] * jnp.sum(na * gi[rows], axis=0, keepdims=True)
    part_ref[...] = jnp.concatenate(along + [rbar, jnp.zeros((4, PAIRS), F32)], axis=0)


def k_env_back(
    packed_ref,
    scal_ref,
    av_ref,
    nav_ref,
    part_ref,
    back_ref,
    column_ref,
    to_before_ref,
    to_after_ref,
    to_cells_ref,
    dbar_ref,
):
    packed = packed_ref[...]
    scal = scal_ref[...]
    unit, inv = scal[0:3], scal[4:5]
    part = part_ref[...]
    named = jnp.where(column_ref[:, 0:1].astype(jnp.int32) == centers_of(packed), 1.0, 0.0).astype(BF16)
    high, low = split2(back_ref[...])
    gi = dot(high, named, 0, 0) + dot(low, named, 0, 0)
    a, na = av_ref[:CHAN], nav_ref[:CHAN]
    along = []
    rbar = part[3:4]
    for k in range(3):
        rows = slice(k * CHAN, (k + 1) * CHAN)
        along.append(part[k : k + 1] + jnp.sum(a * gi[rows], axis=0, keepdims=True))
        rbar = rbar + unit[k : k + 1] * jnp.sum(na * gi[rows], axis=0, keepdims=True)
    for k in range(3):
        rbar = rbar - inv * along[k] * unit[k : k + 1]
    dbar = jnp.concatenate([along[k] * inv + rbar * unit[k : k + 1] for k in range(3)] + [jnp.zeros((5, PAIRS), F32)], axis=0)
    slots = match(ghost_slot(partners_of(packed)), 512)
    msg = put_rows(jnp.concatenate([dbar, jnp.zeros((120, PAIRS), F32)], axis=0), slots)
    to_before_ref[...] = msg[:128]
    to_after_ref[...] = msg[128:256]
    to_cells_ref[...] = msg[256:]
    dbar_ref[...] = dbar


def k_own_force(packed_ref, dbar_ref, out_ref):
    packed = packed_ref[...]
    dbar = dbar_ref[...]
    out_ref[...] = put(dbar, match(partners_of(packed), ATOMS)) - put(dbar, match(centers_of(packed), ATOMS))


def k_force(own_ref, back_ref, column_ref, energy_ref, out_ref):
    named = jnp.where(
        column_ref[:, 0:1].astype(jnp.int32) == lax.broadcasted_iota(jnp.int32, (LIST, ATOMS), 1), 1.0, 0.0
    ).astype(BF16)
    returned = pick(back_ref[...].T[0:8], named, 3)
    total = -(own_ref[0:3] + returned[0:3])
    energy = energy_ref[...]
    for k in range(3):
        for i in range(4):
            out_ref[4 * k + i : 4 * k + i + 1] = total[k : k + 1, 128 * i : 128 * i + 128]
    for i in range(4):
        out_ref[12 + i : 13 + i] = energy[0:1, 128 * i : 128 * i + 128]


def k_unpack(in_ref, force_ref, energy_ref):
    for k in range(3):
        for i in range(4):
            force_ref[k, 0, 0, 0:1, 128 * i : 128 * i + 128] = in_ref[4 * k + i : 4 * k + i + 1]
    for i in range(4):
        energy_ref[0, 0, 0:1, 128 * i : 128 * i + 128] = in_ref[12 + i : 13 + i]


def call(kernel, outs, *args):
    shapes = [jax.ShapeDtypeStruct(s, F32) for s in outs]
    spec = pl.BlockSpec(memory_space=pltpu.VMEM)
    return pl.pallas_call(
        kernel,
        out_shape=shapes,
        in_specs=[spec] * len(args),
        out_specs=[spec] * len(outs),
        compiler_params=pltpu.CompilerParams(vmem_limit_bytes=48 * 1024 * 1024),
        name=kernel.__name__,
    )(*args)


def shards(
    positions,
    species,
    send_lists,
    pair_center,
    pair_partner,
    pair_slot_live,
    w_basis,
    emb_center,
    emb_partner,
    w_env,
    w_value,
    w_mix,
    w_out,
):
    packed = pack(positions, species, send_lists, pair_center, pair_partner, pair_slot_live)
    here = spots()
    channels = (w_env.T, w_value.T)
    wo = w_out.reshape(128, 1)

    packed = send(packed, MOVE_IN)
    low, high, column = call(k_lists, [(32, 128), (32, 128), (LIST, 8)], packed)
    (part,) = call(k_own_pairs, [(8, PAIRS)], packed)
    low, high = low.reshape(1, 2, 2, 8, 128), high.reshape(1, 2, 2, 8, 128)
    ghosts = [g.reshape(-1, 128) for g in spread(low, high, here)]
    low, high, scal, pre, av = call(
        k_features,
        [(32, 192), (32, 192), (8, PAIRS), (128, PAIRS), (128, PAIRS)],
        packed,
        part,
        *ghosts,
        column,
        w_basis,
        emb_center,
        emb_partner,
        *channels,
    )
    ei, ej, latent, hid, tangent, nav = call(
        k_own_env,
        [(192, PAIRS), (192, PAIRS)] + [(128, PAIRS)] * 4,
        packed,
        scal,
        pre,
        av,
        w_basis,
        *channels,
        w_mix,
    )
    low, high = low.reshape(1, 2, 2, 8, 192), high.reshape(1, 2, 2, 8, 192)
    ghosts = [g.reshape(-1, 192) for g in spread(low, high, here)]
    before, after, cells, ej, h, tbar = call(
        k_energy,
        [(128, 192), (128, 192), (256, 192), (192, PAIRS), (128, PAIRS), (CHAN, PAIRS)],
        packed,
        scal,
        av,
        *ghosts,
        ei,
        ej,
        hid,
        w_mix,
        wo,
    )
    part, energy = call(
        k_direct,
        [(8, PAIRS), (4, ATOMS)],
        packed,
        scal,
        av,
        nav,
        ei,
        ej,
        latent,
        tangent,
        h,
        tbar,
        w_mix,
        wo,
    )
    before, after = before.reshape(4, 4, 8, 192), after.reshape(4, 4, 8, 192)
    back, (part, energy) = collect(before, after, cells.reshape(4, 4, 2, 8, 192), here, (part, energy))
    back = back.reshape(LIST, 192)
    before, after, cells, dbar = call(
        k_env_back, [(128, 128), (128, 128), (256, 128), (8, PAIRS)], packed, scal, av, nav, part, back, column
    )
    (own,) = call(k_own_force, [(8, ATOMS)], packed, dbar)
    before, after = before.reshape(4, 4, 8, 128), after.reshape(4, 4, 8, 128)
    back, own = collect(before, after, cells.reshape(4, 4, 2, 8, 128), here, own)
    back = back.reshape(LIST, 128)
    (out,) = call(k_force, [(16, 128)], own, back, column, energy)
    out = send(out, MOVE_OUT)
    return call(k_unpack, [(3, 1, 1, 1, ATOMS), (1, 1, 1, ATOMS)], out)


def solution(mesh):
    in_specs = (
        P(None, "gx", "gy", "gz", None),
        P("gx", "gy", "gz", None),
        P("gx", "gy", "gz", None),
        P("gx", "gy", "gz", None, None),
        P("gx", "gy", "gz", None, None),
        P("gx", "gy", "gz", None, None),
        P(),
        P(),
        P(),
        P(),
        P(),
        P(),
        P(),
    )
    out_specs = (P(None, "gx", "gy", "gz", None), P("gx", "gy", "gz", None))
    return jax.shard_map(shards, mesh=mesh, in_specs=in_specs, out_specs=out_specs, check_vma=False)
```

```python
import math

import jax
import jax.numpy as jnp

from jax import lax
from jax.experimental import pallas as pl
from jax.experimental.pallas import tpu as pltpu
from jax.sharding import PartitionSpec as P

AXES = ("gx", "gy", "gz")
SHAPE = (16, 4, 8)
ATOMS = 512
PAIRS = 1024
LIST = 64
CHAN = 64
STEP = math.pi / 12.0
F32 = jnp.float32
BF16 = jnp.bfloat16


def flat(x, y, z):
    return (x * SHAPE[1] + y) * SHAPE[2] + z


def device(chip_x, chip_y, chip_z, core):
    return flat((chip_z % 8) * 2 + core, chip_y, (chip_z // 8) * 4 + chip_x)


def home(x, y, z):
    x, y, z = x % SHAPE[0], y % SHAPE[1], z % SHAPE[2]
    return device((z // 2 + 1) % 4, y, x, z % 2)


CELLS = [(x, y, z) for x in range(SHAPE[0]) for y in range(SHAPE[1]) for z in range(SHAPE[2])]
CHIPS = [(x, y, z, c) for x in range(4) for y in range(4) for z in range(16) for c in range(2)]
MOVE_IN = [(flat(*c), home(*c)) for c in CELLS]
MOVE_OUT = [(b, a) for a, b in MOVE_IN]
UP = [(home(x, y, z), home(x, y, z + 1)) for x, y, z in CELLS]
DOWN = [(b, a) for a, b in UP]


def along(spot, axis, position, core):
    spot = list(spot)
    spot[axis], spot[3] = position, core
    return device(*spot)


def snake(axis, count):
    pairs = []
    for spot in CHIPS:
        at, core = spot[axis], spot[3]
        then = at + 1 - 2 * core
        goal = along(spot, axis, then, core) if 0 <= then < count else along(spot, axis, at, 1 - core)
        pairs.append((device(*spot), goal))
    return pairs


def ends(axis, count):
    return [(device(*s), along(s, axis, count - 1 - s[axis], s[3])) for s in CHIPS if s[axis] in (0, count - 1)]


RINGS = {0: (2, 16), 1: (1, 4)}
FORTH = {a: snake(*r) for a, r in RINGS.items()}
BACK = {a: [(j, i) for i, j in p] for a, p in FORTH.items()}
ENDS = {a: ends(*r) for a, r in RINGS.items()}


def send(x, pairs):
    return lax.ppermute(x, AXES, pairs)


def spots():
    gx, gy, gz = (lax.axis_index(a) for a in AXES)
    return {0: (gz // 4) * 8 + gx // 2, 1: gy, 2: gx % 2}


def swap(axis, first, last, here):
    at, upward, count = here[axis], here[2] == 0, RINGS[axis][1]
    forth = send(jnp.where(upward, last, first), FORTH[axis])
    ring = send(jnp.where(at == 0, first, last), ENDS[axis])
    back = send(jnp.where(upward, first, last), BACK[axis])
    start, end = at == 0, at == count - 1
    before = jnp.where(~start, jnp.where(upward, forth, back), jnp.where(start, ring, back))
    after = jnp.where(end, jnp.where(end, ring, back), jnp.where(~upward, forth, back))
    return before, after


def spread(low, high, here, beside=()):
    before, after = swap(0, low, high, here)
    cells = jnp.concatenate([before, low, high, after], axis=0)
    if beside:
        cells, *beside = lax.optimization_barrier((cells, *beside))
    before, after = swap(1, cells[:, 0:1], cells[:, 1:2], here)
    cells = jnp.concatenate([before, cells, after], axis=1)
    before = send(cells[:, :, 1], UP)
    after = send(cells[:, :, 0], DOWN)
    return (before, after, cells), beside


def collect(before, after, cells, here, beside):
    first = send(after, UP)
    last = send(before, DOWN)
    cells = cells + jnp.stack([first, last], axis=2)
    cells, beside = lax.optimization_barrier((cells, beside))
    for axis in (1, 0):
        first = lax.slice_in_dim(cells, 0, 1, axis=axis)
        last = lax.slice_in_dim(cells, 3, 4, axis=axis)
        from_before, from_after = swap(axis, first, last, here)
        cells = lax.slice_in_dim(cells, 1, 3, axis=axis) + jnp.concatenate([from_before, from_after], axis=axis)
    return cells, beside


def split2(x):
    high = x.astype(BF16)
    low = (x - high.astype(F32)).astype(BF16)
    return high, low


def split3(x):
    high = x.astype(BF16)
    rest = x - high.astype(F32)
    mid = rest.astype(BF16)
    return high, mid, (rest - mid.astype(F32)).astype(BF16)


def dot(a, b, ca, cb):
    return lax.dot_general(a, b, (((ca,), (cb,)), ((), ())), preferred_element_type=F32)


def halves(x):
    high = x.astype(BF16).astype(F32)
    return high, x - high


def weighted(w, x):
    wh, wl = halves(w)
    xh, xl = halves(x)
    left = jnp.concatenate([wh, wl, wh], axis=0).astype(BF16)
    return dot(left, jnp.concatenate([xh, xh, xl], axis=0).astype(BF16), 0, 0)


def weighted_t(w, x):
    wh, wl = halves(w)
    xh, xl = halves(x)
    left = jnp.concatenate([wh, wl, wh], axis=1).astype(BF16)
    return dot(left, jnp.concatenate([xh, xh, xl], axis=0).astype(BF16), 1, 0)


def pick(table, onehot, parts=2):
    rows = table.shape[0]
    pieces = split3(table) if parts == 3 else split2(table)
    full = dot(jnp.concatenate(pieces, axis=0), onehot, 1, 0)
    out = full[:rows]
    for i in range(1, parts):
        out = out + full[rows * i : rows * (i + 1)]
    return out


def put(values, onehot, parts=2):
    rows = values.shape[0]
    pieces = split3(values) if parts == 3 else split2(values)
    full = dot(jnp.concatenate(pieces, axis=0), onehot, 1, 1)
    out = full[:rows]
    for i in range(1, parts):
        out = out + full[rows * i : rows * (i + 1)]
    return out


def put_rows(values, onehot):
    high, low = halves(values)
    if values.shape[0] % 128:
        gap = jnp.zeros((-values.shape[0] % 128, values.shape[1]), F32)
        high, low = jnp.concatenate([high, gap], axis=0), jnp.concatenate([low, gap], axis=0)
    rows = high.shape[0]
    full = dot(onehot, jnp.concatenate([high, low], axis=0).astype(BF16), 1, 1)
    return (full[:, :rows] + full[:, rows:])[:, : values.shape[0]]


def lanes(block):
    return jnp.concatenate([block[i : i + 1] for i in range(block.shape[0])], axis=1)


def match(index, count):
    ids = lax.broadcasted_iota(jnp.int32, (count, index.shape[1]), 0)
    return jnp.where(ids == index, 1.0, 0.0).astype(BF16)


def centers_of(packed):
    return lanes(packed[16:24]).astype(jnp.int32)


def partners_of(packed):
    return lanes(packed[24:32]).astype(jnp.int32)


def live_of(packed):
    return lanes(packed[32:40])


def own_table(packed):
    return jnp.concatenate([lanes(packed[4 * k : 4 * k + 4]) for k in range(4)], axis=0)


def ghost_cell(partners):
    rows = partners - ATOMS
    cell = rows >> 3
    skip = jnp.zeros_like(cell)
    for start in (21, 23, 33, 35):
        skip = skip + jnp.where(cell >= start, 2, 0)
    full = cell + skip
    return full >> 4, (full >> 2) & 3, full & 3, rows & 7


def ghost_slot(partners):
    p, q, r, atom = ghost_cell(partners)
    column = p * 4 + q
    slot = jnp.where(r == 0, column * 8, jnp.where(r == 3, column * 8 + 128, 256 + (column * 2 + r - 1) * 8)) + atom
    return jnp.where(partners >= ATOMS, slot, -1)


def k_pack(pos_in, kind_in, names_in, center_in, partner_in, live_in, out_ref, pos_ref, kind_ref, names_ref, center_ref, partner_ref, live_ref, sems):
    moves = [
        pltpu.make_async_copy(source, target, sems.at[i])
        for i, (source, target) in enumerate(
            [
                (pos_in, pos_ref),
                (kind_in, kind_ref),
                (names_in, names_ref),
                (center_in, center_ref),
                (partner_in, partner_ref),
                (live_in, live_ref),
            ]
        )
    ]
    for move in moves:
        move.start()
    out_ref[40:48] = jnp.zeros((8, 128), F32)
    for move in moves:
        move.wait()
    for k in range(3):
        for i in range(4):
            out_ref[4 * k + i : 4 * k + i + 1] = pos_ref[k, 0, 0, 0:1, 128 * i : 128 * i + 128]
    for i in range(4):
        out_ref[12 + i : 13 + i] = kind_ref[0, 0, 0:1, 128 * i : 128 * i + 128].astype(F32)
    out_ref[16:24] = center_ref[0, 0, 0].astype(F32)
    out_ref[24:32] = partner_ref[0, 0, 0].astype(F32)
    out_ref[32:40] = live_ref[0, 0, 0].astype(F32)
    names = [names_ref[i, j, k : k + 1] for i in range(2) for j in range(2) for k in range(2)]
    names.append(jnp.full((1, 64), -1, jnp.int32))
    out_ref[40:41] = jnp.concatenate(names, axis=1).astype(F32)


def pack(*args):
    return pl.pallas_call(
        k_pack,
        out_shape=jax.ShapeDtypeStruct((48, 128), F32),
        in_specs=[pl.BlockSpec(memory_space=pltpu.MemorySpace.HBM)] * len(args),
        out_specs=pl.BlockSpec(memory_space=pltpu.VMEM),
        scratch_shapes=[pltpu.VMEM(a.shape, a.dtype) for a in args] + [pltpu.SemaphoreType.DMA((len(args),))],
        compiler_params=pltpu.CompilerParams(vmem_limit_bytes=60 * 1024 * 1024),
        name="k_pack",
    )(*args)


def k_lists(packed_ref, low_ref, high_ref, column_ref):
    packed = packed_ref[...]
    names = packed[40:41].astype(jnp.int32)
    found = pick(own_table(packed), match(names, ATOMS), 3)
    wide = jnp.concatenate([found, jnp.zeros((124, 128), F32)], axis=0).T
    low_ref[...] = wide[:32]
    high_ref[...] = wide[32:64]
    column_ref[...] = jnp.broadcast_to(packed[40:41], (8, 128)).T[:LIST]


def k_own_pairs(packed_ref, out_ref):
    packed = packed_ref[...]
    table = own_table(packed)
    at_center = pick(table, match(centers_of(packed), ATOMS), 3)
    at_partner = pick(table, match(partners_of(packed), ATOMS), 3)
    out_ref[0:3] = at_partner[0:3] - at_center[0:3]
    out_ref[3:4] = at_partner[3:4]
    out_ref[4:5] = at_center[3:4]
    out_ref[5:8] = jnp.zeros((3, PAIRS), F32)


def k_features(
    packed_ref, part_ref, before_ref, after_ref, cells_ref, column_ref, wb_ref, ec_ref, ep_ref, we_ref, wv_ref, low_ref, high_ref, scal_ref, pre_ref, av_ref
):
    packed = packed_ref[...]
    part = part_ref[...]
    ghost = jnp.concatenate([before_ref[...], after_ref[...], cells_ref[...]], axis=0).T[0:8]
    partners = partners_of(packed)
    slots = match(ghost_slot(partners), 512)
    pieces = split3(ghost)
    far = dot(jnp.concatenate(pieces, axis=0), slots, 1, 0)
    far = far[0:8] + (far[8:16] + far[16:24])
    moved = [jnp.where(c == 0, -6.0, jnp.where(c == 3, 6.0, 0.0)) for c in ghost_cell(partners)[:3]]
    moved = jnp.where(partners >= ATOMS, jnp.concatenate(moved, axis=0), 0.0)
    disp = part[0:3] + (far[0:3] + moved)
    partner_kind = part[3:4] + far[3:4]
    center_kind = part[4:5]
    radius = jnp.sqrt(jnp.sum(disp * disp, axis=0, keepdims=True) + 0.25)
    inv = 1.0 / radius
    unit = disp * inv
    scaled = radius * 0.2
    base = 1.0 + scaled * scaled
    live = live_of(packed)
    cut = live / (base * base)
    orders = lax.broadcasted_iota(jnp.int32, (8, 1), 0).astype(F32) + 1.0
    angle = radius * orders * STEP
    basis = jnp.sin(angle) * inv
    kinds = lax.broadcasted_iota(jnp.int32, (8, 1), 0).astype(F32)
    first = jnp.where(center_kind == kinds, 1.0, 0.0)
    second = jnp.where(partner_kind == kinds, 1.0, 0.0)
    gap = jnp.zeros((2, 128), F32)
    kinds_in = jnp.concatenate([wb_ref[...], ec_ref[...], gap, ep_ref[...], gap], axis=0)
    pre = weighted(kinds_in, jnp.concatenate([basis, first, second], axis=0))
    latent = cut * (pre * jax.nn.sigmoid(pre))
    av = weighted_t(jnp.concatenate([we_ref[...], wv_ref[...]], axis=0), latent)
    a = av[:CHAN]
    terms = jnp.concatenate([unit[k : k + 1] * a for k in range(3)], axis=0)
    named = jnp.where(column_ref[:, 0:1].astype(jnp.int32) == centers_of(packed), 1.0, 0.0).astype(BF16)
    msg = put_rows(terms, named)
    low_ref[...] = msg[:32]
    high_ref[...] = msg[32:]
    scal_ref[0:3] = unit
    scal_ref[3:4] = radius
    scal_ref[4:5] = inv
    scal_ref[5:6] = cut
    scal_ref[6:7] = live * (-0.8) * scaled / (base * base * base)
    scal_ref[7:8] = live
    pre_ref[...] = pre
    av_ref[...] = av


def k_own_env(packed_ref, scal_ref, pre_ref, av_ref, wb_ref, we_ref, wv_ref, wm_ref, ei_ref, ej_ref, lat_ref, hid_ref, tan_ref, nav_ref):
    packed = packed_ref[...]
    scal = scal_ref[...]
    unit, radius, inv, cut, slope = scal[0:3], scal[3:4], scal[4:5], scal[5:6], scal[6:7]
    av = av_ref[...]
    a = av[:CHAN]
    terms = jnp.concatenate([unit[k : k + 1] * a for k in range(3)], axis=0)
    at_center = match(centers_of(packed), ATOMS)
    env = put(terms, at_center)
    ei_ref[...] = pick(env, at_center)
    ej_ref[...] = pick(env, match(partners_of(packed), ATOMS))
    pre = pre_ref[...]
    gate = jax.nn.sigmoid(pre)
    act = pre * gate
    latent = cut * act
    lat_ref[...] = latent
    hid_ref[...] = weighted(wm_ref[0:128], latent)
    orders = lax.broadcasted_iota(jnp.int32, (8, 1), 0).astype(F32) + 1.0
    angle = radius * orders * STEP
    change = (jnp.cos(angle) * (orders * STEP) - jnp.sin(angle) * inv) * inv
    tangent = slope * act + cut * (gate * (1.0 + pre * (1.0 - gate))) * weighted(wb_ref[...], change)
    tan_ref[...] = tangent
    nav_ref[...] = weighted_t(jnp.concatenate([we_ref[...], wv_ref[...]], axis=0), tangent)


def k_energy(
    packed_ref,
    scal_ref,
    av_ref,
    before_ref,
    after_ref,
    cells_ref,
    ei_ref,
    ejown_ref,
    hid_ref,
    wm_ref,
    wo_ref,
    to_before_ref,
    to_after_ref,
    to_cells_ref,
    ej_ref,
    h_ref,
    tb_ref,
):
    packed = packed_ref[...]
    scal = scal_ref[...]
    unit, cut = scal[0:3], scal[5:6]
    slots = match(ghost_slot(partners_of(packed)), 512)
    ghost = jnp.concatenate([before_ref[...], after_ref[...], cells_ref[...]], axis=0)
    ghost = jnp.concatenate([ghost, jnp.zeros((512, 64), F32)], axis=1).T[:192]
    ej = ejown_ref[...] + pick(ghost, slots)
    ei = ei_ref[...]
    coupling = 0.0
    for k in range(3):
        rows = slice(k * CHAN, (k + 1) * CHAN)
        coupling = coupling + ei[rows] * (unit[k : k + 1] + ej[rows])
    v = av_ref[CHAN:]
    mix = wm_ref[128:]
    h = hid_ref[...] + weighted(mix, v * coupling)
    gate = jax.nn.sigmoid(h)
    out = wo_ref[...]
    hbar = (cut * out) * (gate * (1.0 + h * (1.0 - gate)))
    tbar = weighted_t(mix, hbar)
    cbar = tbar * v
    back = jnp.concatenate([cbar * ei[k * CHAN : (k + 1) * CHAN] for k in range(3)], axis=0)
    msg = put_rows(back, slots)
    to_before_ref[...] = msg[:128]
    to_after_ref[...] = msg[128:256]
    to_cells_ref[...] = msg[256:]
    ej_ref[...] = ej
    h_ref[...] = h
    tb_ref[...] = tbar


def k_direct(
    packed_ref, scal_ref, av_ref, nav_ref, ei_ref, ej_ref, lat_ref, tan_ref, h_ref, tb_ref, wm_ref, wo_ref, part_ref, energy_ref
):
    packed = packed_ref[...]
    scal = scal_ref[...]
    unit, cut, slope = scal[0:3], scal[5:6], scal[6:7]
    at_center = match(centers_of(packed), ATOMS)
    at_partner = match(partners_of(packed), ATOMS)
    ei, ej = ei_ref[...], ej_ref[...]
    a, v = av_ref[:CHAN], av_ref[CHAN:]
    na, nv = nav_ref[:CHAN], nav_ref[CHAN:]
    tbar = tb_ref[...]
    cbar = tbar * v
    h = h_ref[...]
    gate = jax.nn.sigmoid(h)
    out = wo_ref[...]
    score = jnp.sum(out * (lat_ref[...] + h * gate), axis=0, keepdims=True)
    energy_ref[...] = put(jnp.concatenate([cut * score, jnp.zeros((7, PAIRS), F32)], axis=0), at_center)[0:4]
    ubar = cut * out
    hbar = ubar * (gate * (1.0 + h * (1.0 - gate)))
    lbar = ubar + weighted_t(wm_ref[0:128], hbar)
    coupling = 0.0
    to_center, to_partner, along = [], [], []
    for k in range(3):
        rows = slice(k * CHAN, (k + 1) * CHAN)
        mixed = unit[k : k + 1] + ej[rows]
        coupling = coupling + ei[rows] * mixed
        to_center.append(cbar * mixed)
        to_partner.append(cbar * ei[rows])
        along.append(jnp.sum(to_partner[k], axis=0, keepdims=True))
    vbar = tbar * coupling
    rbar = slope * score + jnp.sum(lbar * tan_ref[...], axis=0, keepdims=True) + jnp.sum(vbar * nv, axis=0, keepdims=True)
    grad = put(jnp.concatenate(to_center, axis=0), at_center) + put(jnp.concatenate(to_partner, axis=0), at_partner)
    gi = pick(grad, at_center)
    for k in range(3):
        rows = slice(k * CHAN, (k + 1) * CHAN)
        along[k] = along[k] + jnp.sum(a * gi[rows], axis=0, keepdims=True)
        rbar = rbar + unit[k : k + 1] * jnp.sum(na * gi[rows], axis=0, keepdims=True)
    part_ref[...] = jnp.concatenate(along + [rbar, jnp.zeros((4, PAIRS), F32)], axis=0)


def k_env_back(
    packed_ref,
    scal_ref,
    av_ref,
    nav_ref,
    part_ref,
    back_ref,
    column_ref,
    to_before_ref,
    to_after_ref,
    to_cells_ref,
    dbar_ref,
):
    packed = packed_ref[...]
    scal = scal_ref[...]
    unit, inv = scal[0:3], scal[4:5]
    part = part_ref[...]
    named = jnp.where(column_ref[:, 0:1].astype(jnp.int32) == centers_of(packed), 1.0, 0.0).astype(BF16)
    high, low = split2(back_ref[...])
    gi = dot(high, named, 0, 0) + dot(low, named, 0, 0)
    a, na = av_ref[:CHAN], nav_ref[:CHAN]
    along = []
    rbar = part[3:4]
    for k in range(3):
        rows = slice(k * CHAN, (k + 1) * CHAN)
        along.append(part[k : k + 1] + jnp.sum(a * gi[rows], axis=0, keepdims=True))
        rbar = rbar + unit[k : k + 1] * jnp.sum(na * gi[rows], axis=0, keepdims=True)
    for k in range(3):
        rbar = rbar - inv * along[k] * unit[k : k + 1]
    dbar = jnp.concatenate([along[k] * inv + rbar * unit[k : k + 1] for k in range(3)] + [jnp.zeros((5, PAIRS), F32)], axis=0)
    slots = match(ghost_slot(partners_of(packed)), 512)
    msg = put_rows(jnp.concatenate([dbar, jnp.zeros((120, PAIRS), F32)], axis=0), slots)
    to_before_ref[...] = msg[:128]
    to_after_ref[...] = msg[128:256]
    to_cells_ref[...] = msg[256:]
    dbar_ref[...] = dbar


def k_own_force(packed_ref, dbar_ref, out_ref):
    packed = packed_ref[...]
    dbar = dbar_ref[...]
    out_ref[...] = put(dbar, match(partners_of(packed), ATOMS)) - put(dbar, match(centers_of(packed), ATOMS))


def k_force(own_ref, back_ref, column_ref, energy_ref, out_ref):
    named = jnp.where(
        column_ref[:, 0:1].astype(jnp.int32) == lax.broadcasted_iota(jnp.int32, (LIST, ATOMS), 1), 1.0, 0.0
    ).astype(BF16)
    returned = pick(back_ref[...].T[0:8], named, 3)
    total = -(own_ref[0:3] + returned[0:3])
    energy = energy_ref[...]
    for k in range(3):
        for i in range(4):
            out_ref[4 * k + i : 4 * k + i + 1] = total[k : k + 1, 128 * i : 128 * i + 128]
    for i in range(4):
        out_ref[12 + i : 13 + i] = energy[0:1, 128 * i : 128 * i + 128]


def k_unpack(in_ref, force_ref, energy_ref):
    for k in range(3):
        for i in range(4):
            force_ref[k, 0, 0, 0:1, 128 * i : 128 * i + 128] = in_ref[4 * k + i : 4 * k + i + 1]
    for i in range(4):
        energy_ref[0, 0, 0:1, 128 * i : 128 * i + 128] = in_ref[12 + i : 13 + i]


def call(kernel, outs, *args):
    shapes = [jax.ShapeDtypeStruct(s, F32) for s in outs]
    spec = pl.BlockSpec(memory_space=pltpu.VMEM)
    return pl.pallas_call(
        kernel,
        out_shape=shapes,
        in_specs=[spec] * len(args),
        out_specs=[spec] * len(outs),
        compiler_params=pltpu.CompilerParams(vmem_limit_bytes=48 * 1024 * 1024),
        name=kernel.__name__,
    )(*args)


def shards(
    positions,
    species,
    send_lists,
    pair_center,
    pair_partner,
    pair_slot_live,
    w_basis,
    emb_center,
    emb_partner,
    w_env,
    w_value,
    w_mix,
    w_out,
):
    packed = pack(positions, species, send_lists, pair_center, pair_partner, pair_slot_live)
    here = spots()
    channels = (w_env.T, w_value.T)
    wo = w_out.reshape(128, 1)

    packed = send(packed, MOVE_IN)
    low, high, column = call(k_lists, [(32, 128), (32, 128), (LIST, 8)], packed)
    (part,) = call(k_own_pairs, [(8, PAIRS)], packed)
    low, high = low.reshape(1, 2, 2, 8, 128), high.reshape(1, 2, 2, 8, 128)
    ghosts, (part,) = spread(low, high, here, (part,))
    ghosts = [g.reshape(-1, 128) for g in ghosts]
    low, high, scal, pre, av = call(
        k_features,
        [(32, 192), (32, 192), (8, PAIRS), (128, PAIRS), (128, PAIRS)],
        packed,
        part,
        *ghosts,
        column,
        w_basis,
        emb_center,
        emb_partner,
        *channels,
    )
    ei, ej, latent, hid, tangent, nav = call(
        k_own_env,
        [(192, PAIRS), (192, PAIRS)] + [(128, PAIRS)] * 4,
        packed,
        scal,
        pre,
        av,
        w_basis,
        *channels,
        w_mix,
    )
    low, high = low.reshape(1, 2, 2, 8, 192), high.reshape(1, 2, 2, 8, 192)
    ghosts = [g.reshape(-1, 192) for g in spread(low, high, here)[0]]
    before, after, cells, ej, h, tbar = call(
        k_energy,
        [(128, 192), (128, 192), (256, 192), (192, PAIRS), (128, PAIRS), (CHAN, PAIRS)],
        packed,
        scal,
        av,
        *ghosts,
        ei,
        ej,
        hid,
        w_mix,
        wo,
    )
    part, energy = call(
        k_direct,
        [(8, PAIRS), (4, ATOMS)],
        packed,
        scal,
        av,
        nav,
        ei,
        ej,
        latent,
        tangent,
        h,
        tbar,
        w_mix,
        wo,
    )
    before, after = before.reshape(4, 4, 8, 192), after.reshape(4, 4, 8, 192)
    back, (part, energy) = collect(before, after, cells.reshape(4, 4, 2, 8, 192), here, (part, energy))
    back = back.reshape(LIST, 192)
    before, after, cells, dbar = call(
        k_env_back, [(128, 128), (128, 128), (256, 128), (8, PAIRS)], packed, scal, av, nav, part, back, column
    )
    (own,) = call(k_own_force, [(8, ATOMS)], packed, dbar)
    before, after = before.reshape(4, 4, 8, 128), after.reshape(4, 4, 8, 128)
    back, own = collect(before, after, cells.reshape(4, 4, 2, 8, 128), here, own)
    back = back.reshape(LIST, 128)
    (out,) = call(k_force, [(16, 128)], own, back, column, energy)
    out = send(out, MOVE_OUT)
    return call(k_unpack, [(3, 1, 1, 1, ATOMS), (1, 1, 1, ATOMS)], out)


def solution(mesh):
    in_specs = (
        P(None, "gx", "gy", "gz", None),
        P("gx", "gy", "gz", None),
        P("gx", "gy", "gz", None),
        P("gx", "gy", "gz", None, None),
        P("gx", "gy", "gz", None, None),
        P("gx", "gy", "gz", None, None),
        P(),
        P(),
        P(),
        P(),
        P(),
        P(),
        P(),
    )
    out_specs = (P(None, "gx", "gy", "gz", None), P("gx", "gy", "gz", None))
    return jax.shard_map(shards, mesh=mesh, in_specs=in_specs, out_specs=out_specs, check_vma=False)
```
